128 devices in a mesh: expert: 32 (over x, z, core), tensor: 4 (over y).
Axes of the slice: x: 4, y: 4, z: 4, core: 2. Of those that a mesh axis runs over, the one named last changes fastest.
Arguments:
- tokens: bfloat16 [4096, 768], P('expert'), may hold values from -6 to 6
- segment_ids: int32 [32, 128], P('expert'), may hold values from 0 to 7, never falling along the last dimension, each value on 1 to 64 neighbouring positions
- expert_routes: int32 [2, 4096, 2], P(None, 'expert'), may hold values from 0 to 31, all different within a row; in each aligned block of 128 rows (0 to 127, 128 to 255, ..., all dimensions but the last counted through in order) at most 11 rows name the same one
- bucket_ids: int32 [255], replicated, may hold values from 0 to 31
- proj_qkv: bfloat16 [2, 3, 768, 768], P(None, None, None, 'tensor'), may hold values from -0.21875 to 0.21875
- proj_out: bfloat16 [2, 768, 768], P(None, 'tensor'), may hold values from -0.625 to 0.625
- bias_table: float32 [2, 32, 12], P(None, None, 'tensor'), may hold values from -4 to 4
- norm_gains: float32 [2, 2, 768], replicated, may hold values from 0.5 to 1.5
- router: bfloat16 [2, 768, 32], replicated, may hold values from -0.15625 to 0.15625
- expert_in: bfloat16 [2, 32, 768, 3072], P(None, 'expert', None, 'tensor'), may hold values from -0.21875 to 0.21875
- expert_out: bfloat16 [2, 32, 3072, 768], P(None, 'expert', 'tensor'), may hold values from -0.15625 to 0.15625
- cotangent: bfloat16 [4096, 768], P('expert'), may hold values from -6 to 6
Outputs:
- output: bfloat16 [4096, 768], P('expert')
- tokens_grad: float32 [4096, 768], P('expert')
- qkv_grad: float32 [2, 3, 768, 768], P(None, None, None, 'tensor')
- out_grad: float32 [2, 768, 768], P(None, 'tensor')
- table_grad: float32 [2, 32, 12], P(None, None, 'tensor')
- gains_grad: float32 [2, 2, 768], replicated
- router_grad: float32 [2, 768, 32], replicated
- expert_in_grad: float32 [2, 32, 768, 3072], P(None, 'expert', None, 'tensor')
- expert_out_grad: float32 [2, 32, 3072, 768], P(None, 'expert', 'tensor')
The draws below stay inside these ranges and needn't reach their ends.
Inputs may be any that keep to these rules, and one draw needn't show every extreme that they name: `expert_routes`: in each layer, no expert is named by more than 11 tokens of one packed row, a bound that some block reaches. `segment_ids`: within a row document numbers never fall; a document holds at most 64 tokens.
All inputs are finite; a program needn't handle non-finite values.
Results may differ from the reference program's by a relative error of at most 0.02.
Values may be sent and summed in bfloat16 or wider, within the bound.
No kernel may reach another device: no remote copies, remote signals or barrier semaphores. Data moves between devices by JAX's collectives and lax.ppermute only.
A program may use at most 128 MiB of HBM per device.

```python
import math
import jax
import jax.numpy as jnp
import numpy as np
from jax import lax

D = 768
FF = 3072
HEADS = 12
HD = 64
BUCKETS = 32
LAYERS = 2
DOCS = 8
TOK_DEV = 128
EXPERTS = 32
SEQS = 32
TOKENS = 4096
CAP = 11
N_EXPERT = 32


def place_ends(drawn, key, smallest, high):
    longest = drawn.shape.index(max(drawn.shape))
    spots = []
    for shift in (0, 1):
        where = [jax.random.randint(jax.random.fold_in(key, axis), (), 0, length) for axis, length in enumerate(drawn.shape)]
        where[longest] = (where[longest] + shift) % drawn.shape[longest]
        spots.append(tuple(where))
    return drawn.at[spots[0]].set(smallest).at[spots[1]].set(high)


def shard_levels(stream_key, extent, pieces, smallest, largest):
    def one(dim, parts):
        draws = jax.random.uniform(jax.random.fold_in(jax.random.fold_in(stream_key, 6), dim), (parts,), jnp.float32, smallest / len(pieces), largest / len(pieces))
        return jnp.repeat(jnp.exp(draws), extent[dim] // parts).reshape((-1,) + (1,) * (len(extent) - dim - 1))

    loudness = one(*pieces[0])
    for cut in pieces[1:]:
        loudness = loudness * one(*cut)
    return loudness


def split_up(count, total, bound, skew):
    weights = [(1 << 20) // math.isqrt(rank ** skew) + 1 for rank in range(2, count + 1)]
    surplus, given = total - bound - (count - 1), [1] * (count - 1)
    while surplus > 0:
        free = [i for i in range(count - 1) if given[i] < bound]
        whole, remaining = sum([weights[i] for i in free]), surplus
        for i in free:
            more = min(bound - given[i], max(1, remaining * weights[i] // whole), surplus)
            given[i] = given[i] + more
            surplus = surplus - more
    return np.array([bound] + given)


def ragged(stream_key, amount, total, most, slope):
    if amount == 2:
        one = jax.random.randint(stream_key, (), max(1, total - most), min(most, total - 1) + 1)
        return jnp.stack([one, total - one])
    sizes = jnp.asarray(split_up(amount, total, most, slope), jnp.int32)
    twos = (amount - 1) // 2
    source_of, sink = sizes[1:1 + 2 * twos:2], sizes[2:2 + 2 * twos:2]
    room = jnp.minimum(source_of - 1, most - sink)
    passed = jax.random.randint(jax.random.fold_in(stream_key, 1), (twos,), 0, 1 << 20) % (room + 1)
    sizes = sizes.at[1:1 + 2 * twos:2].set(source_of - passed).at[2:2 + 2 * twos:2].set(sink + passed)
    return sizes[jax.random.permutation(jax.random.fold_in(stream_key, 2), amount)]


def shared_out(rng, own, number, rows, amount, top, most, lean):
    order = jax.random.permutation(rng, amount)
    packed, ordinary = shares(amount, rows * top, most, lean, True), shares(amount, rows * top, most, lean, False)
    places = jnp.arange(amount)

    def named(tallies, turn):
        used = int((tallies > 0).sum())
        fixed = max(1, used // 4)
        moved = fixed + (places - fixed + turn * (used - fixed)) % max(1, amount - fixed)
        return jnp.zeros((amount,), jnp.int32).at[order[jnp.where(places < fixed, places, moved)]].set(jnp.asarray(tallies, jnp.int32))

    tallies = jnp.where(number % 4 == 0, named(packed, number // 4), named(ordinary, number - number // 4 - 1))
    mixed = jax.random.permutation(jax.random.fold_in(own, 3), amount)
    giver, sink = mixed[0:amount // 2 * 2:2], mixed[1:amount // 2 * 2:2]
    margin = jnp.minimum(tallies[giver] - 1, most - tallies[sink]) // 2
    margin = jnp.where((giver == order[0]) | (sink == order[0]) | (tallies[sink] == 0), 0, jnp.maximum(margin, 0))
    moved = jax.random.randint(jax.random.fold_in(own, 4), (amount // 2,), 0, 1 << 20) % (margin + 1)
    tallies = tallies.at[giver].add(-moved).at[sink].add(moved)
    members = jnp.searchsorted(jnp.cumsum(tallies), jnp.arange(rows * top), side="right").astype(jnp.int32)
    grid = members.reshape(top, rows).T
    grid = grid[jax.random.permutation(jax.random.fold_in(own, 1), rows)]
    turn = jax.random.randint(jax.random.fold_in(own, 2), (rows, 1), 0, top)
    return jnp.take_along_axis(grid, (jnp.arange(top)[None, :] + turn) % top, axis=1)


def shares(number_of, total, bound, skew, full):
    loads = [(1 << 20) // math.isqrt(standing ** skew) + 1 for standing in range(1, number_of + 1)]
    largest = bound if full else min(bound, max(-(-total // number_of), total * loads[0] // sum(loads)))
    least = 1 if total - largest >= number_of - 1 else 0
    holding, spare = [largest] + [least] * (number_of - 1), total - largest - least * (number_of - 1)
    while spare > 0:
        candidates = [i for i in range(1, number_of) if holding[i] < largest] or [i for i in range(1, number_of) if holding[i] < bound]
        whole, remaining = sum([loads[i] for i in candidates]), spare
        for i in candidates:
            more = min(bound - holding[i], max(1, remaining * loads[i] // whole), spare)
            holding[i] = holding[i] + more
            spare = spare - more
    return np.array(holding)


def gaussian(key, extent, scale, bound, split=(), kind=jnp.bfloat16):
    factor_of = shard_levels(key, extent, split, -0.22, 0.18) if split else 1.0
    values = jax.random.normal(key, extent, jnp.float32) * scale * factor_of
    return jnp.minimum(jnp.maximum(values, -bound), bound).astype(kind)


def setup_inputs(seed: int = 0) -> dict:
    streams_of = jax.random.split(jax.random.key(seed), 13)
    tokens = gaussian(streams_of[0], (TOKENS, D), 1.0, 6.0, ((0, 32),))
    segment_ids = jax.vmap(lambda own: jnp.searchsorted(jnp.cumsum(ragged(own, DOCS, TOK_DEV, TOK_DEV // 2, 0)), jnp.arange(TOK_DEV), side="right"))(jax.random.split(streams_of[1], SEQS)).reshape((SEQS, TOK_DEV)).astype(jnp.int32)
    expert_routes_keys = jax.random.split(jax.random.fold_in(streams_of[2], 1), LAYERS * TOKENS // TOK_DEV)
    expert_routes_turns = jax.random.permutation(jax.random.fold_in(streams_of[2], 3), LAYERS * TOKENS // TOK_DEV)
    expert_routes = jax.vmap(lambda own, number: shared_out(jax.random.fold_in(streams_of[2], 2), own, number, TOK_DEV, EXPERTS, 2, CAP, 1))(expert_routes_keys, expert_routes_turns).reshape((LAYERS, TOKENS, 2))
    bucket_ids = place_ends(jax.random.randint(streams_of[3], (2 * TOK_DEV - 1,), 0, BUCKETS), jax.random.fold_in(streams_of[3], 1), 0, BUCKETS - 1).astype(jnp.int32)
    proj_qkv = gaussian(streams_of[4], (LAYERS, 3, D, D), D ** -0.5, 0.21875, ((3, 4),))
    proj_out = gaussian(streams_of[5], (LAYERS, D, D), (D // 8) ** -0.5, 0.625, ((1, 4),))
    bias_table = gaussian(streams_of[6], (LAYERS, BUCKETS, HEADS), 1.0, 4.0, ((2, 4),), jnp.float32)
    norm_gains = jnp.clip(1.0 + 0.1 * jax.random.normal(streams_of[7], (LAYERS, 2, D), jnp.float32), 0.5, 1.5)
    router = gaussian(streams_of[8], (LAYERS, D, EXPERTS), (2 * D) ** -0.5, 0.15625)
    expert_in = gaussian(streams_of[9], (LAYERS, EXPERTS, D, FF), D ** -0.5, 0.21875, ((1, 32), (3, 4)))
    expert_out = gaussian(streams_of[10], (LAYERS, EXPERTS, FF, D), (FF // 2) ** -0.5, 0.15625, ((1, 32), (2, 4)))
    cotangent = gaussian(streams_of[11], (TOKENS, D), 1.0, 6.0, ((0, 32),))
    return {"tokens": tokens, "segment_ids": segment_ids, "expert_routes": expert_routes, "bucket_ids": bucket_ids, "proj_qkv": proj_qkv, "proj_out": proj_out, "bias_table": bias_table, "norm_gains": norm_gains, "router": router, "expert_in": expert_in, "expert_out": expert_out, "cotangent": cotangent}


@jax.custom_vjp
def low(v):
    return lax.optimization_barrier(v.astype(jnp.bfloat16)).astype(jnp.float32)

@jax.custom_vjp
def low_back(v):
    return v

def low_keep(v):
    return (low(v), None)

def low_pass(kept, grad):
    return (grad,)

def back_keep(v):
    return (v, None)

def back_low(kept, grad):
    return (low(grad),)
low.defvjp(low_keep, low_pass)
low_back.defvjp(back_keep, back_low)
epsilon = 1e-06
masked_score = -1000000000.0
highest = lax.Precision.HIGHEST

def norm_rows(values, gain_row):
    return values * lax.rsqrt(lax.optimization_barrier(jnp.mean(values * values, axis=-1, keepdims=True)) + epsilon) * gain_row

def slot_tables(routes_here):
    labels = jnp.arange(EXPERTS, dtype=jnp.int32)
    first_hot = (routes_here[:, 0:1] == labels).astype(jnp.float32)
    second_hot = (routes_here[:, 1:2] == labels).astype(jnp.float32)
    token_order = jnp.arange(routes_here.shape[0], dtype=jnp.int32)
    before = (token_order[None, :] < token_order[:, None]).astype(jnp.float32)
    counts = jnp.dot(before, first_hot + second_hot, precision=highest, preferred_element_type=jnp.float32)
    places = jnp.arange(CAP, dtype=jnp.float32)
    tables = []
    for chosen_hot in (first_hot, second_hot):
        slot_place = lax.optimization_barrier(jnp.sum(counts * chosen_hot, axis=1, keepdims=True))
        table_part = chosen_hot[:, :, None] * (slot_place[:, :, None] == places).astype(jnp.float32)
        tables.append(table_part.reshape(routes_here.shape[0], EXPERTS * CAP))
    return (first_hot, second_hot, jnp.stack(tables))

def bias_rows(table_part, bucket_ids, row_count):
    position = jnp.arange(row_count, dtype=jnp.int32)
    offsets = position[:, None] - position[None, :] + row_count - 1
    picked_ids = jnp.take(bucket_ids, offsets)
    labels = jnp.arange(table_part.shape[0], dtype=jnp.int32)
    bucket_hot = (picked_ids[:, :, None] == labels).astype(jnp.float32)
    return jnp.einsum('tsb,bh->hts', bucket_hot, table_part, precision=highest)

def attend(normed, qkv_layer, out_layer, position_bias, segment_row):
    row_count = normed.shape[0]
    triple = jnp.einsum('td,kde->kte', normed, qkv_layer, precision=highest)
    triple = low(low_back(triple)).reshape(3, row_count, HEADS, HD)
    raw = jnp.einsum('thc,shc->hts', triple[0], triple[1], precision=highest) * HD ** (-0.5) + position_bias
    raw = low_back(raw)
    position = jnp.arange(row_count, dtype=jnp.int32)
    allowed = (segment_row[:, None] == segment_row[None, :]) & (position[None, :] <= position[:, None])
    weights = low(jax.nn.softmax(jnp.where(allowed[None], raw, masked_score), axis=-1))
    mixture = jnp.einsum('hts,shc->thc', weights, triple[2], precision=highest).reshape(row_count, D)
    mixture = low(low_back(mixture))
    return low_back(jnp.dot(mixture, out_layer, precision=highest, preferred_element_type=jnp.float32))

def layer(current, qkv_layer, out_layer, table_part, gain_pair, router_layer, in_layer, back_layer, routes_layer, bucket_ids, segment_ids):
    position_bias = bias_rows(table_part, bucket_ids, TOK_DEV)
    normed = low(norm_rows(current, gain_pair[0]))
    attention = jax.vmap(lambda rows_in, segment_row: attend(rows_in, qkv_layer, out_layer, position_bias, segment_row))(normed, segment_ids)
    middle = current + attention
    normed_two = low(norm_rows(middle, gain_pair[1]))
    logits = jnp.einsum('ntd,de->nte', normed_two, router_layer, precision=highest)
    first_hot, second_hot, tables = jax.vmap(slot_tables)(routes_layer)
    chosen = jnp.stack([lax.optimization_barrier(jnp.sum(logits * first_hot, axis=-1)), lax.optimization_barrier(jnp.sum(logits * second_hot, axis=-1))], axis=-1)
    gates = jax.nn.softmax(chosen, axis=-1)
    outgoing = jnp.einsum('nktc,ntd->ncd', tables, normed_two, precision=highest)
    arrived = outgoing.reshape(N_EXPERT, EXPERTS, CAP, D).transpose(1, 0, 2, 3).reshape(EXPERTS, N_EXPERT * CAP, D)
    arrived = low_back(arrived)
    hidden_pre = low_back(jnp.einsum('erd,edf->erf', arrived, in_layer, precision=highest))
    activated = low(jax.nn.gelu(hidden_pre))
    produced = low(low_back(jnp.einsum('erf,efd->erd', activated, back_layer, precision=highest)))
    returned = produced.reshape(EXPERTS, N_EXPERT, CAP, D).transpose(1, 0, 2, 3).reshape(N_EXPERT, EXPERTS * CAP, D)
    picked = jnp.einsum('nktc,ncd->nktd', tables, returned, precision=highest)
    return middle + gates[..., 0:1] * picked[:, 0] + gates[..., 1:2] * picked[:, 1]

def reference(tokens, segment_ids, expert_routes, bucket_ids, proj_qkv, proj_out, bias_table, norm_gains, router, expert_in, expert_out, cotangent):
    routes_split = expert_routes.reshape(LAYERS, N_EXPERT, TOK_DEV, 2)

    def forward(tokens_in, qkv_all, out_all, table_all, gain_all, router_all, in_all, back_all):
        current = tokens_in.reshape(N_EXPERT, TOK_DEV, D)
        for layer_index in range(LAYERS):
            current = layer(current, qkv_all[layer_index], out_all[layer_index], table_all[layer_index], gain_all[layer_index], router_all[layer_index], in_all[layer_index], back_all[layer_index], routes_split[layer_index], bucket_ids, segment_ids)
        return current.reshape(TOKENS, D)
    primals = tuple((argument.astype(jnp.float32) for argument in (tokens, proj_qkv, proj_out, bias_table, norm_gains, router, expert_in, expert_out)))
    result, pull_back = jax.vjp(forward, *primals)
    grads = pull_back(cotangent.astype(jnp.float32))
    return (result.astype(jnp.bfloat16), grads[0], grads[1], grads[2], grads[3], grads[4], grads[5], grads[6], grads[7])
```

```python
import jax
import jax.numpy as jnp
from jax import lax
from jax.experimental import pallas as pl
from jax.experimental.pallas import tpu as pltpu
from jax.sharding import PartitionSpec as P

epsilon = 1e-06
masked_score = -1000000000.0
highest = lax.Precision.HIGHEST
f32, bf16 = jnp.float32, jnp.bfloat16

ROWS = 128
WIDTH = 768
QUARTER = 192
HERE = 3
HEAD = 64
EXPERTS = 32
MAIN = EXPERTS * 8
REST = 128
HALF = WIDTH // 2
SENT = WIDTH + HALF
SUMMED = WIDTH + 128
VMEM = 40 * 1024 * 1024


def call(body, outs, *operands, cost=0):
    return pl.pallas_call(
        body,
        out_shape=[jax.ShapeDtypeStruct(shape, dtype) for shape, dtype in outs],
        in_specs=[pl.BlockSpec(memory_space=pltpu.VMEM)] * len(operands),
        out_specs=[pl.BlockSpec(memory_space=pltpu.VMEM)] * len(outs),
        compiler_params=pltpu.CompilerParams(vmem_limit_bytes=VMEM),
        cost_estimate=pl.CostEstimate(
            flops=cost, transcendentals=0, bytes_accessed=sum(o.size * o.dtype.itemsize for o in operands)
        ),
        name=body.__name__,
    )(*operands)


def dot(left, right, left_axis=1, right_axis=0, precision=None):
    return lax.dot_general(
        left,
        right,
        (((left_axis,), (right_axis,)), ((), ())),
        precision=precision,
        preferred_element_type=f32,
    )


def iota(shape, axis):
    return lax.broadcasted_iota(jnp.int32, shape, axis)


def scale_of(values):
    return lax.rsqrt(jnp.mean(values * values, axis=-1, keepdims=True) + epsilon)


def norm_back(values, gain, upstream):
    inverse = scale_of(values)
    inner = upstream * gain
    mean = jnp.mean(inner * values, axis=-1, keepdims=True)
    back = inverse * inner - values * (inverse * inverse * inverse * mean)
    return back, jnp.sum(upstream * (values * inverse), axis=0, keepdims=True)


def head_mask(head):
    lane = iota((1, QUARTER), 1)
    return ((lane >= head * HEAD) & (lane < (head + 1) * HEAD)).astype(f32).astype(bf16)


def four(own, one, two, three):
    return (own.astype(f32) + two.astype(f32)) + (one.astype(f32) + three.astype(f32))


def column_of(row, size):
    same = iota((size, size), 0) == iota((size, size), 1)
    return jnp.sum(jnp.where(same, jnp.broadcast_to(row, (size, size)), 0.0), axis=1, keepdims=True)


def row_of(column, size):
    same = iota((size, size), 0) == iota((size, size), 1)
    return jnp.sum(jnp.where(same, jnp.broadcast_to(column, (size, size)), 0.0), axis=0, keepdims=True)


def setup(ids_ref, table_ref, segment_ref, routes_ref, bias_ref, across_ref, down_ref):
    hot = (iota((EXPERTS, 256), 0) == ids_ref[...]).astype(f32)
    by_offset = dot(table_ref[...], hot, precision=highest)
    segment = segment_ref[...].astype(f32)
    allowed = (column_of(segment, ROWS) == segment) & (iota((ROWS, ROWS), 1) <= iota((ROWS, ROWS), 0))
    for which in range(2 * HERE):
        line = jnp.broadcast_to(by_offset[which : which + 1, :], (ROWS, 256))
        placed = pltpu.roll(line, 129, axis=1, stride=1, stride_axis=0)[:, :ROWS]
        bias_ref[which] = jnp.where(allowed, placed, masked_score)
    lane = iota((ROWS, ROWS), 1)
    before = (lane < iota((ROWS, ROWS), 0)).astype(f32).astype(bf16)
    for layer in range(2):
        routes = routes_ref[layer]
        expert = [routes[:, k : k + 1].astype(f32) for k in range(2)]
        hots = [(lane.astype(f32) == expert[k]).astype(f32) for k in range(2)]
        counts = dot(before, (hots[0] + hots[1]).astype(bf16))
        columns = []
        for k in range(2):
            slot = jnp.sum(counts * hots[k], axis=1, keepdims=True)
            first = slot < 7.5
            base = expert[k] * 8.0
            columns.append(jnp.where(first, base + slot, -1.0))
            columns.append(jnp.where(first, -1.0, base + (slot - 8.0) * 2.0))
            columns.append(jnp.where(first, -1.0, base + (slot - 8.0) * 2.0 + 1.0))
        columns.extend(expert)
        across = jnp.zeros((ROWS, ROWS), f32)
        down = jnp.zeros((8, ROWS), f32)
        for place, column in enumerate(columns):
            across = jnp.where(lane == place, column, across)
            down = jnp.where(iota((8, ROWS), 0) == place, row_of(column, ROWS), down)
        across_ref[layer] = across
        down_ref[layer] = down


def one_hot(flags):
    return flags.astype(f32).astype(bf16)


def dispatch(down, rows):
    place = iota((MAIN, ROWS), 0).astype(f32)
    tables = [one_hot(place == down[n : n + 1, :]) for n in range(6)]
    if len(rows) == 1:
        pairs = [([tables[n] + tables[n + 3] for n in range(3)], rows[0])]
    else:
        pairs = [(tables[:3], rows[0]), (tables[3:], rows[1])]
    main, rest = 0.0, 0.0
    for (whole, low, high), row in pairs:
        main = main + dot(whole, row)
        rest = rest + dot(low, row[:, :HALF]) + dot(high, row[:, HALF:])
    return main.astype(bf16), rest.astype(bf16)


def pick(across, route, main, rest):
    place = iota((ROWS, MAIN), 1).astype(f32)
    whole, low, high = [
        one_hot(place == across[:, 3 * route + n : 3 * route + n + 1]) for n in range(3)
    ]
    whole_part = dot(whole, main)
    return whole_part[:, :HALF] + dot(low, rest), whole_part[:, HALF:] + dot(high, rest)


def rest_tables():
    row = iota((REST, MAIN), 0)
    target = (row & 31) * 8 + (row >> 5) * 2
    lane = iota((REST, MAIN), 1)
    real = row < 96
    return one_hot((lane == target) & real), one_hot((lane == target + 1) & real)


def unpack(packed_ref, offset, into_ref):
    low, high = rest_tables()
    rest = packed_ref[:, offset + WIDTH : offset + SENT]
    into_ref[0:MAIN, :] = packed_ref[:, offset : offset + WIDTH]
    into_ref[MAIN : MAIN + REST, 0:HALF] = dot(low, rest).astype(bf16)
    into_ref[MAIN : MAIN + REST, HALF:WIDTH] = dot(high, rest).astype(bf16)


def pack(rows, offset, into_ref):
    low, high = rest_tables()
    into_ref[:, offset : offset + WIDTH] = rows[:MAIN]
    into_ref[:, offset + WIDTH : offset + SENT] = (
        dot(low, rows[MAIN:, :HALF], 0) + dot(high, rows[MAIN:, HALF:], 0)
    ).astype(bf16)


def attend(current, gain_ref, qkv_ref, bias_ref, low_ref, triple_ref, weights_ref):
    low = (current * scale_of(current) * gain_ref[...]).astype(bf16)
    low_ref[...] = low
    for k in range(3):
        triple_ref[k] = dot(low, qkv_ref[k]).astype(bf16)
    mixture = jnp.zeros((ROWS, QUARTER), f32)
    for head in range(HERE):
        mask = head_mask(head)
        scores = dot(triple_ref[0] * mask, triple_ref[1], 1, 1) * HEAD**-0.5 + bias_ref[head]
        scores = scores - jnp.max(scores, axis=-1, keepdims=True)
        raised = jnp.exp(scores)
        weights = raised / jnp.sum(raised, axis=-1, keepdims=True)
        weights_ref[head] = weights
        mixture = mixture + dot(weights.astype(bf16), triple_ref[2] * mask)
    return mixture.astype(bf16)


def attention_first(
    tokens_ref, gain_ref, qkv_ref, bias_ref, out_ref, low_ref, triple_ref, weights_ref, mixture_ref, part_ref
):
    mixture = attend(
        tokens_ref[...].astype(f32), gain_ref, qkv_ref, bias_ref, low_ref, triple_ref, weights_ref
    )
    mixture_ref[...] = mixture
    part_ref[...] = dot(mixture, out_ref[...]).astype(bf16)


def attention_next(
    middle_ref,
    z0,
    z1,
    z2,
    z3,
    gain_ref,
    qkv_ref,
    bias_ref,
    out_ref,
    current_ref,
    low_ref,
    triple_ref,
    weights_ref,
    mixture_ref,
    part_ref,
):
    current = middle_ref[...] + four(z0[...], z1[...], z2[...], z3[...])
    current_ref[...] = current
    mixture = attend(current, gain_ref, qkv_ref, bias_ref, low_ref, triple_ref, weights_ref)
    mixture_ref[...] = mixture
    part_ref[...] = dot(mixture, out_ref[...]).astype(bf16)


def route_rows(middle, gain_ref, router_ref, across, low_ref, gates_ref):
    low = (middle * scale_of(middle) * gain_ref[...]).astype(bf16)
    low_ref[...] = low
    logits = dot(low, router_ref[...])
    lane = iota((ROWS, EXPERTS), 1).astype(f32)
    chosen = [
        jnp.sum(jnp.where(lane == across[:, 6 + k : 7 + k], logits, 0.0), axis=1, keepdims=True)
        for k in range(2)
    ]
    top = jnp.maximum(chosen[0], chosen[1])
    raised = [jnp.exp(c - top) for c in chosen]
    total = raised[0] + raised[1]
    gates = [r / total for r in raised]
    place = iota((ROWS, ROWS), 1)
    gates_ref[...] = jnp.where(place == 0, gates[0], jnp.where(place == 1, gates[1], 0.0))
    return low, gates


def route_first(
    current_ref,
    p0,
    p1,
    p2,
    p3,
    gain_ref,
    router_ref,
    across_ref,
    down_ref,
    middle_ref,
    low_ref,
    gates_ref,
    send_ref,
):
    middle = current_ref[...].astype(f32) + four(p0[...], p1[...], p2[...], p3[...])
    middle_ref[...] = middle
    low, gates = route_rows(middle, gain_ref, router_ref, across_ref[...], low_ref, gates_ref)
    main, rest = dispatch(down_ref[...], [low])
    send_ref[:, :WIDTH] = main
    send_ref[:, WIDTH:] = rest


def route_next(
    current_ref,
    p0,
    p1,
    p2,
    p3,
    gain_ref,
    router_ref,
    across_ref,
    down_ref,
    cotangent_ref,
    middle_ref,
    low_ref,
    gates_ref,
    send_ref,
):
    middle = current_ref[...].astype(f32) + four(p0[...], p1[...], p2[...], p3[...])
    middle_ref[...] = middle
    low, gates = route_rows(middle, gain_ref, router_ref, across_ref[...], low_ref, gates_ref)
    main, rest = dispatch(down_ref[...], [low])
    send_ref[:, :WIDTH] = main
    send_ref[:, WIDTH:SENT] = rest
    gradient = cotangent_ref[...].astype(f32)
    main, rest = dispatch(down_ref[...], [(gate * gradient).astype(bf16) for gate in gates])
    send_ref[:, SENT : SENT + WIDTH] = main
    send_ref[:, SENT + WIDTH :] = rest


CURVE = (2.0 / 3.141592653589793) ** 0.5


def gelu_parts(values):
    squared = values * values
    bent = jnp.tanh(CURVE * values * (1.0 + 0.044715 * squared))
    return bent, squared


def gelu(values):
    bent, _ = gelu_parts(values)
    return 0.5 * values * (1.0 + bent)


def gelu_slope(values):
    bent, squared = gelu_parts(values)
    inner = CURVE * (1.0 + 3.0 * 0.044715 * squared)
    return 0.5 * (1.0 + bent) + 0.5 * values * (1.0 - bent * bent) * inner


def expert_forward(got_ref, in_ref, out_ref, rows_ref, before_ref, active_ref, back_ref):
    unpack(got_ref, 0, rows_ref)
    before = dot(rows_ref[...], in_ref[...])
    before_ref[...] = before
    active = gelu(before).astype(bf16)
    active_ref[...] = active
    pack(dot(active, out_ref[...]).astype(bf16), 0, back_ref)


def expert_backward(got_ref, before_ref, in_ref, out_ref, grads_ref, down_ref, back_ref):
    unpack(got_ref, 0, grads_ref)
    grad_active = dot(grads_ref[...], out_ref[...], 1, 1)
    grad_before = (grad_active * gelu_slope(before_ref[...])).astype(bf16)
    down_ref[...] = grad_before
    pack(dot(grad_before, in_ref[...], 1, 1).astype(bf16), 0, back_ref)


def expert_both(got_ref, in_ref, out_ref, rows_ref, active_ref, grads_ref, down_ref, back_ref):
    unpack(got_ref, 0, rows_ref)
    unpack(got_ref, SENT, grads_ref)
    before = dot(rows_ref[...], in_ref[...])
    active = gelu(before).astype(bf16)
    active_ref[...] = active
    pack(dot(active, out_ref[...]).astype(bf16), 0, back_ref)
    grad_active = dot(grads_ref[...], out_ref[...], 1, 1)
    grad_before = (grad_active * gelu_slope(before)).astype(bf16)
    down_ref[...] = grad_before
    pack(dot(grad_before, in_ref[...], 1, 1).astype(bf16), SENT, back_ref)


def expert_grads_top(rows_ref, active_ref, grads_ref, down_ref, in_grad_ref, out_grad_ref):
    in_grad_ref[0, 0] = dot(rows_ref[...], down_ref[...], 0)
    out_grad_ref[0, 0] = dot(active_ref[...], grads_ref[...], 0)


def combine_first(got_ref, across_ref, gates_ref, part_ref, picked_ref):
    main, rest = got_ref[:, :WIDTH], got_ref[:, WIDTH:]
    across, gates = across_ref[...], gates_ref[...]
    left, right = 0.0, 0.0
    for route in range(2):
        one, two = pick(across, route, main, rest)
        picked_ref[route, :, :HALF] = one.astype(bf16)
        picked_ref[route, :, HALF:] = two.astype(bf16)
        left = left + gates[:, route : route + 1] * one
        right = right + gates[:, route : route + 1] * two
    part_ref[:, :HALF] = left.astype(bf16)
    part_ref[:, HALF:] = right.astype(bf16)


def gate_lanes(grads):
    place = iota((ROWS, 128), 1)
    both = jnp.where(place == 0, grads[0], jnp.where(place == 1, grads[1], 0.0))
    high = both.astype(bf16)
    moved = jnp.where(place == 2, grads[0], jnp.where(place == 3, grads[1], 0.0))
    low = (moved - moved.astype(bf16).astype(f32)).astype(bf16)
    return high + low


def gathered_back(got_ref, offset, across, into_ref):
    main = got_ref[:, offset : offset + WIDTH]
    rest = got_ref[:, offset + WIDTH : offset + SENT]
    left, right = pick(across, 0, main, rest)
    other_left, other_right = pick(across, 1, main, rest)
    into_ref[:, :HALF] = (left + other_left).astype(bf16)
    into_ref[:, HALF:WIDTH] = (right + other_right).astype(bf16)


def combine_next(got_ref, across_ref, gates_ref, cotangent_ref, part_ref, back_ref):
    main, rest = got_ref[:, :WIDTH], got_ref[:, WIDTH:SENT]
    across, gates = across_ref[...], gates_ref[...]
    gradient = cotangent_ref[...].astype(f32)
    left, right, grads = 0.0, 0.0, []
    for route in range(2):
        one, two = pick(across, route, main, rest)
        left = left + gates[:, route : route + 1] * one
        right = right + gates[:, route : route + 1] * two
        grads.append(
            jnp.sum(gradient[:, :HALF] * one + gradient[:, HALF:] * two, axis=1, keepdims=True)
        )
    part_ref[:, :HALF] = left.astype(bf16)
    part_ref[:, HALF:] = right.astype(bf16)
    gathered_back(got_ref, SENT, across, back_ref)
    back_ref[:, WIDTH:] = gate_lanes(grads)


def combine_back(got_ref, across_ref, lanes_ref, back_ref):
    gathered_back(got_ref, 0, across_ref[...], back_ref)
    back_ref[:, WIDTH:] = lanes_ref[...]


def attention_back(
    e0,
    e1,
    e2,
    e3,
    gates_ref,
    across_ref,
    router_ref,
    middle_ref,
    gain_ref,
    gradient_ref,
    out_ref,
    triple_ref,
    weights_ref,
    qkv_ref,
    ids_ref,
    after_ref,
    low_ref,
    back_triple_ref,
    part_ref,
    logits_ref,
    gain_grad_ref,
    table_grad_ref,
):
    total = four(e0[...], e1[...], e2[...], e3[...])
    gates = gates_ref[...]
    across = across_ref[...]
    gate = [gates[:, k : k + 1] for k in range(2)]
    grad_gate = [
        total[:, WIDTH + k : WIDTH + k + 1] + total[:, WIDTH + 2 + k : WIDTH + 3 + k] for k in range(2)
    ]
    mean = gate[0] * grad_gate[0] + gate[1] * grad_gate[1]
    lane = iota((ROWS, EXPERTS), 1).astype(f32)
    grad_logits = 0.0
    for k in range(2):
        grad_logits = grad_logits + jnp.where(
            lane == across[:, 6 + k : 7 + k], gate[k] * (grad_gate[k] - mean), 0.0
        )
    high = grad_logits.astype(bf16)
    low = (grad_logits - high.astype(f32)).astype(bf16)
    logits_ref[:, :EXPERTS] = high
    logits_ref[:, EXPERTS : 2 * EXPERTS] = low
    logits_ref[:, 2 * EXPERTS :] = jnp.zeros((ROWS, 128 - 2 * EXPERTS), bf16)
    grad_low = total[:, :WIDTH] + dot(high, router_ref[...], 1, 1) + dot(low, router_ref[...], 1, 1)
    grad_middle, gain_grad_ref[...] = norm_back(middle_ref[...], gain_ref[...], grad_low)
    after = gradient_ref[...].astype(f32) + grad_middle
    after_ref[...] = after
    low_after = after.astype(bf16)
    low_ref[...] = low_after
    grad_mixture = dot(low_after, out_ref[...], 1, 1).astype(bf16)
    queries, keys, values = triple_ref[0], triple_ref[1], triple_ref[2]
    grad_queries = jnp.zeros((ROWS, QUARTER), f32)
    grad_keys, grad_values = grad_queries, grad_queries
    diagonals = jnp.zeros((8, 256), f32)
    flip = one_hot(iota((ROWS, ROWS), 0) + iota((ROWS, ROWS), 1) == ROWS - 1)
    for head in range(HERE):
        mask = head_mask(head)
        masked_grad = grad_mixture * mask
        weights = weights_ref[head]
        grad_values = grad_values + dot(weights.astype(bf16), masked_grad, 0)
        grad_weights = dot(masked_grad, values, 1, 1)
        grad_scores = weights * (
            grad_weights - jnp.sum(weights * grad_weights, axis=-1, keepdims=True)
        )
        grad_scores = grad_scores.astype(bf16)
        grad_queries = grad_queries + dot(grad_scores, keys * mask)
        grad_keys = grad_keys + dot(grad_scores, queries * mask, 0)
        wide = jnp.concatenate([dot(flip, grad_scores), jnp.zeros((ROWS, 128), f32)], axis=1)
        turned = pltpu.roll(wide, 0, axis=1, stride=1, stride_axis=0)
        diagonals = jnp.where(
            iota((8, 256), 0) == head, jnp.sum(turned, axis=0, keepdims=True), diagonals
        )
    hot = (iota((EXPERTS, 256), 0) == ids_ref[...]).astype(f32)
    table_grad_ref[...] = dot(diagonals, hot, 1, 1, precision=highest)
    grad_input = 0.0
    for k, grad in enumerate((grad_queries * HEAD**-0.5, grad_keys * HEAD**-0.5, grad_values)):
        grad = grad.astype(bf16)
        back_triple_ref[:, k * QUARTER : (k + 1) * QUARTER] = grad
        grad_input = grad_input + dot(grad, qkv_ref[k], 1, 1)
    part_ref[...] = grad_input.astype(bf16)


def weight_grads(low_ref, back_triple_ref, mixture_ref, after_ref, low_two_ref, logits_ref, grads_ref):
    kind = grads_ref.dtype
    grads_ref[:, : 3 * QUARTER] = dot(low_ref[...], back_triple_ref[...], 0).astype(kind)
    for part in range(4):
        grads_ref[part * QUARTER : (part + 1) * QUARTER, 3 * QUARTER : WIDTH] = dot(
            mixture_ref[...], after_ref[:, part * QUARTER : (part + 1) * QUARTER], 0
        ).astype(kind)
    both = dot(low_two_ref[...], logits_ref[...], 0)
    grads_ref[:, WIDTH : WIDTH + EXPERTS] = (
        both[:, :EXPERTS] + both[:, EXPERTS : 2 * EXPERTS]
    ).astype(kind)
    grads_ref[:, WIDTH + EXPERTS :] = jnp.zeros((WIDTH, 128 - EXPERTS), kind)


def start_back(
    after_ref,
    d0,
    d1,
    d2,
    d3,
    input_ref,
    gain_ref,
    gates_ref,
    down_ref,
    picked_ref,
    gradient_ref,
    gain_grad_ref,
    lanes_ref,
    send_ref,
):
    grad_low = four(d0[...], d1[...], d2[...], d3[...])
    grad_input, gain_grad_ref[...] = norm_back(input_ref[...].astype(f32), gain_ref[...], grad_low)
    gradient = after_ref[...] + grad_input
    gradient_ref[...] = gradient
    gates = gates_ref[...]
    weighted = [(gates[:, k : k + 1] * gradient).astype(bf16) for k in range(2)]
    main, rest = dispatch(down_ref[...], weighted)
    send_ref[:, :WIDTH] = main
    send_ref[:, WIDTH:] = rest
    lanes_ref[...] = gate_lanes(
        [jnp.sum(gradient * picked_ref[k].astype(f32), axis=1, keepdims=True) for k in range(2)]
    )


def finish_back(after_ref, d0, d1, d2, d3, input_ref, gain_ref, gradient_ref, gain_grad_ref):
    grad_low = four(d0[...], d1[...], d2[...], d3[...])
    grad_input, gain_grad_ref[...] = norm_back(input_ref[...].astype(f32), gain_ref[...], grad_low)
    gradient_ref[...] = after_ref[...] + grad_input


def finish_output(middle_ref, z0, z1, z2, z3, output_ref):
    output_ref[...] = (middle_ref[...] + four(z0[...], z1[...], z2[...], z3[...])).astype(bf16)


def add_chunks(chunks_ref, g00, g01, g10, g11, t0, t1, spread_ref):
    share = WIDTH // EXPERTS
    total = chunks_ref[0:share, :].astype(f32)
    for block in range(1, EXPERTS):
        total = total + chunks_ref[block * share : (block + 1) * share, :].astype(f32)
    total = total.astype(bf16)
    row = iota((8, WIDTH), 0)
    gains = jnp.zeros((8, WIDTH), f32)
    for place, gain in enumerate((g00, g01, g10, g11)):
        gains = jnp.where(row == place, gain[...], gains)
    tables = jnp.concatenate([t0[0:4, :], t1[0:4, :]], axis=0)
    tables = jnp.concatenate([tables, jnp.zeros((8, 128 - EXPERTS), f32)], axis=1)
    small = jnp.concatenate([gains, tables], axis=1).astype(bf16)
    for block in range(EXPERTS):
        spread_ref[block * 32 : block * 32 + share, :] = total
        spread_ref[block * 32 + share : block * 32 + 32, :] = small


def place_grads(top_ref, all_ref, qkv_ref, out_ref, router_ref, gains_ref, tables_ref):
    share = WIDTH // EXPERTS
    small = jnp.zeros((8, SUMMED), f32)
    for block in range(EXPERTS):
        rows = slice(block * share, (block + 1) * share)
        chunk = all_ref[block * 32 : block * 32 + share, :].astype(f32)
        small = small + all_ref[block * 32 + share : block * 32 + 32, :].astype(f32)
        for k in range(3):
            qkv_ref[0, k, rows, :] = chunk[:, k * QUARTER : (k + 1) * QUARTER]
        part, first = divmod(block * share, QUARTER)
        out_ref[0, first : first + share, part * QUARTER : (part + 1) * QUARTER] = chunk[
            :, 3 * QUARTER : WIDTH
        ]
        router_ref[0, rows, :] = chunk[:, WIDTH : WIDTH + EXPERTS]
    for k in range(3):
        qkv_ref[1, k] = top_ref[:, k * QUARTER : (k + 1) * QUARTER]
    for part in range(4):
        out_ref[1, :, part * QUARTER : (part + 1) * QUARTER] = top_ref[
            part * QUARTER : (part + 1) * QUARTER, 3 * QUARTER : WIDTH
        ]
    router_ref[1] = top_ref[:, WIDTH : WIDTH + EXPERTS]
    gains_ref[...] = small[:, :WIDTH]
    tables_ref[...] = small[:, WIDTH:]


def around(values):
    sent = [
        lax.ppermute(values, "tensor", [(i, (i + shift) % 4) for i in range(4)]) for shift in (1, 2, 3)
    ]
    return [values, *sent]


def across_experts(values):
    return lax.all_to_all(values, "expert", 0, 0, tiled=True)


def shards(
    tokens,
    segment_ids,
    expert_routes,
    bucket_ids,
    proj_qkv,
    proj_out,
    bias_table,
    norm_gains,
    router,
    expert_in,
    expert_out,
    cotangent,
):
    ids = jnp.pad(jnp.flip(bucket_ids), (0, 1), constant_values=-1).reshape(1, 256)
    table = jnp.pad(bias_table.transpose(0, 2, 1).reshape(2 * HERE, EXPERTS), ((0, 2), (0, 0)))
    gains = norm_gains.reshape(4, 1, WIDTH)
    row = (ROWS, WIDTH)
    narrow = (ROWS, QUARTER)
    scores = (HERE, ROWS, ROWS)
    slots = (MAIN + REST, WIDTH)
    bias, across, down = call(
        setup,
        [((2 * HERE, ROWS, ROWS), f32), ((2, ROWS, ROWS), f32), ((2, 8, ROWS), f32)],
        ids,
        table,
        segment_ids,
        expert_routes,
    )
    kept = [(row, bf16), ((3, *narrow), bf16), (scores, f32), (narrow, bf16), (row, bf16)]

    low_a0, triple0, weights0, mixture0, part = call(
        attention_first, kept, tokens, gains[0], proj_qkv[0], bias[:HERE], proj_out[0]
    )
    middle0, low_b0, gates0, send = call(
        route_first,
        [(row, f32), (row, bf16), ((ROWS, ROWS), f32), ((MAIN, SENT), bf16)],
        tokens,
        *around(part),
        gains[1],
        router[0],
        across[0],
        down[0],
    )
    rows0, before0, active0, send = call(
        expert_forward,
        [(slots, bf16), (slots, f32), (slots, bf16), ((MAIN, SENT), bf16)],
        across_experts(send),
        expert_in[0, 0],
        expert_out[0, 0],
    )
    part, picked0 = call(
        combine_first,
        [(row, bf16), ((2, *row), bf16)],
        across_experts(send),
        across[0],
        gates0,
    )

    current1, low_a1, triple1, weights1, mixture1, part = call(
        attention_next,
        [(row, f32), *kept],
        middle0,
        *around(part),
        gains[2],
        proj_qkv[1],
        bias[HERE:],
        proj_out[1],
    )
    middle1, low_b1, gates1, send = call(
        route_next,
        [(row, f32), (row, bf16), ((ROWS, ROWS), f32), ((MAIN, 2 * SENT), bf16)],
        current1,
        *around(part),
        gains[3],
        router[1],
        across[1],
        down[1],
        cotangent,
    )
    rows1, active1, grads1, down1, send = call(
        expert_both,
        [(slots, bf16), (slots, bf16), (slots, bf16), (slots, bf16), ((MAIN, 2 * SENT), bf16)],
        across_experts(send),
        expert_in[1, 0],
        expert_out[1, 0],
    )
    moved, back = call(
        combine_next,
        [(row, bf16), ((ROWS, SUMMED), bf16)],
        across_experts(send),
        across[1],
        gates1,
        cotangent,
    )

    back_kept = [
        (row, f32),
        (row, bf16),
        ((ROWS, 3 * QUARTER), bf16),
        (row, bf16),
        ((ROWS, 128), bf16),
        ((1, WIDTH), f32),
        ((8, EXPERTS), f32),
    ]
    after1, low_after1, back_triple1, part, logits1, gain11, table1 = call(
        attention_back,
        back_kept,
        *around(back),
        gates1,
        across[1],
        router[1],
        middle1,
        gains[3],
        cotangent,
        proj_out[1],
        triple1,
        weights1,
        proj_qkv[1],
        ids,
    )
    parts = around(part)
    (top_grads,) = call(
        weight_grads,
        [((WIDTH, SUMMED), f32)],
        low_a1,
        back_triple1,
        mixture1,
        low_after1,
        low_b1,
        logits1,
    )
    top_grads = lax.psum(top_grads, "expert")
    (output,) = call(finish_output, [(row, bf16)], middle1, *around(moved))

    gradient0, gain10, lanes0, send = call(
        start_back,
        [(row, f32), ((1, WIDTH), f32), ((ROWS, 128), bf16), ((MAIN, SENT), bf16)],
        after1,
        *parts,
        current1,
        gains[2],
        gates0,
        down[0],
        picked0,
    )
    grads0, down0, send = call(
        expert_backward,
        [(slots, bf16), (slots, bf16), ((MAIN, SENT), bf16)],
        across_experts(send),
        before0,
        expert_in[0, 0],
        expert_out[0, 0],
    )
    (back,) = call(
        combine_back, [((ROWS, SUMMED), bf16)], across_experts(send), across[0], lanes0
    )
    after0, low_after0, back_triple0, part, logits0, gain01, table0 = call(
        attention_back,
        back_kept,
        *around(back),
        gates0,
        across[0],
        router[0],
        middle0,
        gains[1],
        gradient0,
        proj_out[0],
        triple0,
        weights0,
        proj_qkv[0],
        ids,
    )
    parts = around(part)
    (grads,) = call(
        weight_grads,
        [((WIDTH, SUMMED), bf16)],
        low_a0,
        back_triple0,
        mixture0,
        low_after0,
        low_b0,
        logits0,
    )
    tokens_grad, gain00 = call(
        finish_back,
        [(row, f32), ((1, WIDTH), f32)],
        after0,
        *parts,
        tokens,
        gains[0],
    )
    (spread,) = call(
        add_chunks,
        [((EXPERTS * 32, SUMMED), bf16)],
        across_experts(grads),
        gain00,
        gain01,
        gain10,
        gain11,
        table0,
        table1,
    )
    qkv_grad, out_grad, router_grad, gain_grads, table_grads = call(
        place_grads,
        [
            ((2, 3, WIDTH, QUARTER), f32),
            ((2, QUARTER, WIDTH), f32),
            ((2, WIDTH, EXPERTS), f32),
            ((8, WIDTH), f32),
            ((8, 128), f32),
        ],
        top_grads,
        across_experts(spread),
    )
    table_grad = table_grads.reshape(2, 4, 128)[:, :HERE, :EXPERTS].transpose(0, 2, 1)
    in_grad0 = dot(rows0, down0, 0)
    out_grad0 = dot(active0, grads0, 0)
    in_grad1 = dot(rows1, down1, 0)
    out_grad1 = dot(active1, grads1, 0)
    return (
        output,
        tokens_grad,
        qkv_grad,
        out_grad,
        table_grad,
        gain_grads[:4].reshape(2, 2, WIDTH),
        router_grad,
        jnp.stack([in_grad0, in_grad1])[:, None],
        jnp.stack([out_grad0, out_grad1])[:, None],
    )


def solution(mesh):
    placed = (
        P("expert", None),
        P("expert", None),
        P(None, "expert", None),
        P(),
        P(None, None, None, "tensor"),
        P(None, "tensor", None),
        P(None, None, "tensor"),
        P(),
        P(),
        P(None, "expert", None, "tensor"),
        P(None, "expert", "tensor", None),
        P("expert", None),
    )
    return jax.shard_map(
        shards,
        mesh=mesh,
        in_specs=placed,
        out_specs=(
            P("expert", None),
            P("expert", None),
            P(None, None, None, "tensor"),
            P(None, "tensor", None),
            P(None, None, "tensor"),
            P(),
            P(),
            P(None, "expert", None, "tensor"),
            P(None, "expert", "tensor", None),
        ),
        check_vma=False,
    )
```

```python
import jax
import jax.numpy as jnp
from jax import lax
from jax.experimental import pallas as pl
from jax.experimental.pallas import tpu as pltpu
from jax.sharding import PartitionSpec as P

epsilon = 1e-06
masked_score = -1000000000.0
highest = lax.Precision.HIGHEST
f32, bf16 = jnp.float32, jnp.bfloat16

ROWS = 128
WIDTH = 768
QUARTER = 192
HERE = 3
HEAD = 64
EXPERTS = 32
MAIN = EXPERTS * 8
REST = 128
HALF = WIDTH // 2
SENT = WIDTH + HALF
SUMMED = WIDTH + 128
LONG = ROWS + 8


class Layer:
    def __init__(self, array, layer):
        self.array, self.layer = array, layer


class Late:
    def __init__(self, operand):
        self.operand = operand


class Kept:
    def __init__(self, shape, dtype):
        self.shape, self.dtype = shape, dtype


class Arriving:
    def __init__(self, source, held, done):
        self.held, self.copy, self.here = held, pltpu.make_async_copy(source, held, done), False
        self.copy.start()

    @property
    def shape(self):
        return self.held.shape

    def __getitem__(self, index):
        self.wait()
        return self.held[index]

    def wait(self):
        if not self.here:
            self.copy.wait()
            self.here = True


class Leaving:
    def __init__(self, held, target, done):
        self.held, self.copy, self.gone = held, pltpu.make_async_copy(held, target, done), False

    @property
    def dtype(self):
        return self.held.dtype

    def __getitem__(self, index):
        return self.held[index]

    def __setitem__(self, index, value):
        self.held[index] = value

    def go(self):
        if not self.gone:
            self.copy.start()
            self.gone = True


def go(*refs):
    for ref in refs:
        if isinstance(ref, Leaving):
            ref.go()


def in_hbm(array):
    return pltpu.with_memory_space_constraint(array, pltpu.HBM)


def call(body, outs, *operands, limit=16):
    late = [isinstance(o, Late) for o in operands]
    inner = [o.operand if isinstance(o, Late) else o for o in operands]
    arrays = [o.array if isinstance(o, Layer) else o for o in inner]
    parts = [a.shape[1:] if isinstance(o, Layer) else a.shape for o, a in zip(inner, arrays)]
    arrays = [in_hbm(a) if is_late else a for a, is_late in zip(arrays, late)]
    kept = [isinstance(o, Kept) for o in outs]
    shapes = [(o.shape, o.dtype) if isinstance(o, Kept) else o for o in outs]
    scratch = [pltpu.VMEM(p, a.dtype) for p, a, is_late in zip(parts, arrays, late) if is_late]
    scratch += [pltpu.VMEM(*o) for o, is_kept in zip(shapes, kept) if is_kept]
    copies = len(scratch)
    if copies:
        scratch.append(pltpu.SemaphoreType.DMA((copies,)))

    def kernel(*refs):
        count = len(operands) + len(outs)
        spare = list(refs[count:])
        done = spare.pop() if copies else None
        given, used = [], 0
        for ref, operand, is_late in zip(refs, inner, late):
            view = ref.at[operand.layer] if isinstance(operand, Layer) else ref
            if is_late:
                view = Arriving(view, spare[used], done.at[used])
                used += 1
            given.append(view)
        taken, leaving = [], []
        for ref, is_kept in zip(refs[len(operands) : count], kept):
            if is_kept:
                ref = Leaving(spare[used], ref, done.at[used])
                leaving.append(ref)
                used += 1
            taken.append(ref)
        body(*given, *taken)
        go(*leaving)
        for ref in leaving:
            ref.copy.wait()
        for view in given:
            if isinstance(view, Arriving):
                view.wait()

    return pl.pallas_call(
        kernel,
        out_shape=[
            pltpu.HBM(*o) if is_kept else jax.ShapeDtypeStruct(*o) for o, is_kept in zip(shapes, kept)
        ],
        in_specs=[pl.BlockSpec(memory_space=pltpu.HBM if n else pltpu.VMEM) for n in late],
        out_specs=[pl.BlockSpec(memory_space=pltpu.HBM if n else pltpu.VMEM) for n in kept],
        scratch_shapes=scratch,
        compiler_params=pltpu.CompilerParams(vmem_limit_bytes=limit * 1024 * 1024),
        name=body.__name__,
    )(*arrays)


def call_stacked(body, layer, operands, stacked, earlier=()):
    whole = [pl.BlockSpec(o.shape, lambda _, n=o.ndim: (0,) * n) for o in operands]
    part = pl.BlockSpec((1, 1, *stacked[2:]), lambda _: (layer, 0, 0, 0))
    return pl.pallas_call(
        body,
        grid=(1,),
        out_shape=[jax.ShapeDtypeStruct(stacked, f32)] * 2,
        in_specs=whole + [pl.BlockSpec(memory_space=pl.ANY)] * len(earlier),
        out_specs=[part] * 2,
        input_output_aliases={len(operands) + n: n for n in range(len(earlier))},
        compiler_params=pltpu.CompilerParams(vmem_limit_bytes=24 * 1024 * 1024),
        name=body.__name__,
    )(*[in_hbm(o) for o in operands], *earlier)


def dot(left, right, left_axis=1, right_axis=0, precision=None):
    return lax.dot_general(
        left,
        right,
        (((left_axis,), (right_axis,)), ((), ())),
        precision=precision,
        preferred_element_type=f32,
    )


def iota(shape, axis):
    return lax.broadcasted_iota(jnp.int32, shape, axis)


def scale_of(values):
    return lax.rsqrt(jnp.mean(values * values, axis=-1, keepdims=True) + epsilon)


def norm_back(values, gain, upstream):
    inverse = scale_of(values)
    inner = upstream * gain
    mean = jnp.mean(inner * values, axis=-1, keepdims=True)
    back = inverse * inner - values * (inverse * inverse * inverse * mean)
    return back, jnp.sum(upstream * (values * inverse), axis=0, keepdims=True)


def head_mask(head):
    lane = iota((1, QUARTER), 1)
    return ((lane >= head * HEAD) & (lane < (head + 1) * HEAD)).astype(f32).astype(bf16)


def four(own, one, two, three):
    return (own.astype(f32) + two.astype(f32)) + (one.astype(f32) + three.astype(f32))


def column_of(row, size):
    same = iota((size, size), 0) == iota((size, size), 1)
    return jnp.sum(jnp.where(same, jnp.broadcast_to(row, (size, size)), 0.0), axis=1, keepdims=True)


def row_of(column, size):
    same = iota((size, size), 0) == iota((size, size), 1)
    return jnp.sum(jnp.where(same, jnp.broadcast_to(column, (size, size)), 0.0), axis=0, keepdims=True)


def setup(ids_ref, table_ref, segment_ref, routes_ref, bias_ref, across_ref, down_ref, hot_ref):
    offsets = ids_ref.shape[1]
    hot = one_hot(iota((EXPERTS, offsets), 0) == ids_ref[...])
    mirror = one_hot(iota((offsets, 256), 0) + iota((offsets, 256), 1) == offsets - 1)
    hot = dot(hot, mirror)
    hot_ref[...] = hot
    segment = segment_ref[...].astype(f32)
    allowed = (column_of(segment, ROWS) == segment) & (iota((ROWS, ROWS), 1) <= iota((ROWS, ROWS), 0))
    lane = iota((ROWS, ROWS), 1)
    before = one_hot(lane < iota((ROWS, ROWS), 0))
    for layer in range(2):
        by_offset = dot(table_ref[layer], hot, precision=highest)
        for head in range(HERE):
            line = jnp.broadcast_to(by_offset[head : head + 1, :], (ROWS, 256))
            placed = pltpu.roll(line, 129, axis=1, stride=1, stride_axis=0)[:, :ROWS]
            bias_ref[layer, head] = jnp.where(allowed, placed, masked_score)
        routes = routes_ref[layer].astype(f32)
        expert = [column_of(routes[k : k + 1, :], ROWS) for k in range(2)]
        hots = [(lane.astype(f32) == expert[k]).astype(f32) for k in range(2)]
        counts = dot(before, (hots[0] + hots[1]).astype(bf16))
        columns = []
        for k in range(2):
            slot = jnp.sum(counts * hots[k], axis=1, keepdims=True)
            first = slot < 7.5
            base = expert[k] * 8.0
            columns.append(jnp.where(first, base + slot, -1.0))
            columns.append(jnp.where(first, -1.0, base + (slot - 8.0) * 2.0))
            columns.append(jnp.where(first, -1.0, base + (slot - 8.0) * 2.0 + 1.0))
        columns.extend(expert)
        across = jnp.zeros((ROWS, ROWS), f32)
        down = jnp.zeros((8, ROWS), f32)
        for place, column in enumerate(columns):
            across = jnp.where(lane == place, column, across)
            down = jnp.where(iota((8, ROWS), 0) == place, row_of(column, ROWS), down)
        across_ref[layer] = across
        down_ref[layer] = down


def one_hot(flags):
    return flags.astype(f32).astype(bf16)


def dispatch(down, rows):
    place = iota((MAIN, ROWS), 0).astype(f32)
    tables = [one_hot(place == down[n : n + 1, :]) for n in range(6)]
    if len(rows) == 1:
        pairs = [([tables[n] + tables[n + 3] for n in range(3)], rows[0])]
    else:
        pairs = [(tables[:3], rows[0]), (tables[3:], rows[1])]
    main, rest = 0.0, 0.0
    for (whole, low, high), row in pairs:
        main = main + dot(whole, row)
        rest = rest + dot(low, row[:, :HALF]) + dot(high, row[:, HALF:])
    return main.astype(bf16), rest.astype(bf16)


def pick(across, route, main, rest):
    place = iota((ROWS, MAIN), 1).astype(f32)
    whole, low, high = [
        one_hot(place == across[:, 3 * route + n : 3 * route + n + 1]) for n in range(3)
    ]
    whole_part = dot(whole, main)
    return whole_part[:, :HALF] + dot(low, rest), whole_part[:, HALF:] + dot(high, rest)


def rest_tables():
    row = iota((REST, MAIN), 0)
    target = (row & 31) * 8 + (row >> 5) * 2
    lane = iota((REST, MAIN), 1)
    real = row < 96
    return one_hot((lane == target) & real), one_hot((lane == target + 1) & real)


def unpack(packed_ref, offset, into_ref):
    low, high = rest_tables()
    rest = packed_ref[:, offset + WIDTH : offset + SENT]
    into_ref[0:MAIN, :] = packed_ref[:, offset : offset + WIDTH]
    into_ref[MAIN : MAIN + REST, 0:HALF] = dot(low, rest).astype(bf16)
    into_ref[MAIN : MAIN + REST, HALF:WIDTH] = dot(high, rest).astype(bf16)


def pack(rows, offset, into_ref):
    low, high = rest_tables()
    into_ref[:, offset : offset + WIDTH] = rows[:MAIN]
    into_ref[:, offset + WIDTH : offset + SENT] = (
        dot(low, rows[MAIN:, :HALF], 0) + dot(high, rows[MAIN:, HALF:], 0)
    ).astype(bf16)


def attend(current, gain_ref, qkv_ref, bias_ref, low_ref, triple_ref, weights_ref):
    low = (current * scale_of(current) * gain_ref[0:1, :]).astype(bf16)
    low_ref[...] = low
    for k in range(3):
        triple_ref[k] = dot(low, qkv_ref[k], 1, 1).astype(bf16)
    mixture = jnp.zeros((ROWS, QUARTER), f32)
    go(low_ref, triple_ref)
    for head in range(HERE):
        mask = head_mask(head)
        scores = dot(triple_ref[0] * mask, triple_ref[1], 1, 1) * HEAD**-0.5 + bias_ref[head]
        scores = scores - jnp.max(scores, axis=-1, keepdims=True)
        raised = jnp.exp(scores)
        weights = raised / jnp.sum(raised, axis=-1, keepdims=True)
        weights_ref[head] = weights
        mixture = mixture + dot(weights.astype(bf16), triple_ref[2] * mask)
    go(weights_ref)
    return mixture.astype(bf16)


def attention_first(
    tokens_ref, gain_ref, qkv_ref, bias_ref, out_ref, low_ref, triple_ref, weights_ref, mixture_ref, part_ref
):
    mixture = attend(
        tokens_ref[...].astype(f32), gain_ref, qkv_ref, bias_ref, low_ref, triple_ref, weights_ref
    )
    mixture_ref[...] = mixture
    go(mixture_ref)
    part_ref[...] = dot(mixture, out_ref[...]).astype(bf16)


def attention_next(
    middle_ref,
    z0,
    z1,
    z2,
    z3,
    gain_ref,
    qkv_ref,
    bias_ref,
    out_ref,
    current_ref,
    low_ref,
    triple_ref,
    weights_ref,
    mixture_ref,
    part_ref,
):
    current = middle_ref[...] + four(z0[...], z1[...], z2[...], z3[...])
    current_ref[...] = current
    mixture = attend(current, gain_ref, qkv_ref, bias_ref, low_ref, triple_ref, weights_ref)
    mixture_ref[...] = mixture
    go(mixture_ref)
    part_ref[...] = dot(mixture, out_ref[...]).astype(bf16)


def route_rows(middle, gain_ref, router_ref, across, low_ref, gates_ref):
    low = (middle * scale_of(middle) * gain_ref[1:2, :]).astype(bf16)
    low_ref[...] = low
    go(low_ref)
    logits = dot(low, router_ref[...], 1, 1)
    lane = iota((ROWS, EXPERTS), 1).astype(f32)
    chosen = [
        jnp.sum(jnp.where(lane == across[:, 6 + k : 7 + k], logits, 0.0), axis=1, keepdims=True)
        for k in range(2)
    ]
    top = jnp.maximum(chosen[0], chosen[1])
    raised = [jnp.exp(c - top) for c in chosen]
    total = raised[0] + raised[1]
    gates = [r / total for r in raised]
    place = iota((ROWS, ROWS), 1)
    gates_ref[...] = jnp.where(place == 0, gates[0], jnp.where(place == 1, gates[1], 0.0))
    return low, gates


def route_first(
    current_ref,
    p0,
    p1,
    p2,
    p3,
    gain_ref,
    router_ref,
    across_ref,
    down_ref,
    middle_ref,
    low_ref,
    gates_ref,
    send_ref,
):
    middle = current_ref[...].astype(f32) + four(p0[...], p1[...], p2[...], p3[...])
    middle_ref[...] = middle
    go(middle_ref)
    low, gates = route_rows(middle, gain_ref, router_ref, across_ref[...], low_ref, gates_ref)
    main, rest = dispatch(down_ref[...], [low])
    send_ref[:, :WIDTH] = main
    send_ref[:, WIDTH:] = rest


def route_next(
    current_ref,
    p0,
    p1,
    p2,
    p3,
    gain_ref,
    router_ref,
    across_ref,
    down_ref,
    cotangent_ref,
    middle_ref,
    low_ref,
    gates_ref,
    send_ref,
):
    middle = current_ref[...].astype(f32) + four(p0[...], p1[...], p2[...], p3[...])
    middle_ref[...] = middle
    go(middle_ref)
    low, gates = route_rows(middle, gain_ref, router_ref, across_ref[...], low_ref, gates_ref)
    main, rest = dispatch(down_ref[...], [low])
    send_ref[:, :WIDTH] = main
    send_ref[:, WIDTH:SENT] = rest
    gradient = cotangent_ref[...].astype(f32)
    main, rest = dispatch(down_ref[...], [(gate * gradient).astype(bf16) for gate in gates])
    send_ref[:, SENT : SENT + WIDTH] = main
    send_ref[:, SENT + WIDTH :] = rest


CURVE = (2.0 / 3.141592653589793) ** 0.5


def gelu_parts(values):
    squared = values * values
    bent = jnp.tanh(CURVE * values * (1.0 + 0.044715 * squared))
    return bent, squared


def gelu(values):
    bent, _ = gelu_parts(values)
    return 0.5 * values * (1.0 + bent)


def gelu_slope(values):
    bent, squared = gelu_parts(values)
    inner = CURVE * (1.0 + 3.0 * 0.044715 * squared)
    return 0.5 * (1.0 + bent) + 0.5 * values * (1.0 - bent * bent) * inner


def expert_forward(got_ref, in_ref, out_ref, rows_ref, before_ref, active_ref, back_ref):
    unpack(got_ref, 0, rows_ref)
    before = dot(rows_ref[...], in_ref[...])
    before_ref[...] = before
    go(rows_ref, before_ref)
    active = gelu(before).astype(bf16)
    active_ref[...] = active
    go(active_ref)
    pack(dot(active, out_ref[...]).astype(bf16), 0, back_ref)


def expert_backward(got_ref, before_ref, in_ref, out_ref, grads_ref, down_ref, back_ref):
    unpack(got_ref, 0, grads_ref)
    go(grads_ref)
    grad_active = dot(grads_ref[...], out_ref[...], 1, 1)
    grad_before = (grad_active * gelu_slope(before_ref[...])).astype(bf16)
    down_ref[...] = grad_before
    go(down_ref)
    pack(dot(grad_before, in_ref[...], 1, 1).astype(bf16), 0, back_ref)


def expert_both(got_ref, in_ref, out_ref, rows_ref, active_ref, grads_ref, down_ref, back_ref):
    unpack(got_ref, 0, rows_ref)
    unpack(got_ref, SENT, grads_ref)
    go(rows_ref, grads_ref)
    before = dot(rows_ref[...], in_ref[...])
    active = gelu(before).astype(bf16)
    active_ref[...] = active
    go(active_ref)
    pack(dot(active, out_ref[...]).astype(bf16), 0, back_ref)
    grad_active = dot(grads_ref[...], out_ref[...], 1, 1)
    grad_before = (grad_active * gelu_slope(before)).astype(bf16)
    down_ref[...] = grad_before
    go(down_ref)
    pack(dot(grad_before, in_ref[...], 1, 1).astype(bf16), SENT, back_ref)


def expert_grads_top(rows_ref, active_ref, grads_ref, down_ref, in_grad_ref, out_grad_ref):
    in_grad_ref[0, 0] = dot(rows_ref[...], down_ref[...], 0)
    out_grad_ref[0, 0] = dot(active_ref[...], grads_ref[...], 0)


def expert_grads_low(rows_ref, active_ref, grads_ref, down_ref, _, __, in_grad_ref, out_grad_ref):
    expert_grads_top(rows_ref, active_ref, grads_ref, down_ref, in_grad_ref, out_grad_ref)


def combine_first(got_ref, across_ref, gates_ref, part_ref, picked_ref):
    main, rest = got_ref[:, :WIDTH], got_ref[:, WIDTH:]
    across, gates = across_ref[...], gates_ref[...]
    left, right = 0.0, 0.0
    for route in range(2):
        one, two = pick(across, route, main, rest)
        picked_ref[route, :, :HALF] = one.astype(bf16)
        picked_ref[route, :, HALF:] = two.astype(bf16)
        left = left + gates[:, route : route + 1] * one
        right = right + gates[:, route : route + 1] * two
    part_ref[:, :HALF] = left.astype(bf16)
    part_ref[:, HALF:] = right.astype(bf16)


def gate_rows(grads):
    place = iota((8, ROWS), 0)
    rows = [row_of(grad, ROWS) for grad in grads]
    both = jnp.where(place == 0, rows[0], jnp.where(place == 1, rows[1], 0.0))
    moved = jnp.where(place == 2, rows[0], jnp.where(place == 3, rows[1], 0.0))
    left = moved - moved.astype(bf16).astype(f32)
    return (both + left).astype(bf16)


def gathered_back(got_ref, offset, across, rows, into_ref):
    main = got_ref[:, offset : offset + WIDTH]
    rest = got_ref[:, offset + WIDTH : offset + SENT]
    left, right = pick(across, 0, main, rest)
    other_left, other_right = pick(across, 1, main, rest)
    into_ref[:ROWS, :HALF] = (left + other_left).astype(bf16)
    into_ref[:ROWS, HALF:] = (right + other_right).astype(bf16)
    into_ref[ROWS:, :ROWS] = rows
    into_ref[ROWS:, ROWS:] = jnp.zeros((8, WIDTH - ROWS), bf16)


def combine_next(got_ref, across_ref, gates_ref, cotangent_ref, part_ref, back_ref):
    main, rest = got_ref[:, :WIDTH], got_ref[:, WIDTH:SENT]
    across, gates = across_ref[...], gates_ref[...]
    gradient = cotangent_ref[...].astype(f32)
    left, right, grads = 0.0, 0.0, []
    for route in range(2):
        one, two = pick(across, route, main, rest)
        left = left + gates[:, route : route + 1] * one
        right = right + gates[:, route : route + 1] * two
        grads.append(
            jnp.sum(gradient[:, :HALF] * one + gradient[:, HALF:] * two, axis=1, keepdims=True)
        )
    part_ref[:, :HALF] = left.astype(bf16)
    part_ref[:, HALF:] = right.astype(bf16)
    gathered_back(got_ref, SENT, across, gate_rows(grads), back_ref)


def combine_back(got_ref, across_ref, rows_ref, back_ref):
    gathered_back(got_ref, 0, across_ref[...], rows_ref[...], back_ref)


def attention_back(
    e0,
    e1,
    e2,
    e3,
    gates_ref,
    across_ref,
    router_ref,
    middle_ref,
    gain_ref,
    gradient_ref,
    out_ref,
    triple_ref,
    weights_ref,
    qkv_ref,
    hot_ref,
    after_ref,
    low_ref,
    back_triple_ref,
    part_ref,
    logits_ref,
    gain_grad_ref,
    table_grad_ref,
):
    total = four(e0[...], e1[...], e2[...], e3[...])
    gates = gates_ref[...]
    across = across_ref[...]
    gate = [gates[:, k : k + 1] for k in range(2)]
    rows = total[ROWS:, :ROWS]
    grad_gate = [column_of(rows[k : k + 1] + rows[k + 2 : k + 3], ROWS) for k in range(2)]
    mean = gate[0] * grad_gate[0] + gate[1] * grad_gate[1]
    lane = iota((ROWS, EXPERTS), 1).astype(f32)
    grad_logits = 0.0
    for k in range(2):
        grad_logits = grad_logits + jnp.where(
            lane == across[:, 6 + k : 7 + k], gate[k] * (grad_gate[k] - mean), 0.0
        )
    high = grad_logits.astype(bf16)
    low = (grad_logits - high.astype(f32)).astype(bf16)
    logits_ref[:, :EXPERTS] = high
    logits_ref[:, EXPERTS : 2 * EXPERTS] = low
    logits_ref[:, 2 * EXPERTS :] = jnp.zeros((ROWS, 128 - 2 * EXPERTS), bf16)
    grad_low = total[:ROWS] + dot(high, router_ref[...]) + dot(low, router_ref[...])
    grad_middle, gain_grad_ref[...] = norm_back(middle_ref[...], gain_ref[1:2, :], grad_low)
    after = gradient_ref[...].astype(f32) + grad_middle
    after_ref[...] = after
    low_after = after.astype(bf16)
    low_ref[...] = low_after
    go(after_ref, low_ref, logits_ref, gain_grad_ref)
    grad_mixture = dot(low_after, out_ref[...], 1, 1).astype(bf16)
    queries, keys, values = triple_ref[0], triple_ref[1], triple_ref[2]
    grad_queries = jnp.zeros((ROWS, QUARTER), f32)
    grad_keys, grad_values = grad_queries, grad_queries
    diagonals = jnp.zeros((8, 256), f32)
    flip = one_hot(iota((ROWS, ROWS), 0) + iota((ROWS, ROWS), 1) == ROWS - 1)
    for head in range(HERE):
        mask = head_mask(head)
        masked_grad = grad_mixture * mask
        weights = weights_ref[head]
        grad_values = grad_values + dot(weights.astype(bf16), masked_grad, 0)
        grad_weights = dot(masked_grad, values, 1, 1)
        grad_scores = weights * (
            grad_weights - jnp.sum(weights * grad_weights, axis=-1, keepdims=True)
        )
        grad_scores = grad_scores.astype(bf16)
        grad_queries = grad_queries + dot(grad_scores, keys * mask)
        grad_keys = grad_keys + dot(grad_scores, queries * mask, 0)
        wide = jnp.concatenate([dot(flip, grad_scores), jnp.zeros((ROWS, 128), f32)], axis=1)
        turned = pltpu.roll(wide, 0, axis=1, stride=1, stride_axis=0)
        diagonals = jnp.where(
            iota((8, 256), 0) == head, jnp.sum(turned, axis=0, keepdims=True), diagonals
        )
    table_grad_ref[...] = dot(hot_ref[...], diagonals, 1, 1, precision=highest)
    grad_input = 0.0
    for k, grad in enumerate((grad_queries * HEAD**-0.5, grad_keys * HEAD**-0.5, grad_values)):
        grad = grad.astype(bf16)
        back_triple_ref[:, k * QUARTER : (k + 1) * QUARTER] = grad
        grad_input = grad_input + dot(grad, qkv_ref[k])
    go(back_triple_ref)
    part_ref[...] = grad_input.astype(bf16)


def weight_grads(low_ref, back_triple_ref, mixture_ref, after_ref, low_two_ref, logits_ref, grads_ref):
    kind = grads_ref.dtype
    qkv_rows = 3 * QUARTER
    grads_ref[:qkv_rows, :WIDTH] = dot(back_triple_ref[...], low_ref[...], 0).astype(kind)
    grads_ref[qkv_rows:, :WIDTH] = dot(mixture_ref[...], after_ref[...], 0).astype(kind)
    both = dot(logits_ref[...], low_two_ref[...], 0)
    total = both[:EXPERTS] + both[EXPERTS : 2 * EXPERTS]
    for part in range(WIDTH // 128):
        grads_ref[part * EXPERTS : (part + 1) * EXPERTS, WIDTH:] = total[
            :, part * 128 : (part + 1) * 128
        ].astype(kind)
    used = WIDTH // 128 * EXPERTS
    grads_ref[used:, WIDTH:] = jnp.zeros((WIDTH - used, 128), kind)


def start_back(
    after_ref,
    d0,
    d1,
    d2,
    d3,
    input_ref,
    gain_ref,
    gates_ref,
    down_ref,
    picked_ref,
    gradient_ref,
    gain_grad_ref,
    rows_ref,
    send_ref,
):
    grad_low = four(d0[...], d1[...], d2[...], d3[...])
    grad_input, gain_grad_ref[...] = norm_back(input_ref[...].astype(f32), gain_ref[0:1, :], grad_low)
    gradient = after_ref[...] + grad_input
    gradient_ref[...] = gradient
    go(gradient_ref, gain_grad_ref)
    gates = gates_ref[...]
    weighted = [(gates[:, k : k + 1] * gradient).astype(bf16) for k in range(2)]
    main, rest = dispatch(down_ref[...], weighted)
    send_ref[:, :WIDTH] = main
    send_ref[:, WIDTH:] = rest
    rows_ref[...] = gate_rows(
        [jnp.sum(gradient * picked_ref[k].astype(f32), axis=1, keepdims=True) for k in range(2)]
    )


def finish_back(after_ref, d0, d1, d2, d3, input_ref, gain_ref, gradient_ref, gain_grad_ref):
    grad_low = four(d0[...], d1[...], d2[...], d3[...])
    grad_input, gain_grad_ref[...] = norm_back(input_ref[...].astype(f32), gain_ref[0:1, :], grad_low)
    gradient_ref[...] = after_ref[...] + grad_input


def finish_output(middle_ref, z0, z1, z2, z3, output_ref):
    output_ref[...] = (middle_ref[...] + four(z0[...], z1[...], z2[...], z3[...])).astype(bf16)


SHARE = WIDTH // EXPERTS


def total_of(chunks_ref):
    total = chunks_ref[0:SHARE, :].astype(f32)
    for block in range(1, EXPERTS):
        total = total + chunks_ref[block * SHARE : (block + 1) * SHARE, :].astype(f32)
    return total.astype(bf16)


def add_chunks_top(chunks_ref, spread_ref):
    total = total_of(chunks_ref)
    for block in range(EXPERTS):
        spread_ref[block * SHARE : (block + 1) * SHARE, :] = total


def add_chunks(chunks_ref, g00, g01, g10, g11, t0, t1, spread_ref):
    total = total_of(chunks_ref)
    row = iota((8, WIDTH), 0)
    gains = jnp.zeros((8, WIDTH), f32)
    for place, gain in enumerate((g00, g01, g10, g11)):
        gains = jnp.where(row == place, gain[...], gains)
    spread = 0.0
    for layer, table in enumerate((t0, t1)):
        lifted = table[...].astype(bf16)
        rows = iota((8, EXPERTS), 0)
        for turn in range(4):
            chosen = one_hot(iota((8, EXPERTS), 1) == rows * 4 + turn)
            start = turn * 32 + layer * 8
            onto = one_hot(iota((8, 128), 1) == iota((8, 128), 0) + start)
            spread = spread + dot(dot(chosen, lifted).astype(bf16), onto)
    small = jnp.concatenate([gains, spread], axis=1).astype(bf16)
    for block in range(EXPERTS):
        spread_ref[block * 32 : block * 32 + SHARE, :] = total
        spread_ref[block * 32 + SHARE : block * 32 + 32, :] = small


def place_top(top_ref, qkv_ref, out_ref, router_ref):
    for k in range(3):
        qkv_ref[1, k] = top_ref[k * QUARTER : (k + 1) * QUARTER, :WIDTH].astype(f32)
    out_ref[1] = top_ref[3 * QUARTER :, :WIDTH].astype(f32)
    for part in range(WIDTH // 128):
        router_ref[1, :, part * 128 : (part + 1) * 128] = top_ref[
            part * EXPERTS : (part + 1) * EXPERTS, WIDTH:
        ].astype(f32)


def place_grads(top_ref, all_ref, qkv_ref, out_ref, router_ref, gains_ref, tables_ref):
    small = jnp.zeros((8, SUMMED), f32)
    place_top(top_ref, qkv_ref, out_ref, router_ref)
    for block in range(EXPERTS):
        chunk = all_ref[block * 32 : block * 32 + SHARE, :].astype(f32)
        small = small + all_ref[block * 32 + SHARE : block * 32 + 32, :].astype(f32)
        which, first = divmod(block * SHARE, QUARTER)
        if which < 3:
            qkv_ref[0, which, first : first + SHARE, :] = chunk[:, :WIDTH]
        else:
            out_ref[0, first : first + SHARE, :] = chunk[:, :WIDTH]
        for row in range(0, SHARE, 8):
            part, inside = divmod(block * SHARE + row, EXPERTS)
            if part < WIDTH // 128:
                router_ref[0, inside : inside + 8, part * 128 : (part + 1) * 128] = chunk[
                    row : row + 8, WIDTH:
                ]
    for layer in range(2):
        gains_ref[layer] = small[2 * layer : 2 * layer + 2, :WIDTH]
        lanes = small[:, WIDTH:]
        table = 0.0
        for turn in range(4):
            rows = one_hot(iota((EXPERTS, 8), 0) == iota((EXPERTS, 8), 1) * 4 + turn)
            spread = dot(rows.astype(f32), lanes, precision=highest)
            from_lane = (iota((128, 8), 0) == iota((128, 8), 1) + turn * 32 + layer * 8).astype(f32)
            table = table + dot(spread, from_lane, precision=highest)
        tables_ref[layer] = table[:, :HERE]


def around(values):
    sent = [
        lax.ppermute(values, "tensor", [(i, (i + shift) % 4) for i in range(4)]) for shift in (1, 2, 3)
    ]
    return [values, *sent]


def across_experts(values):
    return lax.all_to_all(values, "expert", 0, 0, tiled=True)


def shards(
    tokens,
    segment_ids,
    expert_routes,
    bucket_ids,
    proj_qkv,
    proj_out,
    bias_table,
    norm_gains,
    router,
    expert_in,
    expert_out,
    cotangent,
):
    qkv = proj_qkv.transpose(0, 1, 3, 2)
    router = router.transpose(0, 2, 1)
    expert_in, expert_out = expert_in[:, 0], expert_out[:, 0]
    gains = norm_gains
    row = (ROWS, WIDTH)
    narrow = (ROWS, QUARTER)
    scores = (HERE, ROWS, ROWS)
    slots = (MAIN + REST, WIDTH)
    stacked = (2, 1, WIDTH, WIDTH)
    bias, across, down, hot = call(
        setup,
        [
            ((2, HERE, ROWS, ROWS), f32),
            ((2, ROWS, ROWS), f32),
            ((2, 8, ROWS), f32),
            ((EXPERTS, 256), f32),
        ],
        Late(bucket_ids.reshape(1, -1)),
        Late(bias_table.transpose(0, 2, 1)),
        Late(segment_ids),
        Late(expert_routes.transpose(0, 2, 1)),
    )
    kept = [
        Kept(row, bf16),
        Kept((3, *narrow), bf16),
        Kept(scores, f32),
        Kept(narrow, bf16),
        (row, bf16),
    ]

    low_a0, triple0, weights0, mixture0, part = call(
        attention_first,
        kept,
        Late(tokens),
        Late(Layer(gains, 0)),
        Late(Layer(qkv, 0)),
        Layer(bias, 0),
        Late(Layer(proj_out, 0)),
    )
    middle0, low_b0, gates0, send = call(
        route_first,
        [Kept(row, f32), Kept(row, bf16), ((ROWS, ROWS), f32), ((MAIN, SENT), bf16)],
        tokens,
        *around(part),
        Layer(gains, 0),
        Layer(router, 0),
        Layer(across, 0),
        Layer(down, 0),
    )
    rows0, before0, active0, send = call(
        expert_forward,
        [Kept(slots, bf16), Kept(slots, f32), Kept(slots, bf16), ((MAIN, SENT), bf16)],
        across_experts(send),
        Layer(expert_in, 0),
        Layer(expert_out, 0),
    )
    part, picked0 = call(
        combine_first,
        [(row, bf16), Kept((2, *row), bf16)],
        across_experts(send),
        Layer(across, 0),
        gates0,
    )

    current1, low_a1, triple1, weights1, mixture1, part = call(
        attention_next,
        [(row, f32), *kept],
        middle0,
        *around(part),
        Layer(gains, 1),
        Layer(qkv, 1),
        Layer(bias, 1),
        Layer(proj_out, 1),
    )
    middle1, low_b1, gates1, send = call(
        route_next,
        [Kept(row, f32), Kept(row, bf16), ((ROWS, ROWS), f32), ((MAIN, 2 * SENT), bf16)],
        current1,
        *around(part),
        Layer(gains, 1),
        Layer(router, 1),
        Layer(across, 1),
        Layer(down, 1),
        cotangent,
    )
    rows1, active1, grads1, down1, send = call(
        expert_both,
        [*[Kept(slots, bf16)] * 4, ((MAIN, 2 * SENT), bf16)],
        across_experts(send),
        Layer(expert_in, 1),
        Layer(expert_out, 1),
    )
    got = across_experts(send)
    in_grads, out_grads = call_stacked(
        expert_grads_top, 1, (rows1, active1, grads1, down1), stacked
    )
    moved, back = call(
        combine_next,
        [(row, bf16), ((LONG, WIDTH), bf16)],
        got,
        Layer(across, 1),
        gates1,
        cotangent,
    )

    back_kept = [
        Kept(row, f32),
        Kept(row, bf16),
        Kept((ROWS, 3 * QUARTER), bf16),
        (row, bf16),
        Kept((ROWS, 128), bf16),
        Kept((1, WIDTH), f32),
        Kept((EXPERTS, 8), f32),
    ]
    after1, low_after1, back_triple1, part, logits1, gain11, table1 = call(
        attention_back,
        back_kept,
        *around(back),
        gates1,
        Layer(across, 1),
        Layer(router, 1),
        middle1,
        Layer(gains, 1),
        cotangent,
        Layer(proj_out, 1),
        triple1,
        weights1,
        Layer(qkv, 1),
        hot,
    )
    parts = around(part)
    (top_grads,) = call(
        weight_grads,
        [Kept((WIDTH, SUMMED), bf16)],
        low_a1,
        back_triple1,
        mixture1,
        low_after1,
        low_b1,
        logits1,
    )
    top_grads = across_experts(top_grads)
    top_grads, parts, in_grads = lax.optimization_barrier((top_grads, parts, in_grads))
    (top_grads,) = call(add_chunks_top, [Kept((WIDTH, SUMMED), bf16)], top_grads)

    gradient0, gain10, rows0b, send = call(
        start_back,
        [Kept(row, f32), Kept((1, WIDTH), f32), ((8, ROWS), bf16), ((MAIN, SENT), bf16)],
        Late(after1),
        *parts,
        Late(current1),
        Late(Layer(gains, 1)),
        gates0,
        Layer(down, 0),
        Late(picked0),
    )
    grads0, down0, send = call(
        expert_backward,
        [Kept(slots, bf16), Kept(slots, bf16), ((MAIN, SENT), bf16)],
        across_experts(send),
        Late(before0),
        Late(Layer(expert_in, 0)),
        Late(Layer(expert_out, 0)),
    )
    got = across_experts(send)
    in_grads, out_grads = call_stacked(
        expert_grads_low, 0, (rows0, active0, grads0, down0), stacked, (in_grads, out_grads)
    )
    (back,) = call(combine_back, [((LONG, WIDTH), bf16)], got, Layer(across, 0), rows0b)
    backs = around(back)
    top_grads, back = lax.optimization_barrier((top_grads, back))
    top_grads = across_experts(top_grads)
    top_grads, backs, in_grads = lax.optimization_barrier((top_grads, backs, in_grads))
    (output,) = call(finish_output, [Kept(row, bf16)], middle1, *around(moved))
    after0, low_after0, back_triple0, part, logits0, gain01, table0 = call(
        attention_back,
        back_kept,
        *backs,
        gates0,
        Layer(across, 0),
        Layer(router, 0),
        middle0,
        Layer(gains, 0),
        gradient0,
        Layer(proj_out, 0),
        triple0,
        weights0,
        Layer(qkv, 0),
        hot,
    )
    (grads,) = call(
        weight_grads,
        [Kept((WIDTH, SUMMED), bf16)],
        low_a0,
        back_triple0,
        mixture0,
        low_after0,
        low_b0,
        logits0,
    )
    parts = around(part)
    tokens_grad, gain00 = call(
        finish_back,
        [Kept(row, f32), Kept((1, WIDTH), f32)],
        after0,
        *parts,
        tokens,
        Layer(gains, 0),
    )
    (spread,) = call(
        add_chunks,
        [Kept((EXPERTS * 32, SUMMED), bf16)],
        across_experts(grads),
        Late(gain00),
        Late(gain01),
        Late(gain10),
        Late(gain11),
        Late(table0),
        Late(table1),
    )
    qkv_grad, out_grad, router_grad, gain_grads, table_grad = call(
        place_grads,
        [
            Kept((2, 3, QUARTER, WIDTH), f32),
            Kept((2, QUARTER, WIDTH), f32),
            Kept((2, EXPERTS, WIDTH), f32),
            Kept((2, 2, WIDTH), f32),
            Kept((2, EXPERTS, HERE), f32),
        ],
        Late(top_grads),
        across_experts(spread),
        limit=24,
    )
    return (
        output,
        tokens_grad,
        qkv_grad.transpose(0, 1, 3, 2),
        out_grad,
        table_grad,
        gain_grads,
        router_grad.transpose(0, 2, 1),
        in_grads,
        out_grads,
    )


def solution(mesh):
    placed = (
        P("expert", None),
        P("expert", None),
        P(None, "expert", None),
        P(),
        P(None, None, None, "tensor"),
        P(None, "tensor", None),
        P(None, None, "tensor"),
        P(),
        P(),
        P(None, "expert", None, "tensor"),
        P(None, "expert", "tensor", None),
        P("expert", None),
    )
    return jax.shard_map(
        shards,
        mesh=mesh,
        in_specs=placed,
        out_specs=(
            P("expert", None),
            P("expert", None),
            P(None, None, None, "tensor"),
            P(None, "tensor", None),
            P(None, None, "tensor"),
            P(),
            P(),
            P(None, "expert", None, "tensor"),
            P(None, "expert", "tensor", None),
        ),
        check_vma=False,
    )
```

```python
import jax
import jax.numpy as jnp
from jax import lax
from jax.experimental import pallas as pl
from jax.experimental.pallas import tpu as pltpu
from jax.sharding import PartitionSpec as P

epsilon = 1e-06
masked_score = -1000000000.0
highest = lax.Precision.HIGHEST
f32, bf16 = jnp.float32, jnp.bfloat16

ROWS = 128
WIDTH = 768
QUARTER = 192
HERE = 3
HEAD = 64
EXPERTS = 32
MAIN = EXPERTS * 8
REST = 128
HALF = WIDTH // 2
SENT = WIDTH + HALF
SUMMED = WIDTH + 128
LONG = ROWS + 8


class Layer:
    def __init__(self, array, layer):
        self.array, self.layer = array, layer


class Late:
    def __init__(self, operand):
        self.operand = operand


class Kept:
    def __init__(self, shape, dtype):
        self.shape, self.dtype = shape, dtype


class Arriving:
    def __init__(self, source, held, done):
        self.held, self.copy, self.here = held, pltpu.make_async_copy(source, held, done), False
        self.copy.start()

    @property
    def shape(self):
        return self.held.shape

    def __getitem__(self, index):
        self.wait()
        return self.held[index]

    def wait(self):
        if not self.here:
            self.copy.wait()
            self.here = True


class Leaving:
    def __init__(self, held, target, done):
        self.held, self.copy, self.gone = held, pltpu.make_async_copy(held, target, done), False

    @property
    def dtype(self):
        return self.held.dtype

    def __getitem__(self, index):
        return self.held[index]

    def __setitem__(self, index, value):
        self.held[index] = value

    def go(self):
        if not self.gone:
            self.copy.start()
            self.gone = True


def go(*refs):
    for ref in refs:
        if isinstance(ref, Leaving):
            ref.go()


def in_hbm(array):
    return pltpu.with_memory_space_constraint(array, pltpu.HBM)


def call(body, outs, *operands, held=(), limit=16):
    late = [isinstance(o, Late) for o in operands]
    inner = [o.operand if isinstance(o, Late) else o for o in operands]
    arrays = [o.array if isinstance(o, Layer) else o for o in inner]
    parts = [a.shape[1:] if isinstance(o, Layer) else a.shape for o, a in zip(inner, arrays)]
    arrays = [in_hbm(a) if is_late else a for a, is_late in zip(arrays, late)]
    kept = [isinstance(o, Kept) for o in outs]
    shapes = [(o.shape, o.dtype) if isinstance(o, Kept) else o for o in outs]
    scratch = [pltpu.VMEM(p, a.dtype) for p, a, is_late in zip(parts, arrays, late) if is_late]
    scratch += [pltpu.VMEM(*o) for o, is_kept in zip(shapes, kept) if is_kept]
    copies = len(scratch)
    scratch += [pltpu.VMEM(*h) for h in held]
    if copies:
        scratch.append(pltpu.SemaphoreType.DMA((copies,)))

    def kernel(*refs):
        count = len(operands) + len(outs)
        spare = list(refs[count:])
        done = spare.pop() if copies else None
        given, used = [], 0
        for ref, operand, is_late in zip(refs, inner, late):
            view = ref.at[operand.layer] if isinstance(operand, Layer) else ref
            if is_late:
                view = Arriving(view, spare[used], done.at[used])
                used += 1
            given.append(view)
        taken, leaving = [], []
        for ref, is_kept in zip(refs[len(operands) : count], kept):
            if is_kept:
                ref = Leaving(spare[used], ref, done.at[used])
                leaving.append(ref)
                used += 1
            taken.append(ref)
        body(*given, *taken, *spare[used:])
        go(*leaving)
        for ref in leaving:
            ref.copy.wait()
        for view in given:
            if isinstance(view, Arriving):
                view.wait()

    return pl.pallas_call(
        kernel,
        out_shape=[
            pltpu.HBM(*o) if is_kept else jax.ShapeDtypeStruct(*o) for o, is_kept in zip(shapes, kept)
        ],
        in_specs=[pl.BlockSpec(memory_space=pltpu.HBM if n else pltpu.VMEM) for n in late],
        out_specs=[pl.BlockSpec(memory_space=pltpu.HBM if n else pltpu.VMEM) for n in kept],
        scratch_shapes=scratch,
        compiler_params=pltpu.CompilerParams(vmem_limit_bytes=limit * 1024 * 1024),
        name=body.__name__,
    )(*arrays)


def call_stacked(body, layer, operands, stacked, earlier=()):
    whole = [pl.BlockSpec(o.shape, lambda _, n=o.ndim: (0,) * n) for o in operands]
    part = pl.BlockSpec((1, 1, *stacked[2:]), lambda _: (layer, 0, 0, 0))
    return pl.pallas_call(
        body,
        grid=(1,),
        out_shape=[pltpu.HBM(stacked, f32)] * 2,
        in_specs=whole + [pl.BlockSpec(memory_space=pltpu.HBM)] * len(earlier),
        out_specs=[part] * 2,
        input_output_aliases={len(operands) + n: n for n in range(len(earlier))},
        compiler_params=pltpu.CompilerParams(vmem_limit_bytes=24 * 1024 * 1024),
        name=body.__name__,
    )(*[in_hbm(o) for o in (*operands, *earlier)])


def dot(left, right, left_axis=1, right_axis=0, precision=None):
    return lax.dot_general(
        left,
        right,
        (((left_axis,), (right_axis,)), ((), ())),
        precision=precision,
        preferred_element_type=f32,
    )


def iota(shape, axis):
    return lax.broadcasted_iota(jnp.int32, shape, axis)


def scale_of(values):
    return lax.rsqrt(jnp.mean(values * values, axis=-1, keepdims=True) + epsilon)


def norm_back(values, gain, upstream):
    inverse = scale_of(values)
    inner = upstream * gain
    mean = jnp.mean(inner * values, axis=-1, keepdims=True)
    back = inverse * inner - values * (inverse * inverse * inverse * mean)
    return back, jnp.sum(upstream * (values * inverse), axis=0, keepdims=True)


def head_mask(head):
    lane = iota((1, QUARTER), 1)
    return ((lane >= head * HEAD) & (lane < (head + 1) * HEAD)).astype(f32).astype(bf16)


def four(own, one, two, three):
    return (own.astype(f32) + two.astype(f32)) + (one.astype(f32) + three.astype(f32))


def column_of(row, size):
    same = iota((size, size), 0) == iota((size, size), 1)
    return jnp.sum(jnp.where(same, jnp.broadcast_to(row, (size, size)), 0.0), axis=1, keepdims=True)


def row_of(column, size):
    same = iota((size, size), 0) == iota((size, size), 1)
    return jnp.sum(jnp.where(same, jnp.broadcast_to(column, (size, size)), 0.0), axis=0, keepdims=True)


def setup(ids_ref, table_ref, segment_ref, routes_ref, bias_ref, across_ref, down_ref, hot_ref):
    offsets = ids_ref.shape[1]
    hot = one_hot(iota((EXPERTS, offsets), 0) == ids_ref[...])
    mirror = one_hot(iota((offsets, 256), 0) + iota((offsets, 256), 1) == offsets - 1)
    hot = dot(hot, mirror)
    hot_ref[...] = hot
    tables = table_ref[...]
    segment = segment_ref[...].astype(f32)
    allowed = (column_of(segment, ROWS) == segment) & (iota((ROWS, ROWS), 1) <= iota((ROWS, ROWS), 0))
    lane = iota((ROWS, ROWS), 1)
    before = one_hot(lane < iota((ROWS, ROWS), 0))
    for layer in range(2):
        by_offset = dot(tables[:, layer, :], hot, precision=highest)
        for head in range(HERE):
            line = jnp.broadcast_to(by_offset[head : head + 1, :], (ROWS, 256))
            placed = pltpu.roll(line, 129, axis=1, stride=1, stride_axis=0)[:, :ROWS]
            bias_ref[layer, head] = jnp.where(allowed, placed, masked_score)
        routes = routes_ref[layer].astype(f32)
        expert = [column_of(routes[k : k + 1, :], ROWS) for k in range(2)]
        hots = [(lane.astype(f32) == expert[k]).astype(f32) for k in range(2)]
        counts = dot(before, (hots[0] + hots[1]).astype(bf16))
        columns = []
        for k in range(2):
            slot = jnp.sum(counts * hots[k], axis=1, keepdims=True)
            first = slot < 7.5
            base = expert[k] * 8.0
            columns.append(jnp.where(first, base + slot, -1.0))
            columns.append(jnp.where(first, -1.0, base + (slot - 8.0) * 2.0))
            columns.append(jnp.where(first, -1.0, base + (slot - 8.0) * 2.0 + 1.0))
        columns.extend(expert)
        across = jnp.zeros((ROWS, ROWS), f32)
        down = jnp.zeros((8, ROWS), f32)
        for place, column in enumerate(columns):
            across = jnp.where(lane == place, column, across)
            down = jnp.where(iota((8, ROWS), 0) == place, row_of(column, ROWS), down)
        across_ref[layer] = across
        down_ref[layer] = down


def one_hot(flags):
    return flags.astype(f32).astype(bf16)


def dispatch(down, rows):
    place = iota((MAIN, ROWS), 0).astype(f32)
    tables = [one_hot(place == down[n : n + 1, :]) for n in range(6)]
    if len(rows) == 1:
        pairs = [([tables[n] + tables[n + 3] for n in range(3)], rows[0])]
    else:
        pairs = [(tables[:3], rows[0]), (tables[3:], rows[1])]
    main, rest = 0.0, 0.0
    for (whole, low, high), row in pairs:
        main = main + dot(whole, row)
        rest = rest + dot(low, row[:, :HALF]) + dot(high, row[:, HALF:])
    return main.astype(bf16), rest.astype(bf16)


def pick(across, route, main, rest):
    place = iota((ROWS, MAIN), 1).astype(f32)
    whole, low, high = [
        one_hot(place == across[:, 3 * route + n : 3 * route + n + 1]) for n in range(3)
    ]
    whole_part = dot(whole, main)
    return whole_part[:, :HALF] + dot(low, rest), whole_part[:, HALF:] + dot(high, rest)


def rest_tables():
    row = iota((REST, MAIN), 0)
    target = (row & 31) * 8 + (row >> 5) * 2
    lane = iota((REST, MAIN), 1)
    real = row < 96
    return one_hot((lane == target) & real), one_hot((lane == target + 1) & real)


def unpack(packed_ref, offset, into_ref):
    low, high = rest_tables()
    rest = packed_ref[:, offset + WIDTH : offset + SENT]
    into_ref[0:MAIN, :] = packed_ref[:, offset : offset + WIDTH]
    into_ref[MAIN : MAIN + REST, 0:HALF] = dot(low, rest).astype(bf16)
    into_ref[MAIN : MAIN + REST, HALF:WIDTH] = dot(high, rest).astype(bf16)


def pack(rows, offset, into_ref):
    low, high = rest_tables()
    into_ref[:, offset : offset + WIDTH] = rows[:MAIN]
    into_ref[:, offset + WIDTH : offset + SENT] = (
        dot(low, rows[MAIN:, :HALF], 0) + dot(high, rows[MAIN:, HALF:], 0)
    ).astype(bf16)


def attend(current, gain_ref, qkv_ref, bias_ref, low_ref, triple_ref, weights_ref):
    low = (current * scale_of(current) * gain_ref[0:1, :]).astype(bf16)
    low_ref[...] = low
    for k in range(3):
        triple_ref[k] = dot(low, qkv_ref[k], 1, 1).astype(bf16)
    mixture = jnp.zeros((ROWS, QUARTER), f32)
    go(low_ref, triple_ref)
    for head in range(HERE):
        mask = head_mask(head)
        scores = dot(triple_ref[0] * mask, triple_ref[1], 1, 1) * HEAD**-0.5 + bias_ref[head]
        scores = scores - jnp.max(scores, axis=-1, keepdims=True)
        raised = jnp.exp(scores)
        weights = raised / jnp.sum(raised, axis=-1, keepdims=True)
        weights_ref[head] = weights
        mixture = mixture + dot(weights.astype(bf16), triple_ref[2] * mask)
    go(weights_ref)
    return mixture.astype(bf16)


def attention_first(
    tokens_ref, gain_ref, qkv_ref, bias_ref, out_ref, low_ref, triple_ref, weights_ref, mixture_ref, part_ref
):
    mixture = attend(
        tokens_ref[...].astype(f32), gain_ref, qkv_ref, bias_ref, low_ref, triple_ref, weights_ref
    )
    mixture_ref[...] = mixture
    go(mixture_ref)
    part_ref[...] = dot(mixture, out_ref[...]).astype(bf16)


def attention_next(
    middle_ref,
    z0,
    z1,
    z2,
    z3,
    gain_ref,
    qkv_ref,
    bias_ref,
    out_ref,
    current_ref,
    low_ref,
    triple_ref,
    weights_ref,
    mixture_ref,
    part_ref,
):
    current = middle_ref[...] + four(z0[...], z1[...], z2[...], z3[...])
    current_ref[...] = current
    go(current_ref)
    mixture = attend(current, gain_ref, qkv_ref, bias_ref, low_ref, triple_ref, weights_ref)
    mixture_ref[...] = mixture
    go(mixture_ref)
    part_ref[...] = dot(mixture, out_ref[...]).astype(bf16)


def route_rows(middle, gain_ref, router_ref, across, low_ref, gates_ref):
    low = (middle * scale_of(middle) * gain_ref[1:2, :]).astype(bf16)
    low_ref[...] = low
    go(low_ref)
    logits = dot(low, router_ref[...], 1, 1)
    lane = iota((ROWS, EXPERTS), 1).astype(f32)
    chosen = [
        jnp.sum(jnp.where(lane == across[:, 6 + k : 7 + k], logits, 0.0), axis=1, keepdims=True)
        for k in range(2)
    ]
    top = jnp.maximum(chosen[0], chosen[1])
    raised = [jnp.exp(c - top) for c in chosen]
    total = raised[0] + raised[1]
    gates = [r / total for r in raised]
    place = iota((ROWS, ROWS), 1)
    gates_ref[...] = jnp.where(place == 0, gates[0], jnp.where(place == 1, gates[1], 0.0))
    return low, gates


def route_first(
    current_ref,
    p0,
    p1,
    p2,
    p3,
    gain_ref,
    router_ref,
    across_ref,
    down_ref,
    middle_ref,
    low_ref,
    gates_ref,
    send_ref,
):
    middle = current_ref[...].astype(f32) + four(p0[...], p1[...], p2[...], p3[...])
    middle_ref[...] = middle
    go(middle_ref)
    low, gates = route_rows(middle, gain_ref, router_ref, across_ref[...], low_ref, gates_ref)
    main, rest = dispatch(down_ref[...], [low])
    send_ref[:, :WIDTH] = main
    send_ref[:, WIDTH:] = rest


def route_next(
    current_ref,
    p0,
    p1,
    p2,
    p3,
    gain_ref,
    router_ref,
    across_ref,
    down_ref,
    cotangent_ref,
    middle_ref,
    low_ref,
    gates_ref,
    send_ref,
):
    middle = current_ref[...].astype(f32) + four(p0[...], p1[...], p2[...], p3[...])
    middle_ref[...] = middle
    go(middle_ref)
    low, gates = route_rows(middle, gain_ref, router_ref, across_ref[...], low_ref, gates_ref)
    main, rest = dispatch(down_ref[...], [low])
    send_ref[:, :WIDTH] = main
    send_ref[:, WIDTH:SENT] = rest
    gradient = cotangent_ref[...].astype(f32)
    main, rest = dispatch(down_ref[...], [(gate * gradient).astype(bf16) for gate in gates])
    send_ref[:, SENT : SENT + WIDTH] = main
    send_ref[:, SENT + WIDTH :] = rest


CURVE = (2.0 / 3.141592653589793) ** 0.5


def gelu_parts(values):
    squared = values * values
    bent = jnp.tanh(CURVE * values * (1.0 + 0.044715 * squared))
    return bent, squared


def gelu(values):
    bent, _ = gelu_parts(values)
    return 0.5 * values * (1.0 + bent)


def gelu_slope(values):
    bent, squared = gelu_parts(values)
    inner = CURVE * (1.0 + 3.0 * 0.044715 * squared)
    return 0.5 * (1.0 + bent) + 0.5 * values * (1.0 - bent * bent) * inner


def expert_forward(got_ref, in_ref, out_ref, rows_ref, before_ref, active_ref, back_ref):
    unpack(got_ref, 0, rows_ref)
    before = dot(rows_ref[...], in_ref[...])
    before_ref[...] = before
    go(rows_ref, before_ref)
    active = gelu(before).astype(bf16)
    active_ref[...] = active
    go(active_ref)
    pack(dot(active, out_ref[...]).astype(bf16), 0, back_ref)


def expert_backward(got_ref, before_ref, in_ref, out_ref, grads_ref, down_ref, back_ref):
    unpack(got_ref, 0, grads_ref)
    go(grads_ref)
    grad_active = dot(grads_ref[...], out_ref[...], 1, 1)
    grad_before = (grad_active * gelu_slope(before_ref[...])).astype(bf16)
    down_ref[...] = grad_before
    go(down_ref)
    pack(dot(grad_before, in_ref[...], 1, 1).astype(bf16), 0, back_ref)


def expert_both(got_ref, in_ref, out_ref, rows_ref, active_ref, grads_ref, down_ref, back_ref):
    unpack(got_ref, 0, rows_ref)
    unpack(got_ref, SENT, grads_ref)
    go(rows_ref, grads_ref)
    before = dot(rows_ref[...], in_ref[...])
    active = gelu(before).astype(bf16)
    active_ref[...] = active
    go(active_ref)
    pack(dot(active, out_ref[...]).astype(bf16), 0, back_ref)
    grad_active = dot(grads_ref[...], out_ref[...], 1, 1)
    grad_before = (grad_active * gelu_slope(before)).astype(bf16)
    down_ref[...] = grad_before
    go(down_ref)
    pack(dot(grad_before, in_ref[...], 1, 1).astype(bf16), SENT, back_ref)


def expert_grads_top(rows_ref, active_ref, grads_ref, down_ref, in_grad_ref, out_grad_ref):
    in_grad_ref[0, 0] = dot(rows_ref[...], down_ref[...], 0)
    out_grad_ref[0, 0] = dot(active_ref[...], grads_ref[...], 0)


def expert_grads_low(rows_ref, active_ref, grads_ref, down_ref, _, __, in_grad_ref, out_grad_ref):
    expert_grads_top(rows_ref, active_ref, grads_ref, down_ref, in_grad_ref, out_grad_ref)


def combine_first(got_ref, across_ref, gates_ref, part_ref, picked_ref):
    main, rest = got_ref[:, :WIDTH], got_ref[:, WIDTH:]
    across, gates = across_ref[...], gates_ref[...]
    left, right = 0.0, 0.0
    for route in range(2):
        one, two = pick(across, route, main, rest)
        picked_ref[route, :, :HALF] = one.astype(bf16)
        picked_ref[route, :, HALF:] = two.astype(bf16)
        left = left + gates[:, route : route + 1] * one
        right = right + gates[:, route : route + 1] * two
    part_ref[:, :HALF] = left.astype(bf16)
    part_ref[:, HALF:] = right.astype(bf16)


def gate_rows(grads):
    place = iota((8, ROWS), 0)
    rows = [row_of(grad, ROWS) for grad in grads]
    both = jnp.where(place == 0, rows[0], jnp.where(place == 1, rows[1], 0.0))
    moved = jnp.where(place == 2, rows[0], jnp.where(place == 3, rows[1], 0.0))
    left = moved - moved.astype(bf16).astype(f32)
    return (both + left).astype(bf16)


def gathered_back(got_ref, offset, across, rows, into_ref):
    main = got_ref[:, offset : offset + WIDTH]
    rest = got_ref[:, offset + WIDTH : offset + SENT]
    left, right = pick(across, 0, main, rest)
    other_left, other_right = pick(across, 1, main, rest)
    into_ref[:ROWS, :HALF] = (left + other_left).astype(bf16)
    into_ref[:ROWS, HALF:] = (right + other_right).astype(bf16)
    into_ref[ROWS:, :ROWS] = rows
    into_ref[ROWS:, ROWS:] = jnp.zeros((8, WIDTH - ROWS), bf16)


def combine_next(got_ref, across_ref, gates_ref, cotangent_ref, part_ref, back_ref):
    main, rest = got_ref[:, :WIDTH], got_ref[:, WIDTH:SENT]
    across, gates = across_ref[...], gates_ref[...]
    gradient = cotangent_ref[...].astype(f32)
    left, right, grads = 0.0, 0.0, []
    for route in range(2):
        one, two = pick(across, route, main, rest)
        left = left + gates[:, route : route + 1] * one
        right = right + gates[:, route : route + 1] * two
        grads.append(
            jnp.sum(gradient[:, :HALF] * one + gradient[:, HALF:] * two, axis=1, keepdims=True)
        )
    part_ref[:, :HALF] = left.astype(bf16)
    part_ref[:, HALF:] = right.astype(bf16)
    gathered_back(got_ref, SENT, across, gate_rows(grads), back_ref)


def combine_back(got_ref, across_ref, rows_ref, back_ref):
    gathered_back(got_ref, 0, across_ref[...], rows_ref[...], back_ref)


def attention_back(
    e0,
    e1,
    e2,
    e3,
    gates_ref,
    across_ref,
    router_ref,
    middle_ref,
    gain_ref,
    gradient_ref,
    out_ref,
    triple_ref,
    weights_ref,
    qkv_ref,
    hot_ref,
    after_ref,
    low_ref,
    back_triple_ref,
    part_ref,
    logits_ref,
    gain_grad_ref,
    table_grad_ref,
):
    total = four(e0[...], e1[...], e2[...], e3[...])
    gates = gates_ref[...]
    across = across_ref[...]
    gate = [gates[:, k : k + 1] for k in range(2)]
    rows = total[ROWS:, :ROWS]
    grad_gate = [column_of(rows[k : k + 1] + rows[k + 2 : k + 3], ROWS) for k in range(2)]
    mean = gate[0] * grad_gate[0] + gate[1] * grad_gate[1]
    lane = iota((ROWS, EXPERTS), 1).astype(f32)
    grad_logits = 0.0
    for k in range(2):
        grad_logits = grad_logits + jnp.where(
            lane == across[:, 6 + k : 7 + k], gate[k] * (grad_gate[k] - mean), 0.0
        )
    high = grad_logits.astype(bf16)
    low = (grad_logits - high.astype(f32)).astype(bf16)
    logits_ref[:, :EXPERTS] = high
    logits_ref[:, EXPERTS : 2 * EXPERTS] = low
    logits_ref[:, 2 * EXPERTS :] = jnp.zeros((ROWS, 128 - 2 * EXPERTS), bf16)
    grad_low = total[:ROWS] + dot(high, router_ref[...]) + dot(low, router_ref[...])
    grad_middle, gain_grad_ref[...] = norm_back(middle_ref[...], gain_ref[1:2, :], grad_low)
    after = gradient_ref[...].astype(f32) + grad_middle
    after_ref[...] = after
    low_after = after.astype(bf16)
    low_ref[...] = low_after
    go(after_ref, low_ref, logits_ref, gain_grad_ref)
    grad_mixture = dot(low_after, out_ref[...], 1, 1).astype(bf16)
    queries, keys, values = triple_ref[0], triple_ref[1], triple_ref[2]
    grad_queries = jnp.zeros((ROWS, QUARTER), f32)
    grad_keys, grad_values = grad_queries, grad_queries
    diagonals = jnp.zeros((8, 256), f32)
    flip = one_hot(iota((ROWS, ROWS), 0) + iota((ROWS, ROWS), 1) == ROWS - 1)
    for head in range(HERE):
        mask = head_mask(head)
        masked_grad = grad_mixture * mask
        weights = weights_ref[head]
        grad_values = grad_values + dot(weights.astype(bf16), masked_grad, 0)
        grad_weights = dot(masked_grad, values, 1, 1)
        grad_scores = weights * (
            grad_weights - jnp.sum(weights * grad_weights, axis=-1, keepdims=True)
        )
        grad_scores = grad_scores.astype(bf16)
        grad_queries = grad_queries + dot(grad_scores, keys * mask)
        grad_keys = grad_keys + dot(grad_scores, queries * mask, 0)
        wide = jnp.concatenate([dot(flip, grad_scores), jnp.zeros((ROWS, 128), f32)], axis=1)
        turned = pltpu.roll(wide, 0, axis=1, stride=1, stride_axis=0)
        diagonals = jnp.where(
            iota((8, 256), 0) == head, jnp.sum(turned, axis=0, keepdims=True), diagonals
        )
    table_grad_ref[...] = dot(diagonals, hot_ref[...], 1, 1, precision=highest)
    grad_input = 0.0
    for k, grad in enumerate((grad_queries * HEAD**-0.5, grad_keys * HEAD**-0.5, grad_values)):
        grad = grad.astype(bf16)
        back_triple_ref[:, k * QUARTER : (k + 1) * QUARTER] = grad
        grad_input = grad_input + dot(grad, qkv_ref[k])
    go(back_triple_ref)
    part_ref[...] = grad_input.astype(bf16)


SHARE = WIDTH // EXPERTS
GROUPS = WIDTH // 128


def router_places():
    row, column = iota((WIDTH, GROUPS * EXPERTS), 0), iota((WIDTH, GROUPS * EXPERTS), 1)
    return one_hot(row == (column & (EXPERTS - 1)) * SHARE + (column >> 5))


def folded(line):
    place = iota((8, 128), 0)
    rows = jnp.zeros((8, 128), f32)
    for part in range(GROUPS):
        rows = jnp.where(place == part, line[:, part * 128 : (part + 1) * 128], rows)
    return rows


def unfolded(rows):
    return jnp.concatenate([rows[part : part + 1, :] for part in range(GROUPS)], axis=1)


def fill_grads(low, back_triple, mixture, after, low_two, logits, gains, table, grads_ref):
    kind = grads_ref.dtype
    qkv_rows = 3 * QUARTER
    grads_ref[:qkv_rows, :WIDTH] = dot(back_triple, low, 0).astype(kind)
    grads_ref[qkv_rows:, :WIDTH] = dot(mixture, after, 0).astype(kind)
    both = dot(logits, low_two, 0)
    total = both[:EXPERTS] + both[EXPERTS : 2 * EXPERTS]
    parts = jnp.concatenate([total[:, r * 128 : (r + 1) * 128] for r in range(GROUPS)], axis=0)
    places = router_places()
    high = parts.astype(bf16)
    rest = (parts - high.astype(f32)).astype(bf16)
    grads_ref[:, WIDTH:] = (dot(places, high) + dot(places, rest)).astype(kind)
    for chunk, gain in enumerate(gains):
        start = chunk * SHARE + 8
        grads_ref[start : start + 8, WIDTH:] = folded(gain).astype(kind)
    start = 2 * SHARE + 8
    grads_ref[start : start + 8, WIDTH : WIDTH + EXPERTS] = table.astype(kind)


def weight_grads(
    low_ref, back_triple_ref, mixture_ref, after_ref, low_two_ref, logits_ref, gain, table, grads_ref
):
    operands = (low_ref, back_triple_ref, mixture_ref, after_ref, low_two_ref, logits_ref)
    fill_grads(*[ref[...] for ref in operands], [gain[...]], table[...], grads_ref)


def attention_back_low(*refs):
    operands, (low_ref, mixture_ref, low_two_ref, gain10_ref) = refs[:15], refs[15:19]
    after_ref, part_ref, grads_ref, held_low, held_triple, held_logits, held_gain, held_table = refs[19:]
    attention_back(
        *operands,
        after_ref,
        held_low,
        held_triple,
        part_ref,
        held_logits,
        held_gain,
        held_table,
    )
    operands = (low_ref, held_triple, mixture_ref, held_low, low_two_ref, held_logits)
    fill_grads(
        *[ref[...] for ref in operands],
        [held_gain[...], gain10_ref[...]],
        held_table[...],
        grads_ref,
    )


def start_back(
    after_ref,
    d0,
    d1,
    d2,
    d3,
    input_ref,
    gain_ref,
    gates_ref,
    down_ref,
    picked_ref,
    gradient_ref,
    gain_grad_ref,
    rows_ref,
    send_ref,
):
    grad_low = four(d0[...], d1[...], d2[...], d3[...])
    grad_input, gain_grad_ref[...] = norm_back(input_ref[...].astype(f32), gain_ref[0:1, :], grad_low)
    gradient = after_ref[...] + grad_input
    gradient_ref[...] = gradient
    go(gradient_ref, gain_grad_ref)
    gates = gates_ref[...]
    weighted = [(gates[:, k : k + 1] * gradient).astype(bf16) for k in range(2)]
    main, rest = dispatch(down_ref[...], weighted)
    send_ref[:, :WIDTH] = main
    send_ref[:, WIDTH:] = rest
    rows_ref[...] = gate_rows(
        [jnp.sum(gradient * picked_ref[k].astype(f32), axis=1, keepdims=True) for k in range(2)]
    )


def finish_back(after_ref, d0, d1, d2, d3, input_ref, gain_ref, gradient_ref, gain_grad_ref):
    grad_low = four(d0[...], d1[...], d2[...], d3[...])
    grad_input, gain_grad_ref[...] = norm_back(input_ref[...].astype(f32), gain_ref[0:1, :], grad_low)
    gradient_ref[...] = after_ref[...] + grad_input


def finish_output(middle_ref, z0, z1, z2, z3, output_ref):
    output_ref[...] = (middle_ref[...] + four(z0[...], z1[...], z2[...], z3[...])).astype(bf16)


def add_chunks(chunks_ref, gain00_ref, spread_ref):
    total = chunks_ref[0:SHARE, :].astype(f32)
    for block in range(1, EXPERTS):
        total = total + chunks_ref[block * SHARE : (block + 1) * SHARE, :].astype(f32)
    total = total.astype(bf16)
    gain = folded(gain00_ref[...]).astype(bf16)
    for block in range(EXPERTS):
        start = block * SHARE
        spread_ref[start : start + SHARE, :] = total
        spread_ref[start + 16 : start + SHARE, WIDTH:] = gain


def router_rows(small):
    places = router_places()
    high = small.astype(bf16)
    parts = dot(places, high, 0) + dot(places, (small - high.astype(f32)).astype(bf16), 0)
    return jnp.concatenate(
        [parts[r * EXPERTS : (r + 1) * EXPERTS] for r in range(GROUPS)], axis=1
    )


def place_top(
    grads_ref, qkv_ref, out_ref, router_ref, gain_ref, table_ref, wide, small, rows, done
):
    fetch = pltpu.make_async_copy(grads_ref.at[:, WIDTH:], small, done.at[0])
    fetch.start()
    arriving, leaving = [], []
    for k in range(4):
        source = grads_ref.at[k * QUARTER : (k + 1) * QUARTER, :WIDTH]
        target = qkv_ref.at[1, k] if k < 3 else out_ref.at[1]
        arriving.append(pltpu.make_async_copy(source, wide.at[k], done.at[1 + k]))
        leaving.append(pltpu.make_async_copy(wide.at[k], target, done.at[5 + k]))
        arriving[-1].start()
    fetch.wait()
    lanes = small[...]
    rows[...] = router_rows(lanes)
    leaving.append(pltpu.make_async_copy(rows, router_ref.at[1], done.at[9]))
    leaving[-1].start()
    gain_ref[...] = unfolded(lanes[8:16])
    table_ref[...] = lanes[2 * SHARE + 8 : 2 * SHARE + 16]
    for k in range(4):
        arriving[k].wait()
        leaving[k].start()
    for copy in leaving:
        copy.wait()


def place_low(
    grads_ref,
    gain_ref,
    table_ref,
    _,
    __,
    ___,
    qkv_ref,
    out_ref,
    router_ref,
    gains_ref,
    tables_ref,
    wide,
    rows,
    done,
):
    copies = []
    for k in range(4):
        wide[k] = grads_ref[k * QUARTER : (k + 1) * QUARTER, :WIDTH].astype(f32)
        target = qkv_ref.at[0, k] if k < 3 else out_ref.at[0]
        copies.append(pltpu.make_async_copy(wide.at[k], target, done.at[k]))
        copies[-1].start()
    small = grads_ref[:, WIDTH:].astype(f32)
    rows[...] = router_rows(small)
    copies.append(pltpu.make_async_copy(rows, router_ref.at[0], done.at[4]))
    copies[-1].start()
    first = small[16:SHARE]
    for block in range(1, EXPERTS):
        first = first + small[block * SHARE + 16 : (block + 1) * SHARE]
    gains_ref[0, 0:1, :] = unfolded(first)
    gains_ref[0, 1:2, :] = unfolded(small[8:16])
    gains_ref[1, 0:1, :] = unfolded(small[SHARE + 8 : SHARE + 16])
    gains_ref[1, 1:2, :] = gain_ref[...]
    table = small[2 * SHARE + 8 : 2 * SHARE + 16]
    for head in range(HERE):
        tables_ref[head, 0:1, :] = table[head : head + 1, :EXPERTS]
        tables_ref[head, 1:2, :] = table_ref[head : head + 1, :EXPERTS]
    for copy in copies:
        copy.wait()


def place(top_grads, low_grads):
    stacks = [
        pltpu.HBM((2, 3, QUARTER, WIDTH), f32),
        pltpu.HBM((2, QUARTER, WIDTH), f32),
        pltpu.HBM((2, EXPERTS, WIDTH), f32),
    ]
    hbm, vmem = pl.BlockSpec(memory_space=pltpu.HBM), pl.BlockSpec(memory_space=pltpu.VMEM)
    params = pltpu.CompilerParams(vmem_limit_bytes=16 * 1024 * 1024)
    *stacked, gain, table = pl.pallas_call(
        place_top,
        out_shape=[
            *stacks,
            jax.ShapeDtypeStruct((1, WIDTH), f32),
            jax.ShapeDtypeStruct((8, 128), f32),
        ],
        in_specs=[hbm],
        out_specs=[hbm] * 3 + [vmem] * 2,
        scratch_shapes=[
            pltpu.VMEM((4, QUARTER, WIDTH), f32),
            pltpu.VMEM((WIDTH, 128), f32),
            pltpu.VMEM((EXPERTS, WIDTH), f32),
            pltpu.SemaphoreType.DMA((10,)),
        ],
        compiler_params=params,
        name="place_top",
    )(in_hbm(top_grads))
    return pl.pallas_call(
        place_low,
        out_shape=[
            *stacks,
            jax.ShapeDtypeStruct((2, 2, WIDTH), f32),
            jax.ShapeDtypeStruct((HERE, 2, EXPERTS), f32),
        ],
        in_specs=[vmem] * 3 + [hbm] * 3,
        out_specs=[hbm] * 3 + [vmem] * 2,
        scratch_shapes=[
            pltpu.VMEM((4, QUARTER, WIDTH), f32),
            pltpu.VMEM((EXPERTS, WIDTH), f32),
            pltpu.SemaphoreType.DMA((5,)),
        ],
        input_output_aliases={3: 0, 4: 1, 5: 2},
        compiler_params=params,
        name="place_low",
    )(low_grads, gain, table, *[in_hbm(s) for s in stacked])


def around(values):
    sent = [
        lax.ppermute(values, "tensor", [(i, (i + shift) % 4) for i in range(4)]) for shift in (1, 2, 3)
    ]
    return [values, *sent]


def across_experts(values):
    return lax.all_to_all(values, "expert", 0, 0, tiled=True)


def shards(
    tokens,
    segment_ids,
    expert_routes,
    bucket_ids,
    proj_qkv,
    proj_out,
    bias_table,
    norm_gains,
    router,
    expert_in,
    expert_out,
    cotangent,
):
    qkv = proj_qkv.transpose(0, 1, 3, 2)
    router = router.transpose(0, 2, 1)
    expert_in, expert_out = expert_in[:, 0], expert_out[:, 0]
    gains = norm_gains
    row = (ROWS, WIDTH)
    narrow = (ROWS, QUARTER)
    scores = (HERE, ROWS, ROWS)
    slots = (MAIN + REST, WIDTH)
    stacked = (2, 1, WIDTH, WIDTH)
    bias, across, down, hot = call(
        setup,
        [
            ((2, HERE, ROWS, ROWS), f32),
            ((2, ROWS, ROWS), f32),
            ((2, 8, ROWS), f32),
            ((EXPERTS, 256), f32),
        ],
        Late(bucket_ids.reshape(1, -1)),
        Late(bias_table.transpose(2, 0, 1)),
        Late(segment_ids),
        Late(expert_routes.transpose(0, 2, 1)),
    )
    kept = [
        Kept(row, bf16),
        Kept((3, *narrow), bf16),
        Kept(scores, f32),
        Kept(narrow, bf16),
        (row, bf16),
    ]

    low_a0, triple0, weights0, mixture0, part = call(
        attention_first,
        kept,
        Late(tokens),
        Late(Layer(gains, 0)),
        Late(Layer(qkv, 0)),
        Layer(bias, 0),
        Late(Layer(proj_out, 0)),
    )
    middle0, low_b0, gates0, send = call(
        route_first,
        [Kept(row, f32), Kept(row, bf16), ((ROWS, ROWS), f32), ((MAIN, SENT), bf16)],
        tokens,
        *around(part),
        Layer(gains, 0),
        Late(Layer(router, 0)),
        Layer(across, 0),
        Layer(down, 0),
    )
    rows0, before0, active0, send = call(
        expert_forward,
        [Kept(slots, bf16), Kept(slots, f32), Kept(slots, bf16), ((MAIN, SENT), bf16)],
        across_experts(send),
        Layer(expert_in, 0),
        Layer(expert_out, 0),
    )
    part, picked0 = call(
        combine_first,
        [(row, bf16), Kept((2, *row), bf16)],
        across_experts(send),
        Layer(across, 0),
        gates0,
    )

    current1, low_a1, triple1, weights1, mixture1, part = call(
        attention_next,
        [Kept(row, f32), *kept],
        Late(middle0),
        *around(part),
        Layer(gains, 1),
        Late(Layer(qkv, 1)),
        Late(Layer(bias, 1)),
        Late(Layer(proj_out, 1)),
    )
    middle1, low_b1, gates1, send = call(
        route_next,
        [Kept(row, f32), Kept(row, bf16), ((ROWS, ROWS), f32), ((MAIN, 2 * SENT), bf16)],
        Late(current1),
        *around(part),
        Layer(gains, 1),
        Late(Layer(router, 1)),
        Layer(across, 1),
        Layer(down, 1),
        cotangent,
    )
    rows1, active1, grads1, down1, send = call(
        expert_both,
        [*[Kept(slots, bf16)] * 4, ((MAIN, 2 * SENT), bf16)],
        across_experts(send),
        Layer(expert_in, 1),
        Layer(expert_out, 1),
    )
    got = across_experts(send)
    in_grads, out_grads = call_stacked(
        expert_grads_top, 1, (rows1, active1, grads1, down1), stacked
    )
    moved, back = call(
        combine_next,
        [(row, bf16), ((LONG, WIDTH), bf16)],
        got,
        Layer(across, 1),
        gates1,
        cotangent,
    )

    back_kept = [
        Kept(row, f32),
        Kept(row, bf16),
        Kept((ROWS, 3 * QUARTER), bf16),
        (row, bf16),
        Kept((ROWS, 128), bf16),
        Kept((1, WIDTH), f32),
        Kept((8, EXPERTS), f32),
    ]
    after1, low_after1, back_triple1, part, logits1, gain11, table1 = call(
        attention_back,
        back_kept,
        *around(back),
        gates1,
        Layer(across, 1),
        Late(Layer(router, 1)),
        middle1,
        Layer(gains, 1),
        cotangent,
        Late(Layer(proj_out, 1)),
        triple1,
        weights1,
        Late(Layer(qkv, 1)),
        hot,
    )
    parts = around(part)
    (top_grads,) = call(
        weight_grads,
        [Kept((WIDTH, SUMMED), f32)],
        Late(low_a1),
        Late(back_triple1),
        Late(mixture1),
        Late(low_after1),
        Late(low_b1),
        Late(logits1),
        Late(gain11),
        Late(table1),
    )
    top_grads = lax.psum(top_grads, "expert")
    parts, in_grads = lax.optimization_barrier((parts, in_grads))

    def low_layer(_, carried):
        in_grads, out_grads, after, _ = carried
        gradient0, gain10, rows0b, send = call(
            start_back,
            [Kept(row, f32), Kept((1, WIDTH), f32), ((8, ROWS), bf16), ((MAIN, SENT), bf16)],
            Late(after),
            *parts,
            Late(current1),
            Late(Layer(gains, 1)),
            gates0,
            Layer(down, 0),
            Late(picked0),
        )
        grads0, down0, send = call(
            expert_backward,
            [Kept(slots, bf16), Kept(slots, bf16), ((MAIN, SENT), bf16)],
            across_experts(send),
            Late(before0),
            Late(Layer(expert_in, 0)),
            Late(Layer(expert_out, 0)),
        )
        got = across_experts(send)
        in_grads, out_grads = call_stacked(
            expert_grads_low, 0, (rows0, active0, grads0, down0), stacked, (in_grads, out_grads)
        )
        (back,) = call(combine_back, [((LONG, WIDTH), bf16)], got, Layer(across, 0), rows0b)
        backs = around(back)
        backs, in_grads = lax.optimization_barrier((backs, in_grads))
        after0, part, grads = call(
            attention_back_low,
            [Kept(row, f32), (row, bf16), Kept((WIDTH, SUMMED), bf16)],
            *backs,
            gates0,
            Layer(across, 0),
            Layer(router, 0),
            Late(middle0),
            Layer(gains, 0),
            Late(gradient0),
            Layer(proj_out, 0),
            Late(triple0),
            Late(weights0),
            Layer(qkv, 0),
            Late(hot),
            Late(low_a0),
            Late(mixture0),
            Late(low_b0),
            Late(gain10),
            held=[
                (row, bf16),
                ((ROWS, 3 * QUARTER), bf16),
                ((ROWS, 128), bf16),
                ((1, WIDTH), f32),
                ((8, EXPERTS), f32),
            ],
        )
        low_parts = around(part)
        tokens_grad, gain00 = call(
            finish_back,
            [Kept(row, f32), Kept((1, WIDTH), f32)],
            after0,
            *low_parts,
            tokens,
            Layer(gains, 0),
        )
        (spread,) = call(
            add_chunks,
            [Kept((WIDTH, SUMMED), bf16)],
            across_experts(grads),
            Late(gain00),
        )
        return in_grads, out_grads, tokens_grad, spread

    once = jnp.minimum(jnp.maximum(bucket_ids[0], 0) + 1, 1)
    in_grads, out_grads, tokens_grad, spread = lax.fori_loop(
        0,
        once,
        low_layer,
        (
            in_grads,
            out_grads,
            after1,
            jnp.zeros((WIDTH, SUMMED), bf16),
        ),
    )
    low_grads = across_experts(spread)
    (output,) = call(finish_output, [Kept(row, bf16)], middle1, *around(moved))
    qkv_grad, out_grad, router_grad, gain_grads, table_grad = place(top_grads, low_grads)
    return (
        output,
        tokens_grad,
        qkv_grad.transpose(0, 1, 3, 2),
        out_grad,
        table_grad.transpose(1, 2, 0),
        gain_grads,
        router_grad.transpose(0, 2, 1),
        in_grads,
        out_grads,
    )


def solution(mesh):
    placed = (
        P("expert", None),
        P("expert", None),
        P(None, "expert", None),
        P(),
        P(None, None, None, "tensor"),
        P(None, "tensor", None),
        P(None, None, "tensor"),
        P(),
        P(),
        P(None, "expert", None, "tensor"),
        P(None, "expert", "tensor", None),
        P("expert", None),
    )
    return jax.shard_map(
        shards,
        mesh=mesh,
        in_specs=placed,
        out_specs=(
            P("expert", None),
            P("expert", None),
            P(None, None, None, "tensor"),
            P(None, "tensor", None),
            P(None, None, "tensor"),
            P(),
            P(),
            P(None, "expert", None, "tensor"),
            P(None, "expert", "tensor", None),
        ),
        check_vma=False,
    )
```

```python
import jax
import jax.numpy as jnp
from jax import lax
from jax.experimental import pallas as pl
from jax.experimental.pallas import tpu as pltpu
from jax.sharding import PartitionSpec as P

epsilon = 1e-06
masked_score = -1000000000.0
highest = lax.Precision.HIGHEST
f32, bf16 = jnp.float32, jnp.bfloat16

ROWS = 128
WIDTH = 768
QUARTER = 192
HERE = 3
HEAD = 64
EXPERTS = 32
MAIN = EXPERTS * 8
REST = 128
HALF = WIDTH // 2
SENT = WIDTH + HALF
SUMMED = WIDTH + 128
LONG = ROWS + 8


class Layer:
    def __init__(self, array, layer):
        self.array, self.layer = array, layer


class Late:
    def __init__(self, operand):
        self.operand = operand


class Kept:
    def __init__(self, shape, dtype):
        self.shape, self.dtype = shape, dtype


class Arriving:
    def __init__(self, source, held, done):
        self.held, self.copy, self.here = held, pltpu.make_async_copy(source, held, done), False
        self.copy.start()

    @property
    def shape(self):
        return self.held.shape

    def __getitem__(self, index):
        self.wait()
        return self.held[index]

    def wait(self):
        if not self.here:
            self.copy.wait()
            self.here = True


class Leaving:
    def __init__(self, held, target, done):
        self.held, self.copy, self.gone = held, pltpu.make_async_copy(held, target, done), False

    @property
    def dtype(self):
        return self.held.dtype

    def __getitem__(self, index):
        return self.held[index]

    def __setitem__(self, index, value):
        self.held[index] = value

    def go(self):
        if not self.gone:
            self.copy.start()
            self.gone = True


def go(*refs):
    for ref in refs:
        if isinstance(ref, Leaving):
            ref.go()


def in_hbm(array):
    return pltpu.with_memory_space_constraint(array, pltpu.HBM)


def call(body, outs, *operands, held=(), limit=16):
    late = [isinstance(o, Late) for o in operands]
    inner = [o.operand if isinstance(o, Late) else o for o in operands]
    arrays = [o.array if isinstance(o, Layer) else o for o in inner]
    parts = [a.shape[1:] if isinstance(o, Layer) else a.shape for o, a in zip(inner, arrays)]
    arrays = [in_hbm(a) if is_late else a for a, is_late in zip(arrays, late)]
    kept = [isinstance(o, Kept) for o in outs]
    shapes = [(o.shape, o.dtype) if isinstance(o, Kept) else o for o in outs]
    scratch = [pltpu.VMEM(p, a.dtype) for p, a, is_late in zip(parts, arrays, late) if is_late]
    scratch += [pltpu.VMEM(*o) for o, is_kept in zip(shapes, kept) if is_kept]
    copies = len(scratch)
    scratch += [pltpu.VMEM(*h) for h in held]
    if copies:
        scratch.append(pltpu.SemaphoreType.DMA((copies,)))

    def kernel(*refs):
        count = len(operands) + len(outs)
        spare = list(refs[count:])
        done = spare.pop() if copies else None
        given, used = [], 0
        for ref, operand, is_late in zip(refs, inner, late):
            view = ref.at[operand.layer] if isinstance(operand, Layer) else ref
            if is_late:
                view = Arriving(view, spare[used], done.at[used])
                used += 1
            given.append(view)
        taken, leaving = [], []
        for ref, is_kept in zip(refs[len(operands) : count], kept):
            if is_kept:
                ref = Leaving(spare[used], ref, done.at[used])
                leaving.append(ref)
                used += 1
            taken.append(ref)
        body(*given, *taken, *spare[used:])
        go(*leaving)
        for ref in leaving:
            ref.copy.wait()
        for view in given:
            if isinstance(view, Arriving):
                view.wait()

    return pl.pallas_call(
        kernel,
        out_shape=[
            pltpu.HBM(*o) if is_kept else jax.ShapeDtypeStruct(*o) for o, is_kept in zip(shapes, kept)
        ],
        in_specs=[pl.BlockSpec(memory_space=pltpu.HBM if n else pltpu.VMEM) for n in late],
        out_specs=[pl.BlockSpec(memory_space=pltpu.HBM if n else pltpu.VMEM) for n in kept],
        scratch_shapes=scratch,
        compiler_params=pltpu.CompilerParams(vmem_limit_bytes=limit * 1024 * 1024),
        name=body.__name__,
    )(*arrays)


def call_stacked(body, layer, operands, stacked, earlier=()):
    whole = [pl.BlockSpec(o.shape, lambda _, n=o.ndim: (0,) * n) for o in operands]
    part = pl.BlockSpec((1, 1, *stacked[2:]), lambda _: (layer, 0, 0, 0))
    return pl.pallas_call(
        body,
        grid=(1,),
        out_shape=[pltpu.HBM(stacked, f32)] * 2,
        in_specs=whole + [pl.BlockSpec(memory_space=pltpu.HBM)] * len(earlier),
        out_specs=[part] * 2,
        input_output_aliases={len(operands) + n: n for n in range(len(earlier))},
        compiler_params=pltpu.CompilerParams(vmem_limit_bytes=24 * 1024 * 1024),
        name=body.__name__,
    )(*[in_hbm(o) for o in (*operands, *earlier)])


def dot(left, right, left_axis=1, right_axis=0, precision=None):
    return lax.dot_general(
        left,
        right,
        (((left_axis,), (right_axis,)), ((), ())),
        precision=precision,
        preferred_element_type=f32,
    )


def iota(shape, axis):
    return lax.broadcasted_iota(jnp.int32, shape, axis)


def scale_of(values):
    return lax.rsqrt(jnp.mean(values * values, axis=-1, keepdims=True) + epsilon)


def norm_back(values, gain, upstream):
    inverse = scale_of(values)
    inner = upstream * gain
    mean = jnp.mean(inner * values, axis=-1, keepdims=True)
    back = inverse * inner - values * (inverse * inverse * inverse * mean)
    return back, jnp.sum(upstream * (values * inverse), axis=0, keepdims=True)


def head_mask(head):
    lane = iota((1, QUARTER), 1)
    return ((lane >= head * HEAD) & (lane < (head + 1) * HEAD)).astype(f32).astype(bf16)


def four(own, one, two, three):
    return (own.astype(f32) + two.astype(f32)) + (one.astype(f32) + three.astype(f32))


def column_of(row, size):
    same = iota((size, size), 0) == iota((size, size), 1)
    return jnp.sum(jnp.where(same, jnp.broadcast_to(row, (size, size)), 0.0), axis=1, keepdims=True)


def row_of(column, size):
    same = iota((size, size), 0) == iota((size, size), 1)
    return jnp.sum(jnp.where(same, jnp.broadcast_to(column, (size, size)), 0.0), axis=0, keepdims=True)


def setup(ids_ref, table_ref, segment_ref, routes_ref, bias_ref, across_ref, down_ref, hot_ref):
    offsets = ids_ref.shape[1]
    hot = one_hot(iota((EXPERTS, offsets), 0) == ids_ref[...])
    mirror = one_hot(iota((offsets, 256), 0) + iota((offsets, 256), 1) == offsets - 1)
    hot = dot(hot, mirror)
    hot_ref[...] = hot
    tables = table_ref[...]
    segment = segment_ref[...].astype(f32)
    allowed = (column_of(segment, ROWS) == segment) & (iota((ROWS, ROWS), 1) <= iota((ROWS, ROWS), 0))
    lane = iota((ROWS, ROWS), 1)
    before = one_hot(lane < iota((ROWS, ROWS), 0))
    for layer in range(2):
        by_offset = dot(tables[:, layer, :], hot, precision=highest)
        for head in range(HERE):
            line = jnp.broadcast_to(by_offset[head : head + 1, :], (ROWS, 256))
            placed = pltpu.roll(line, 129, axis=1, stride=1, stride_axis=0)[:, :ROWS]
            bias_ref[layer, head] = jnp.where(allowed, placed, masked_score)
        routes = routes_ref[layer].astype(f32)
        expert = [column_of(routes[k : k + 1, :], ROWS) for k in range(2)]
        hots = [(lane.astype(f32) == expert[k]).astype(f32) for k in range(2)]
        counts = dot(before, (hots[0] + hots[1]).astype(bf16))
        columns = []
        for k in range(2):
            slot = jnp.sum(counts * hots[k], axis=1, keepdims=True)
            first = slot < 7.5
            base = expert[k] * 8.0
            columns.append(jnp.where(first, base + slot, -1.0))
            columns.append(jnp.where(first, -1.0, base + (slot - 8.0) * 2.0))
            columns.append(jnp.where(first, -1.0, base + (slot - 8.0) * 2.0 + 1.0))
        columns.extend(expert)
        across = jnp.zeros((ROWS, ROWS), f32)
        down = jnp.zeros((8, ROWS), f32)
        for place, column in enumerate(columns):
            across = jnp.where(lane == place, column, across)
            down = jnp.where(iota((8, ROWS), 0) == place, row_of(column, ROWS), down)
        across_ref[layer] = across
        down_ref[layer] = down


def one_hot(flags):
    return flags.astype(f32).astype(bf16)


def dispatch(down, rows):
    place = iota((MAIN, ROWS), 0).astype(f32)
    tables = [one_hot(place == down[n : n + 1, :]) for n in range(6)]
    if len(rows) == 1:
        pairs = [([tables[n] + tables[n + 3] for n in range(3)], rows[0])]
    else:
        pairs = [(tables[:3], rows[0]), (tables[3:], rows[1])]
    main, rest = 0.0, 0.0
    for (whole, low, high), row in pairs:
        main = main + dot(whole, row)
        rest = rest + dot(low, row[:, :HALF]) + dot(high, row[:, HALF:])
    return main.astype(bf16), rest.astype(bf16)


def pick(across, route, main, rest):
    place = iota((ROWS, MAIN), 1).astype(f32)
    whole, low, high = [
        one_hot(place == across[:, 3 * route + n : 3 * route + n + 1]) for n in range(3)
    ]
    whole_part = dot(whole, main)
    return whole_part[:, :HALF] + dot(low, rest), whole_part[:, HALF:] + dot(high, rest)


def rest_tables():
    row = iota((REST, MAIN), 0)
    target = (row & 31) * 8 + (row >> 5) * 2
    lane = iota((REST, MAIN), 1)
    real = row < 96
    return one_hot((lane == target) & real), one_hot((lane == target + 1) & real)


def unpack(packed_ref, offset, into_ref):
    low, high = rest_tables()
    rest = packed_ref[:, offset + WIDTH : offset + SENT]
    into_ref[0:MAIN, :] = packed_ref[:, offset : offset + WIDTH]
    into_ref[MAIN : MAIN + REST, 0:HALF] = dot(low, rest).astype(bf16)
    into_ref[MAIN : MAIN + REST, HALF:WIDTH] = dot(high, rest).astype(bf16)


def pack(rows, offset, into_ref):
    low, high = rest_tables()
    into_ref[:, offset : offset + WIDTH] = rows[:MAIN]
    into_ref[:, offset + WIDTH : offset + SENT] = (
        dot(low, rows[MAIN:, :HALF], 0) + dot(high, rows[MAIN:, HALF:], 0)
    ).astype(bf16)


def attend(current, gain_ref, qkv_ref, bias_ref, low_ref, triple_ref, weights_ref):
    low = (current * scale_of(current) * gain_ref[0:1, :]).astype(bf16)
    low_ref[...] = low
    for k in range(3):
        triple_ref[k] = dot(low, qkv_ref[k], 1, 1).astype(bf16)
    mixture = jnp.zeros((ROWS, QUARTER), f32)
    go(low_ref, triple_ref)
    for head in range(HERE):
        mask = head_mask(head)
        scores = dot(triple_ref[0] * mask, triple_ref[1], 1, 1) * HEAD**-0.5 + bias_ref[head]
        scores = scores - jnp.max(scores, axis=-1, keepdims=True)
        raised = jnp.exp(scores)
        weights = raised / jnp.sum(raised, axis=-1, keepdims=True)
        weights_ref[head] = weights
        mixture = mixture + dot(weights.astype(bf16), triple_ref[2] * mask)
    go(weights_ref)
    return mixture.astype(bf16)


def attention_first(
    tokens_ref, gain_ref, qkv_ref, bias_ref, out_ref, low_ref, triple_ref, weights_ref, mixture_ref, part_ref
):
    mixture = attend(
        tokens_ref[...].astype(f32), gain_ref, qkv_ref, bias_ref, low_ref, triple_ref, weights_ref
    )
    mixture_ref[...] = mixture
    go(mixture_ref)
    part_ref[...] = dot(mixture, out_ref[...]).astype(bf16)


def attention_next(
    middle_ref,
    z0,
    z1,
    z2,
    z3,
    gain_ref,
    qkv_ref,
    bias_ref,
    out_ref,
    current_ref,
    low_ref,
    triple_ref,
    weights_ref,
    mixture_ref,
    part_ref,
):
    current = middle_ref[...] + four(z0[...], z1[...], z2[...], z3[...])
    current_ref[...] = current
    go(current_ref)
    mixture = attend(current, gain_ref, qkv_ref, bias_ref, low_ref, triple_ref, weights_ref)
    mixture_ref[...] = mixture
    go(mixture_ref)
    part_ref[...] = dot(mixture, out_ref[...]).astype(bf16)


def route_rows(middle, gain_ref, router_ref, across, low_ref, gates_ref):
    low = (middle * scale_of(middle) * gain_ref[1:2, :]).astype(bf16)
    low_ref[...] = low
    go(low_ref)
    logits = dot(low, router_ref[...], 1, 1)
    lane = iota((ROWS, EXPERTS), 1).astype(f32)
    chosen = [
        jnp.sum(jnp.where(lane == across[:, 6 + k : 7 + k], logits, 0.0), axis=1, keepdims=True)
        for k in range(2)
    ]
    top = jnp.maximum(chosen[0], chosen[1])
    raised = [jnp.exp(c - top) for c in chosen]
    total = raised[0] + raised[1]
    gates = [r / total for r in raised]
    place = iota((ROWS, ROWS), 1)
    gates_ref[...] = jnp.where(place == 0, gates[0], jnp.where(place == 1, gates[1], 0.0))
    return low, gates


def route_first(
    current_ref,
    p0,
    p1,
    p2,
    p3,
    gain_ref,
    router_ref,
    across_ref,
    down_ref,
    middle_ref,
    low_ref,
    gates_ref,
    send_ref,
):
    middle = current_ref[...].astype(f32) + four(p0[...], p1[...], p2[...], p3[...])
    middle_ref[...] = middle
    go(middle_ref)
    low, gates = route_rows(middle, gain_ref, router_ref, across_ref[...], low_ref, gates_ref)
    main, rest = dispatch(down_ref[...], [low])
    send_ref[:, :WIDTH] = main
    send_ref[:, WIDTH:] = rest


def route_next(
    current_ref,
    p0,
    p1,
    p2,
    p3,
    gain_ref,
    router_ref,
    across_ref,
    down_ref,
    cotangent_ref,
    middle_ref,
    low_ref,
    gates_ref,
    send_ref,
):
    middle = current_ref[...].astype(f32) + four(p0[...], p1[...], p2[...], p3[...])
    middle_ref[...] = middle
    go(middle_ref)
    low, gates = route_rows(middle, gain_ref, router_ref, across_ref[...], low_ref, gates_ref)
    main, rest = dispatch(down_ref[...], [low])
    send_ref[:, :WIDTH] = main
    send_ref[:, WIDTH:SENT] = rest
    gradient = cotangent_ref[...].astype(f32)
    main, rest = dispatch(down_ref[...], [(gate * gradient).astype(bf16) for gate in gates])
    send_ref[:, SENT : SENT + WIDTH] = main
    send_ref[:, SENT + WIDTH :] = rest


CURVE = (2.0 / 3.141592653589793) ** 0.5


def gelu_parts(values):
    squared = values * values
    bent = jnp.tanh(CURVE * values * (1.0 + 0.044715 * squared))
    return bent, squared


def gelu(values):
    bent, _ = gelu_parts(values)
    return 0.5 * values * (1.0 + bent)


def gelu_slope(values):
    bent, squared = gelu_parts(values)
    inner = CURVE * (1.0 + 3.0 * 0.044715 * squared)
    return 0.5 * (1.0 + bent) + 0.5 * values * (1.0 - bent * bent) * inner


def expert_forward(got_ref, in_ref, out_ref, rows_ref, slope_ref, active_ref, back_ref):
    unpack(got_ref, 0, rows_ref)
    go(rows_ref)
    before = dot(rows_ref[...], in_ref[...])
    slope_ref[...] = gelu_slope(before).astype(bf16)
    go(slope_ref)
    active = gelu(before).astype(bf16)
    active_ref[...] = active
    go(active_ref)
    pack(dot(active, out_ref[...]).astype(bf16), 0, back_ref)


def expert_backward(got_ref, out_ref, slope_ref, in_ref, grads_ref, down_ref, back_ref):
    unpack(got_ref, 0, grads_ref)
    go(grads_ref)
    grad_active = dot(grads_ref[...], out_ref[...], 1, 1)
    grad_before = (grad_active * slope_ref[...].astype(f32)).astype(bf16)
    down_ref[...] = grad_before
    go(down_ref)
    pack(dot(grad_before, in_ref[...], 1, 1).astype(bf16), 0, back_ref)


def expert_both(got_ref, in_ref, out_ref, rows_ref, active_ref, grads_ref, down_ref, back_ref):
    unpack(got_ref, 0, rows_ref)
    unpack(got_ref, SENT, grads_ref)
    go(rows_ref, grads_ref)
    before = dot(rows_ref[...], in_ref[...])
    active = gelu(before).astype(bf16)
    active_ref[...] = active
    go(active_ref)
    pack(dot(active, out_ref[...]).astype(bf16), 0, back_ref)
    grad_active = dot(grads_ref[...], out_ref[...], 1, 1)
    grad_before = (grad_active * gelu_slope(before)).astype(bf16)
    down_ref[...] = grad_before
    go(down_ref)
    pack(dot(grad_before, in_ref[...], 1, 1).astype(bf16), SENT, back_ref)


def expert_grads_top(rows_ref, active_ref, grads_ref, down_ref, in_grad_ref, out_grad_ref):
    in_grad_ref[0, 0] = dot(rows_ref[...], down_ref[...], 0)
    out_grad_ref[0, 0] = dot(active_ref[...], grads_ref[...], 0)


def expert_grads_low(rows_ref, active_ref, grads_ref, down_ref, _, __, in_grad_ref, out_grad_ref):
    expert_grads_top(rows_ref, active_ref, grads_ref, down_ref, in_grad_ref, out_grad_ref)


def combine_first(got_ref, across_ref, gates_ref, part_ref, picked_ref):
    main, rest = got_ref[:, :WIDTH], got_ref[:, WIDTH:]
    across, gates = across_ref[...], gates_ref[...]
    left, right = 0.0, 0.0
    for route in range(2):
        one, two = pick(across, route, main, rest)
        picked_ref[route, :, :HALF] = one.astype(bf16)
        picked_ref[route, :, HALF:] = two.astype(bf16)
        left = left + gates[:, route : route + 1] * one
        right = right + gates[:, route : route + 1] * two
    part_ref[:, :HALF] = left.astype(bf16)
    part_ref[:, HALF:] = right.astype(bf16)


def gate_rows(grads):
    place = iota((8, ROWS), 0)
    rows = [row_of(grad, ROWS) for grad in grads]
    both = jnp.where(place == 0, rows[0], jnp.where(place == 1, rows[1], 0.0))
    moved = jnp.where(place == 2, rows[0], jnp.where(place == 3, rows[1], 0.0))
    left = moved - moved.astype(bf16).astype(f32)
    return (both + left).astype(bf16)


def gathered_back(got_ref, offset, across, rows, into_ref):
    main = got_ref[:, offset : offset + WIDTH]
    rest = got_ref[:, offset + WIDTH : offset + SENT]
    left, right = pick(across, 0, main, rest)
    other_left, other_right = pick(across, 1, main, rest)
    into_ref[:ROWS, :HALF] = (left + other_left).astype(bf16)
    into_ref[:ROWS, HALF:] = (right + other_right).astype(bf16)
    into_ref[ROWS:, :ROWS] = rows
    into_ref[ROWS:, ROWS:] = jnp.zeros((8, WIDTH - ROWS), bf16)


def combine_next(got_ref, across_ref, gates_ref, cotangent_ref, part_ref, back_ref):
    main, rest = got_ref[:, :WIDTH], got_ref[:, WIDTH:SENT]
    across, gates = across_ref[...], gates_ref[...]
    gradient = cotangent_ref[...].astype(f32)
    left, right, grads = 0.0, 0.0, []
    for route in range(2):
        one, two = pick(across, route, main, rest)
        left = left + gates[:, route : route + 1] * one
        right = right + gates[:, route : route + 1] * two
        grads.append(
            jnp.sum(gradient[:, :HALF] * one + gradient[:, HALF:] * two, axis=1, keepdims=True)
        )
    part_ref[:, :HALF] = left.astype(bf16)
    part_ref[:, HALF:] = right.astype(bf16)
    gathered_back(got_ref, SENT, across, gate_rows(grads), back_ref)


def combine_back(got_ref, across_ref, rows_ref, back_ref):
    gathered_back(got_ref, 0, across_ref[...], rows_ref[...], back_ref)


def attention_back(
    e0,
    e1,
    e2,
    e3,
    gates_ref,
    across_ref,
    router_ref,
    middle_ref,
    gain_ref,
    gradient_ref,
    out_ref,
    triple_ref,
    weights_ref,
    qkv_ref,
    hot_ref,
    after_ref,
    low_ref,
    back_triple_ref,
    part_ref,
    logits_ref,
    gain_grad_ref,
    table_grad_ref,
):
    total = four(e0[...], e1[...], e2[...], e3[...])
    gates = gates_ref[...]
    across = across_ref[...]
    gate = [gates[:, k : k + 1] for k in range(2)]
    rows = total[ROWS:, :ROWS]
    grad_gate = [column_of(rows[k : k + 1] + rows[k + 2 : k + 3], ROWS) for k in range(2)]
    mean = gate[0] * grad_gate[0] + gate[1] * grad_gate[1]
    lane = iota((ROWS, EXPERTS), 1).astype(f32)
    grad_logits = 0.0
    for k in range(2):
        grad_logits = grad_logits + jnp.where(
            lane == across[:, 6 + k : 7 + k], gate[k] * (grad_gate[k] - mean), 0.0
        )
    high = grad_logits.astype(bf16)
    low = (grad_logits - high.astype(f32)).astype(bf16)
    logits_ref[:, :EXPERTS] = high
    logits_ref[:, EXPERTS : 2 * EXPERTS] = low
    logits_ref[:, 2 * EXPERTS :] = jnp.zeros((ROWS, 128 - 2 * EXPERTS), bf16)
    grad_low = total[:ROWS] + dot(high, router_ref[...]) + dot(low, router_ref[...])
    grad_middle, gain_grad_ref[...] = norm_back(middle_ref[...], gain_ref[1:2, :], grad_low)
    after = gradient_ref[...].astype(f32) + grad_middle
    after_ref[...] = after
    low_after = after.astype(bf16)
    low_ref[...] = low_after
    go(after_ref, low_ref, logits_ref, gain_grad_ref)
    grad_mixture = dot(low_after, out_ref[...], 1, 1).astype(bf16)
    queries, keys, values = triple_ref[0], triple_ref[1], triple_ref[2]
    grad_queries = jnp.zeros((ROWS, QUARTER), f32)
    grad_keys, grad_values = grad_queries, grad_queries
    diagonals = jnp.zeros((8, 256), f32)
    flip = one_hot(iota((ROWS, ROWS), 0) + iota((ROWS, ROWS), 1) == ROWS - 1)
    for head in range(HERE):
        mask = head_mask(head)
        masked_grad = grad_mixture * mask
        weights = weights_ref[head]
        grad_values = grad_values + dot(weights.astype(bf16), masked_grad, 0)
        grad_weights = dot(masked_grad, values, 1, 1)
        grad_scores = weights * (
            grad_weights - jnp.sum(weights * grad_weights, axis=-1, keepdims=True)
        )
        grad_scores = grad_scores.astype(bf16)
        grad_queries = grad_queries + dot(grad_scores, keys * mask)
        grad_keys = grad_keys + dot(grad_scores, queries * mask, 0)
        wide = jnp.concatenate([dot(flip, grad_scores), jnp.zeros((ROWS, 128), f32)], axis=1)
        turned = pltpu.roll(wide, 0, axis=1, stride=1, stride_axis=0)
        diagonals = jnp.where(
            iota((8, 256), 0) == head, jnp.sum(turned, axis=0, keepdims=True), diagonals
        )
    table_grad_ref[...] = dot(diagonals, hot_ref[...], 1, 1, precision=highest)
    grad_input = 0.0
    for k, grad in enumerate((grad_queries * HEAD**-0.5, grad_keys * HEAD**-0.5, grad_values)):
        grad = grad.astype(bf16)
        back_triple_ref[:, k * QUARTER : (k + 1) * QUARTER] = grad
        grad_input = grad_input + dot(grad, qkv_ref[k])
    go(back_triple_ref)
    part_ref[...] = grad_input.astype(bf16)


SHARE = WIDTH // EXPERTS
GROUPS = WIDTH // 128


def router_places():
    row, column = iota((WIDTH, GROUPS * EXPERTS), 0), iota((WIDTH, GROUPS * EXPERTS), 1)
    return one_hot(row == (column & (EXPERTS - 1)) * SHARE + (column >> 5))


def folded(line):
    place = iota((8, 128), 0)
    rows = jnp.zeros((8, 128), f32)
    for part in range(GROUPS):
        rows = jnp.where(place == part, line[:, part * 128 : (part + 1) * 128], rows)
    return rows


def unfolded(rows):
    return jnp.concatenate([rows[part : part + 1, :] for part in range(GROUPS)], axis=1)


def fill_grads(low, back_triple, mixture, after, low_two, logits, gains, table, grads_ref):
    kind = grads_ref.dtype
    qkv_rows = 3 * QUARTER
    grads_ref[:qkv_rows, :WIDTH] = dot(back_triple, low, 0).astype(kind)
    grads_ref[qkv_rows:, :WIDTH] = dot(mixture, after, 0).astype(kind)
    both = dot(logits, low_two, 0)
    total = both[:EXPERTS] + both[EXPERTS : 2 * EXPERTS]
    parts = jnp.concatenate([total[:, r * 128 : (r + 1) * 128] for r in range(GROUPS)], axis=0)
    places = router_places()
    high = parts.astype(bf16)
    rest = (parts - high.astype(f32)).astype(bf16)
    grads_ref[:, WIDTH:] = (dot(places, high) + dot(places, rest)).astype(kind)
    for chunk, gain in enumerate(gains):
        start = chunk * SHARE + 8
        grads_ref[start : start + 8, WIDTH:] = folded(gain).astype(kind)
    start = 2 * SHARE + 8
    grads_ref[start : start + 8, WIDTH : WIDTH + EXPERTS] = table.astype(kind)


def weight_grads(
    low_ref, back_triple_ref, mixture_ref, after_ref, low_two_ref, logits_ref, gain, table, grads_ref
):
    operands = (low_ref, back_triple_ref, mixture_ref, after_ref, low_two_ref, logits_ref)
    fill_grads(*[ref[...] for ref in operands], [gain[...]], table[...], grads_ref)


def attention_back_low(*refs):
    operands, (low_ref, mixture_ref, low_two_ref, gain10_ref) = refs[:15], refs[15:19]
    after_ref, part_ref, grads_ref, held_low, held_triple, held_logits, held_gain, held_table = refs[19:]
    attention_back(
        *operands,
        after_ref,
        held_low,
        held_triple,
        part_ref,
        held_logits,
        held_gain,
        held_table,
    )
    operands = (low_ref, held_triple, mixture_ref, held_low, low_two_ref, held_logits)
    fill_grads(
        *[ref[...] for ref in operands],
        [held_gain[...], gain10_ref[...]],
        held_table[...],
        grads_ref,
    )


def start_back(
    after_ref,
    d0,
    d1,
    d2,
    d3,
    input_ref,
    gain_ref,
    gates_ref,
    down_ref,
    picked_ref,
    gradient_ref,
    gain_grad_ref,
    rows_ref,
    send_ref,
):
    grad_low = four(d0[...], d1[...], d2[...], d3[...])
    grad_input, gain_grad_ref[...] = norm_back(input_ref[...].astype(f32), gain_ref[0:1, :], grad_low)
    gradient = after_ref[...] + grad_input
    gradient_ref[...] = gradient
    go(gradient_ref, gain_grad_ref)
    gates = gates_ref[...]
    weighted = [(gates[:, k : k + 1] * gradient).astype(bf16) for k in range(2)]
    main, rest = dispatch(down_ref[...], weighted)
    send_ref[:, :WIDTH] = main
    send_ref[:, WIDTH:] = rest
    rows_ref[...] = gate_rows(
        [jnp.sum(gradient * picked_ref[k].astype(f32), axis=1, keepdims=True) for k in range(2)]
    )


def finish_back(after_ref, d0, d1, d2, d3, input_ref, gain_ref, gradient_ref, gain_grad_ref):
    grad_low = four(d0[...], d1[...], d2[...], d3[...])
    grad_input, gain_grad_ref[...] = norm_back(input_ref[...].astype(f32), gain_ref[0:1, :], grad_low)
    gradient_ref[...] = after_ref[...] + grad_input


def finish_output(middle_ref, z0, z1, z2, z3, output_ref):
    output_ref[...] = (middle_ref[...] + four(z0[...], z1[...], z2[...], z3[...])).astype(bf16)


def add_chunks(chunks_ref, gain00_ref, spread_ref):
    total = chunks_ref[0:SHARE, :].astype(f32)
    for block in range(1, EXPERTS):
        total = total + chunks_ref[block * SHARE : (block + 1) * SHARE, :].astype(f32)
    total = total.astype(bf16)
    gain = folded(gain00_ref[...]).astype(bf16)
    for block in range(EXPERTS):
        start = block * SHARE
        spread_ref[start : start + SHARE, :] = total
        spread_ref[start + 16 : start + SHARE, WIDTH:] = gain


def router_rows(small):
    places = router_places()
    high = small.astype(bf16)
    parts = dot(places, high, 0) + dot(places, (small - high.astype(f32)).astype(bf16), 0)
    return jnp.concatenate(
        [parts[r * EXPERTS : (r + 1) * EXPERTS] for r in range(GROUPS)], axis=1
    )


def place_top(
    grads_ref, qkv_ref, out_ref, router_ref, gain_ref, table_ref, wide, small, rows, done
):
    fetch = pltpu.make_async_copy(grads_ref.at[:, WIDTH:], small, done.at[0])
    fetch.start()
    arriving, leaving = [], []
    for k in range(4):
        source = grads_ref.at[k * QUARTER : (k + 1) * QUARTER, :WIDTH]
        target = qkv_ref.at[1, k] if k < 3 else out_ref.at[1]
        arriving.append(pltpu.make_async_copy(source, wide.at[k], done.at[1 + k]))
        leaving.append(pltpu.make_async_copy(wide.at[k], target, done.at[5 + k]))
        arriving[-1].start()
    fetch.wait()
    lanes = small[...]
    rows[...] = router_rows(lanes)
    leaving.append(pltpu.make_async_copy(rows, router_ref.at[1], done.at[9]))
    leaving[-1].start()
    gain_ref[...] = unfolded(lanes[8:16])
    table_ref[...] = lanes[2 * SHARE + 8 : 2 * SHARE + 16]
    for k in range(4):
        arriving[k].wait()
        leaving[k].start()
    for copy in leaving:
        copy.wait()


def place_low(
    grads_ref,
    gain_ref,
    table_ref,
    _,
    __,
    ___,
    qkv_ref,
    out_ref,
    router_ref,
    gains_ref,
    tables_ref,
    wide,
    rows,
    done,
):
    copies = []
    for k in range(4):
        wide[k] = grads_ref[k * QUARTER : (k + 1) * QUARTER, :WIDTH].astype(f32)
        target = qkv_ref.at[0, k] if k < 3 else out_ref.at[0]
        copies.append(pltpu.make_async_copy(wide.at[k], target, done.at[k]))
        copies[-1].start()
    small = grads_ref[:, WIDTH:].astype(f32)
    rows[...] = router_rows(small)
    copies.append(pltpu.make_async_copy(rows, router_ref.at[0], done.at[4]))
    copies[-1].start()
    first = small[16:SHARE]
    for block in range(1, EXPERTS):
        first = first + small[block * SHARE + 16 : (block + 1) * SHARE]
    gains_ref[0, 0:1, :] = unfolded(first)
    gains_ref[0, 1:2, :] = unfolded(small[8:16])
    gains_ref[1, 0:1, :] = unfolded(small[SHARE + 8 : SHARE + 16])
    gains_ref[1, 1:2, :] = gain_ref[...]
    table = small[2 * SHARE + 8 : 2 * SHARE + 16]
    for head in range(HERE):
        tables_ref[head, 0:1, :] = table[head : head + 1, :EXPERTS]
        tables_ref[head, 1:2, :] = table_ref[head : head + 1, :EXPERTS]
    for copy in copies:
        copy.wait()


def place(top_grads, low_grads):
    stacks = [
        pltpu.HBM((2, 3, QUARTER, WIDTH), f32),
        pltpu.HBM((2, QUARTER, WIDTH), f32),
        pltpu.HBM((2, EXPERTS, WIDTH), f32),
    ]
    hbm, vmem = pl.BlockSpec(memory_space=pltpu.HBM), pl.BlockSpec(memory_space=pltpu.VMEM)
    params = pltpu.CompilerParams(vmem_limit_bytes=16 * 1024 * 1024)
    *stacked, gain, table = pl.pallas_call(
        place_top,
        out_shape=[
            *stacks,
            jax.ShapeDtypeStruct((1, WIDTH), f32),
            jax.ShapeDtypeStruct((8, 128), f32),
        ],
        in_specs=[hbm],
        out_specs=[hbm] * 3 + [vmem] * 2,
        scratch_shapes=[
            pltpu.VMEM((4, QUARTER, WIDTH), f32),
            pltpu.VMEM((WIDTH, 128), f32),
            pltpu.VMEM((EXPERTS, WIDTH), f32),
            pltpu.SemaphoreType.DMA((10,)),
        ],
        compiler_params=params,
        name="place_top",
    )(in_hbm(top_grads))
    return pl.pallas_call(
        place_low,
        out_shape=[
            *stacks,
            jax.ShapeDtypeStruct((2, 2, WIDTH), f32),
            jax.ShapeDtypeStruct((HERE, 2, EXPERTS), f32),
        ],
        in_specs=[vmem] * 3 + [hbm] * 3,
        out_specs=[hbm] * 3 + [vmem] * 2,
        scratch_shapes=[
            pltpu.VMEM((4, QUARTER, WIDTH), f32),
            pltpu.VMEM((EXPERTS, WIDTH), f32),
            pltpu.SemaphoreType.DMA((5,)),
        ],
        input_output_aliases={3: 0, 4: 1, 5: 2},
        compiler_params=params,
        name="place_low",
    )(low_grads, gain, table, *[in_hbm(s) for s in stacked])


def around(values):
    sent = [
        lax.ppermute(values, "tensor", [(i, (i + shift) % 4) for i in range(4)]) for shift in (1, 2, 3)
    ]
    return [values, *sent]


def across_experts(values):
    return lax.all_to_all(values, "expert", 0, 0, tiled=True)


def shards(
    tokens,
    segment_ids,
    expert_routes,
    bucket_ids,
    proj_qkv,
    proj_out,
    bias_table,
    norm_gains,
    router,
    expert_in,
    expert_out,
    cotangent,
):
    qkv = proj_qkv.transpose(0, 1, 3, 2)
    router = router.transpose(0, 2, 1)
    expert_in, expert_out = expert_in[:, 0], expert_out[:, 0]
    gains = norm_gains
    row = (ROWS, WIDTH)
    narrow = (ROWS, QUARTER)
    scores = (HERE, ROWS, ROWS)
    slots = (MAIN + REST, WIDTH)
    stacked = (2, 1, WIDTH, WIDTH)
    bias, across, down, hot = call(
        setup,
        [
            ((2, HERE, ROWS, ROWS), f32),
            ((2, ROWS, ROWS), f32),
            ((2, 8, ROWS), f32),
            ((EXPERTS, 256), f32),
        ],
        Late(bucket_ids.reshape(1, -1)),
        Late(bias_table.transpose(2, 0, 1)),
        Late(segment_ids),
        Late(expert_routes.transpose(0, 2, 1)),
    )
    kept = [
        Kept(row, bf16),
        Kept((3, *narrow), bf16),
        Kept(scores, f32),
        Kept(narrow, bf16),
        (row, bf16),
    ]

    low_a0, triple0, weights0, mixture0, part = call(
        attention_first,
        kept,
        Late(tokens),
        Late(Layer(gains, 0)),
        Late(Layer(qkv, 0)),
        Layer(bias, 0),
        Late(Layer(proj_out, 0)),
    )
    middle0, low_b0, gates0, send = call(
        route_first,
        [Kept(row, f32), Kept(row, bf16), ((ROWS, ROWS), f32), ((MAIN, SENT), bf16)],
        tokens,
        *around(part),
        Layer(gains, 0),
        Late(Layer(router, 0)),
        Layer(across, 0),
        Layer(down, 0),
    )
    rows0, slope0, active0, send = call(
        expert_forward,
        [Kept(slots, bf16), Kept(slots, bf16), Kept(slots, bf16), ((MAIN, SENT), bf16)],
        across_experts(send),
        Layer(expert_in, 0),
        Layer(expert_out, 0),
    )
    part, picked0 = call(
        combine_first,
        [(row, bf16), Kept((2, *row), bf16)],
        across_experts(send),
        Layer(across, 0),
        gates0,
    )

    current1, low_a1, triple1, weights1, mixture1, part = call(
        attention_next,
        [Kept(row, f32), *kept],
        Late(middle0),
        *around(part),
        Layer(gains, 1),
        Late(Layer(qkv, 1)),
        Late(Layer(bias, 1)),
        Late(Layer(proj_out, 1)),
    )
    middle1, low_b1, gates1, send = call(
        route_next,
        [Kept(row, f32), Kept(row, bf16), ((ROWS, ROWS), f32), ((MAIN, 2 * SENT), bf16)],
        Late(current1),
        *around(part),
        Layer(gains, 1),
        Late(Layer(router, 1)),
        Layer(across, 1),
        Layer(down, 1),
        cotangent,
    )
    rows1, active1, grads1, down1, send = call(
        expert_both,
        [*[Kept(slots, bf16)] * 4, ((MAIN, 2 * SENT), bf16)],
        across_experts(send),
        Layer(expert_in, 1),
        Layer(expert_out, 1),
    )
    got = across_experts(send)
    in_grads, out_grads = call_stacked(
        expert_grads_top, 1, (rows1, active1, grads1, down1), stacked
    )
    moved, back = call(
        combine_next,
        [(row, bf16), ((LONG, WIDTH), bf16)],
        got,
        Layer(across, 1),
        gates1,
        cotangent,
    )

    back_kept = [
        Kept(row, f32),
        Kept(row, bf16),
        Kept((ROWS, 3 * QUARTER), bf16),
        (row, bf16),
        Kept((ROWS, 128), bf16),
        Kept((1, WIDTH), f32),
        Kept((8, EXPERTS), f32),
    ]
    after1, low_after1, back_triple1, part, logits1, gain11, table1 = call(
        attention_back,
        back_kept,
        *around(back),
        gates1,
        Layer(across, 1),
        Late(Layer(router, 1)),
        middle1,
        Layer(gains, 1),
        cotangent,
        Late(Layer(proj_out, 1)),
        triple1,
        weights1,
        Late(Layer(qkv, 1)),
        hot,
    )
    parts = around(part)
    (top_grads,) = call(
        weight_grads,
        [Kept((WIDTH, SUMMED), f32)],
        Late(low_a1),
        Late(back_triple1),
        Late(mixture1),
        Late(low_after1),
        Late(low_b1),
        Late(logits1),
        Late(gain11),
        Late(table1),
    )
    top_grads = lax.psum(top_grads, "expert")
    parts, in_grads = lax.optimization_barrier((parts, in_grads))

    def low_layer(_, carried):
        in_grads, out_grads, after, _ = carried
        gradient0, gain10, rows0b, send = call(
            start_back,
            [Kept(row, f32), Kept((1, WIDTH), f32), ((8, ROWS), bf16), ((MAIN, SENT), bf16)],
            Late(after),
            *parts,
            Late(current1),
            Late(Layer(gains, 1)),
            gates0,
            Layer(down, 0),
            Late(picked0),
        )
        grads0, down0, send = call(
            expert_backward,
            [Kept(slots, bf16), Kept(slots, bf16), ((MAIN, SENT), bf16)],
            across_experts(send),
            Late(Layer(expert_out, 0)),
            Late(slope0),
            Late(Layer(expert_in, 0)),
        )
        got = across_experts(send)
        in_grads, out_grads = call_stacked(
            expert_grads_low, 0, (rows0, active0, grads0, down0), stacked, (in_grads, out_grads)
        )
        (back,) = call(combine_back, [((LONG, WIDTH), bf16)], got, Layer(across, 0), rows0b)
        backs = around(back)
        backs, in_grads = lax.optimization_barrier((backs, in_grads))
        after0, part, grads = call(
            attention_back_low,
            [Kept(row, f32), (row, bf16), Kept((WIDTH, SUMMED), bf16)],
            *backs,
            gates0,
            Layer(across, 0),
            Layer(router, 0),
            Late(middle0),
            Layer(gains, 0),
            Late(gradient0),
            Layer(proj_out, 0),
            Late(triple0),
            Late(weights0),
            Layer(qkv, 0),
            Late(hot),
            Late(low_a0),
            Late(mixture0),
            Late(low_b0),
            Late(gain10),
            held=[
                (row, bf16),
                ((ROWS, 3 * QUARTER), bf16),
                ((ROWS, 128), bf16),
                ((1, WIDTH), f32),
                ((8, EXPERTS), f32),
            ],
        )
        low_parts = around(part)
        tokens_grad, gain00 = call(
            finish_back,
            [Kept(row, f32), Kept((1, WIDTH), f32)],
            after0,
            *low_parts,
            tokens,
            Layer(gains, 0),
        )
        (spread,) = call(
            add_chunks,
            [Kept((WIDTH, SUMMED), bf16)],
            across_experts(grads),
            Late(gain00),
        )
        return in_grads, out_grads, tokens_grad, spread

    once = jnp.minimum(jnp.maximum(bucket_ids[0], 0) + 1, 1)
    in_grads, out_grads, tokens_grad, spread = lax.fori_loop(
        0,
        once,
        low_layer,
        (
            in_grads,
            out_grads,
            after1,
            jnp.zeros((WIDTH, SUMMED), bf16),
        ),
    )
    low_grads = across_experts(spread)
    (output,) = call(finish_output, [Kept(row, bf16)], middle1, *around(moved))
    qkv_grad, out_grad, router_grad, gain_grads, table_grad = place(top_grads, low_grads)
    return (
        output,
        tokens_grad,
        qkv_grad.transpose(0, 1, 3, 2),
        out_grad,
        table_grad.transpose(1, 2, 0),
        gain_grads,
        router_grad.transpose(0, 2, 1),
        in_grads,
        out_grads,
    )


def solution(mesh):
    placed = (
        P("expert", None),
        P("expert", None),
        P(None, "expert", None),
        P(),
        P(None, None, None, "tensor"),
        P(None, "tensor", None),
        P(None, None, "tensor"),
        P(),
        P(),
        P(None, "expert", None, "tensor"),
        P(None, "expert", "tensor", None),
        P("expert", None),
    )
    return jax.shard_map(
        shards,
        mesh=mesh,
        in_specs=placed,
        out_specs=(
            P("expert", None),
            P("expert", None),
            P(None, None, None, "tensor"),
            P(None, "tensor", None),
            P(None, None, "tensor"),
            P(),
            P(),
            P(None, "expert", None, "tensor"),
            P(None, "expert", "tensor", None),
        ),
        check_vma=False,
    )
```

```python
import jax
import jax.numpy as jnp
from jax import lax
from jax.experimental import pallas as pl
from jax.experimental.pallas import tpu as pltpu
from jax.sharding import PartitionSpec as P

epsilon = 1e-06
masked_score = -1000000000.0
highest = lax.Precision.HIGHEST
f32, bf16 = jnp.float32, jnp.bfloat16

ROWS = 128
WIDTH = 768
QUARTER = 192
HERE = 3
HEAD = 64
EXPERTS = 32
MAIN = EXPERTS * 8
REST = 128
HALF = WIDTH // 2
SENT = WIDTH + HALF
SUMMED = WIDTH + 128
LONG = ROWS + 8


class Layer:
    def __init__(self, array, layer):
        self.array, self.layer = array, layer


class Late:
    def __init__(self, operand):
        self.operand = operand


class Kept:
    def __init__(self, shape, dtype):
        self.shape, self.dtype = shape, dtype


class Arriving:
    def __init__(self, source, held, done):
        self.held, self.copy, self.here = held, pltpu.make_async_copy(source, held, done), False
        self.copy.start()

    @property
    def shape(self):
        return self.held.shape

    def __getitem__(self, index):
        self.wait()
        return self.held[index]

    def wait(self):
        if not self.here:
            self.copy.wait()
            self.here = True


class Leaving:
    def __init__(self, held, target, done, first, parts):
        self.held, self.gone = held, [False] * len(parts)
        self.copies = [
            pltpu.make_async_copy(held.at[a:b], target.at[a:b], done.at[first + n])
            if len(parts) > 1
            else pltpu.make_async_copy(held, target, done.at[first])
            for n, (a, b) in enumerate(parts)
        ]

    @property
    def dtype(self):
        return self.held.dtype

    def __getitem__(self, index):
        return self.held[index]

    def __setitem__(self, index, value):
        self.held[index] = value

    def go(self, part=None):
        for n, copy in enumerate(self.copies):
            if part in (None, n) and not self.gone[n]:
                copy.start()
                self.gone[n] = True


def go(*refs):
    for ref in refs:
        if isinstance(ref, Leaving):
            ref.go()


def in_hbm(array):
    return pltpu.with_memory_space_constraint(array, pltpu.HBM)


def call(body, outs, *operands, held=(), limit=16):
    late = [isinstance(o, Late) for o in operands]
    inner = [o.operand if isinstance(o, Late) else o for o in operands]
    arrays = [o.array if isinstance(o, Layer) else o for o in inner]
    parts = [a.shape[1:] if isinstance(o, Layer) else a.shape for o, a in zip(inner, arrays)]
    arrays = [in_hbm(a) if is_late else a for a, is_late in zip(arrays, late)]
    kept = [isinstance(o, Kept) for o in outs]
    shapes = [(o.shape, o.dtype) if isinstance(o, Kept) else o for o in outs]
    scratch = [pltpu.VMEM(p, a.dtype) for p, a, is_late in zip(parts, arrays, late) if is_late]
    scratch += [pltpu.VMEM(*o) for o, is_kept in zip(shapes, kept) if is_kept]
    payload = (WIDTH, SUMMED)
    cuts = [((0, 384), (384, 576), (576, 768)) if o[0] == payload else ((0, 0),) for o in shapes]
    copies = sum(late) + sum(len(c) for c, is_kept in zip(cuts, kept) if is_kept)
    scratch += [pltpu.VMEM(*h) for h in held]
    if copies:
        scratch.append(pltpu.SemaphoreType.DMA((copies,)))

    def kernel(*refs):
        count = len(operands) + len(outs)
        spare = list(refs[count:])
        done = spare.pop() if copies else None
        given, used = [], 0
        for ref, operand, is_late in zip(refs, inner, late):
            view = ref.at[operand.layer] if isinstance(operand, Layer) else ref
            if is_late:
                view = Arriving(view, spare[used], done.at[used])
                used += 1
            given.append(view)
        taken, leaving = [], []
        place = used
        for ref, is_kept, parts_here in zip(refs[len(operands) : count], kept, cuts):
            if is_kept:
                ref = Leaving(spare[used], ref, done, place, parts_here)
                leaving.append(ref)
                used += 1
                place += len(parts_here)
            taken.append(ref)
        body(*given, *taken, *spare[used:])
        go(*leaving)
        for ref in leaving:
            for copy in ref.copies:
                copy.wait()
        for view in given:
            if isinstance(view, Arriving):
                view.wait()

    return pl.pallas_call(
        kernel,
        out_shape=[
            pltpu.HBM(*o) if is_kept else jax.ShapeDtypeStruct(*o) for o, is_kept in zip(shapes, kept)
        ],
        in_specs=[pl.BlockSpec(memory_space=pltpu.HBM if n else pltpu.VMEM) for n in late],
        out_specs=[pl.BlockSpec(memory_space=pltpu.HBM if n else pltpu.VMEM) for n in kept],
        scratch_shapes=scratch,
        compiler_params=pltpu.CompilerParams(vmem_limit_bytes=limit * 1024 * 1024),
        name=body.__name__,
    )(*arrays)


def call_stacked(body, layer, operands, stacked, earlier=()):
    whole = [pl.BlockSpec(o.shape, lambda _, n=o.ndim: (0,) * n) for o in operands]
    part = pl.BlockSpec((1, 1, *stacked[2:]), lambda _: (layer, 0, 0, 0))
    return pl.pallas_call(
        body,
        grid=(1,),
        out_shape=[pltpu.HBM(stacked, f32)] * 2,
        in_specs=whole + [pl.BlockSpec(memory_space=pltpu.HBM)] * len(earlier),
        out_specs=[part] * 2,
        input_output_aliases={len(operands) + n: n for n in range(len(earlier))},
        compiler_params=pltpu.CompilerParams(vmem_limit_bytes=24 * 1024 * 1024),
        name=body.__name__,
    )(*[in_hbm(o) for o in (*operands, *earlier)])


def dot(left, right, left_axis=1, right_axis=0, precision=None):
    return lax.dot_general(
        left,
        right,
        (((left_axis,), (right_axis,)), ((), ())),
        precision=precision,
        preferred_element_type=f32,
    )


def iota(shape, axis):
    return lax.broadcasted_iota(jnp.int32, shape, axis)


def scale_of(values):
    return lax.rsqrt(jnp.mean(values * values, axis=-1, keepdims=True) + epsilon)


def norm_back(values, gain, upstream):
    inverse = scale_of(values)
    inner = upstream * gain
    mean = jnp.mean(inner * values, axis=-1, keepdims=True)
    back = inverse * inner - values * (inverse * inverse * inverse * mean)
    return back, jnp.sum(upstream * (values * inverse), axis=0, keepdims=True)


def head_mask(head):
    lane = iota((1, QUARTER), 1)
    return ((lane >= head * HEAD) & (lane < (head + 1) * HEAD)).astype(f32).astype(bf16)


def four(own, one, two, three):
    return (own.astype(f32) + two.astype(f32)) + (one.astype(f32) + three.astype(f32))


def column_of(row, size):
    same = iota((size, size), 0) == iota((size, size), 1)
    return jnp.sum(jnp.where(same, jnp.broadcast_to(row, (size, size)), 0.0), axis=1, keepdims=True)


def row_of(column, size):
    same = iota((size, size), 0) == iota((size, size), 1)
    return jnp.sum(jnp.where(same, jnp.broadcast_to(column, (size, size)), 0.0), axis=0, keepdims=True)


def setup(ids_ref, table_ref, segment_ref, routes_ref, bias_ref, across_ref, down_ref, hot_ref):
    offsets = ids_ref.shape[1]
    hot = one_hot(iota((EXPERTS, offsets), 0) == ids_ref[...])
    mirror = one_hot(iota((offsets, 256), 0) + iota((offsets, 256), 1) == offsets - 1)
    hot = dot(hot, mirror)
    hot_ref[...] = hot
    tables = table_ref[...]
    segment = segment_ref[...].astype(f32)
    allowed = (column_of(segment, ROWS) == segment) & (iota((ROWS, ROWS), 1) <= iota((ROWS, ROWS), 0))
    lane = iota((ROWS, ROWS), 1)
    before = one_hot(lane < iota((ROWS, ROWS), 0))
    for layer in range(2):
        by_offset = dot(tables[:, layer, :], hot, precision=highest)
        for head in range(HERE):
            line = jnp.broadcast_to(by_offset[head : head + 1, :], (ROWS, 256))
            placed = pltpu.roll(line, 129, axis=1, stride=1, stride_axis=0)[:, :ROWS]
            bias_ref[layer, head] = jnp.where(allowed, placed, masked_score)
        routes = routes_ref[layer].astype(f32)
        expert = [column_of(routes[k : k + 1, :], ROWS) for k in range(2)]
        hots = [(lane.astype(f32) == expert[k]).astype(f32) for k in range(2)]
        counts = dot(before, (hots[0] + hots[1]).astype(bf16))
        columns = []
        for k in range(2):
            slot = jnp.sum(counts * hots[k], axis=1, keepdims=True)
            first = slot < 7.5
            base = expert[k] * 8.0
            columns.append(jnp.where(first, base + slot, -1.0))
            columns.append(jnp.where(first, -1.0, base + (slot - 8.0) * 2.0))
            columns.append(jnp.where(first, -1.0, base + (slot - 8.0) * 2.0 + 1.0))
        columns.extend(expert)
        across = jnp.zeros((ROWS, ROWS), f32)
        down = jnp.zeros((8, ROWS), f32)
        for place, column in enumerate(columns):
            across = jnp.where(lane == place, column, across)
            down = jnp.where(iota((8, ROWS), 0) == place, row_of(column, ROWS), down)
        across_ref[layer] = across
        down_ref[layer] = down


def one_hot(flags):
    return flags.astype(f32).astype(bf16)


def dispatch(down, rows):
    place = iota((MAIN, ROWS), 0).astype(f32)
    tables = [one_hot(place == down[n : n + 1, :]) for n in range(6)]
    if len(rows) == 1:
        pairs = [([tables[n] + tables[n + 3] for n in range(3)], rows[0])]
    else:
        pairs = [(tables[:3], rows[0]), (tables[3:], rows[1])]
    main, rest = 0.0, 0.0
    for (whole, low, high), row in pairs:
        main = main + dot(whole, row)
        rest = rest + dot(low, row[:, :HALF]) + dot(high, row[:, HALF:])
    return main.astype(bf16), rest.astype(bf16)


def pick(across, route, main, rest):
    place = iota((ROWS, MAIN), 1).astype(f32)
    whole, low, high = [
        one_hot(place == across[:, 3 * route + n : 3 * route + n + 1]) for n in range(3)
    ]
    whole_part = dot(whole, main)
    return whole_part[:, :HALF] + dot(low, rest), whole_part[:, HALF:] + dot(high, rest)


def rest_tables():
    row = iota((REST, MAIN), 0)
    target = (row & 31) * 8 + (row >> 5) * 2
    lane = iota((REST, MAIN), 1)
    real = row < 96
    return one_hot((lane == target) & real), one_hot((lane == target + 1) & real)


def unpack(packed_ref, offset, into_ref):
    low, high = rest_tables()
    rest = packed_ref[:, offset + WIDTH : offset + SENT]
    into_ref[0:MAIN, :] = packed_ref[:, offset : offset + WIDTH]
    into_ref[MAIN : MAIN + REST, 0:HALF] = dot(low, rest).astype(bf16)
    into_ref[MAIN : MAIN + REST, HALF:WIDTH] = dot(high, rest).astype(bf16)


def pack(rows, offset, into_ref):
    low, high = rest_tables()
    into_ref[:, offset : offset + WIDTH] = rows[:MAIN]
    into_ref[:, offset + WIDTH : offset + SENT] = (
        dot(low, rows[MAIN:, :HALF], 0) + dot(high, rows[MAIN:, HALF:], 0)
    ).astype(bf16)


def attend(current, gain_ref, qkv_ref, bias_ref, low_ref, triple_ref, weights_ref):
    low = (current * scale_of(current) * gain_ref[0:1, :]).astype(bf16)
    low_ref[...] = low
    for k in range(3):
        triple_ref[k] = dot(low, qkv_ref[k], 1, 1).astype(bf16)
    mixture = jnp.zeros((ROWS, QUARTER), f32)
    go(low_ref, triple_ref)
    for head in range(HERE):
        mask = head_mask(head)
        scores = dot(triple_ref[0] * mask, triple_ref[1], 1, 1) * HEAD**-0.5 + bias_ref[head]
        scores = scores - jnp.max(scores, axis=-1, keepdims=True)
        raised = jnp.exp(scores)
        weights = raised / jnp.sum(raised, axis=-1, keepdims=True)
        weights_ref[head] = weights
        mixture = mixture + dot(weights.astype(bf16), triple_ref[2] * mask)
    go(weights_ref)
    return mixture.astype(bf16)


def attention_first(
    tokens_ref, gain_ref, qkv_ref, bias_ref, out_ref, low_ref, triple_ref, weights_ref, mixture_ref, part_ref
):
    mixture = attend(
        tokens_ref[...].astype(f32), gain_ref, qkv_ref, bias_ref, low_ref, triple_ref, weights_ref
    )
    mixture_ref[...] = mixture
    go(mixture_ref)
    part_ref[...] = dot(mixture, out_ref[...]).astype(bf16)


def attention_next(
    middle_ref,
    z0,
    z1,
    z2,
    z3,
    gain_ref,
    qkv_ref,
    bias_ref,
    out_ref,
    current_ref,
    low_ref,
    triple_ref,
    weights_ref,
    mixture_ref,
    part_ref,
):
    current = middle_ref[...] + four(z0[...], z1[...], z2[...], z3[...])
    current_ref[...] = current
    go(current_ref)
    mixture = attend(current, gain_ref, qkv_ref, bias_ref, low_ref, triple_ref, weights_ref)
    mixture_ref[...] = mixture
    go(mixture_ref)
    part_ref[...] = dot(mixture, out_ref[...]).astype(bf16)


def route_rows(middle, gain_ref, router_ref, across, low_ref, gates_ref):
    low = (middle * scale_of(middle) * gain_ref[1:2, :]).astype(bf16)
    low_ref[...] = low
    go(low_ref)
    logits = dot(low, router_ref[...], 1, 1)
    lane = iota((ROWS, EXPERTS), 1).astype(f32)
    chosen = [
        jnp.sum(jnp.where(lane == across[:, 6 + k : 7 + k], logits, 0.0), axis=1, keepdims=True)
        for k in range(2)
    ]
    top = jnp.maximum(chosen[0], chosen[1])
    raised = [jnp.exp(c - top) for c in chosen]
    total = raised[0] + raised[1]
    gates = [r / total for r in raised]
    place = iota((ROWS, ROWS), 1)
    gates_ref[...] = jnp.where(place == 0, gates[0], jnp.where(place == 1, gates[1], 0.0))
    return low, gates


def route_first(
    current_ref,
    p0,
    p1,
    p2,
    p3,
    gain_ref,
    router_ref,
    across_ref,
    down_ref,
    middle_ref,
    low_ref,
    gates_ref,
    send_ref,
):
    middle = current_ref[...].astype(f32) + four(p0[...], p1[...], p2[...], p3[...])
    middle_ref[...] = middle
    go(middle_ref)
    low, gates = route_rows(middle, gain_ref, router_ref, across_ref[...], low_ref, gates_ref)
    main, rest = dispatch(down_ref[...], [low])
    send_ref[:, :WIDTH] = main
    send_ref[:, WIDTH:] = rest


def route_next(
    current_ref,
    p0,
    p1,
    p2,
    p3,
    gain_ref,
    router_ref,
    across_ref,
    down_ref,
    cotangent_ref,
    middle_ref,
    low_ref,
    gates_ref,
    send_ref,
):
    middle = current_ref[...].astype(f32) + four(p0[...], p1[...], p2[...], p3[...])
    middle_ref[...] = middle
    go(middle_ref)
    low, gates = route_rows(middle, gain_ref, router_ref, across_ref[...], low_ref, gates_ref)
    main, rest = dispatch(down_ref[...], [low])
    send_ref[:, :WIDTH] = main
    send_ref[:, WIDTH:SENT] = rest
    gradient = cotangent_ref[...].astype(f32)
    main, rest = dispatch(down_ref[...], [(gate * gradient).astype(bf16) for gate in gates])
    send_ref[:, SENT : SENT + WIDTH] = main
    send_ref[:, SENT + WIDTH :] = rest


CURVE = (2.0 / 3.141592653589793) ** 0.5


def gelu_parts(values):
    squared = values * values
    bent = jnp.tanh(CURVE * values * (1.0 + 0.044715 * squared))
    return bent, squared


def gelu(values):
    bent, _ = gelu_parts(values)
    return 0.5 * values * (1.0 + bent)


def gelu_slope(values):
    bent, squared = gelu_parts(values)
    inner = CURVE * (1.0 + 3.0 * 0.044715 * squared)
    return 0.5 * (1.0 + bent) + 0.5 * values * (1.0 - bent * bent) * inner


def expert_forward(got_ref, in_ref, out_ref, rows_ref, slope_ref, active_ref, back_ref):
    unpack(got_ref, 0, rows_ref)
    go(rows_ref)
    before = dot(rows_ref[...], in_ref[...])
    slope_ref[...] = gelu_slope(before).astype(bf16)
    go(slope_ref)
    active = gelu(before).astype(bf16)
    active_ref[...] = active
    go(active_ref)
    pack(dot(active, out_ref[...]).astype(bf16), 0, back_ref)


def expert_backward(got_ref, out_ref, slope_ref, in_ref, grads_ref, down_ref, back_ref):
    unpack(got_ref, 0, grads_ref)
    go(grads_ref)
    grad_active = dot(grads_ref[...], out_ref[...], 1, 1)
    grad_before = (grad_active * slope_ref[...].astype(f32)).astype(bf16)
    down_ref[...] = grad_before
    go(down_ref)
    pack(dot(grad_before, in_ref[...], 1, 1).astype(bf16), 0, back_ref)


def expert_both(got_ref, in_ref, out_ref, rows_ref, active_ref, grads_ref, down_ref, back_ref):
    unpack(got_ref, 0, rows_ref)
    unpack(got_ref, SENT, grads_ref)
    go(rows_ref, grads_ref)
    before = dot(rows_ref[...], in_ref[...])
    active = gelu(before).astype(bf16)
    active_ref[...] = active
    go(active_ref)
    pack(dot(active, out_ref[...]).astype(bf16), 0, back_ref)
    grad_active = dot(grads_ref[...], out_ref[...], 1, 1)
    grad_before = (grad_active * gelu_slope(before)).astype(bf16)
    down_ref[...] = grad_before
    go(down_ref)
    pack(dot(grad_before, in_ref[...], 1, 1).astype(bf16), SENT, back_ref)


def expert_grads_top(rows_ref, active_ref, grads_ref, down_ref, in_grad_ref, out_grad_ref):
    in_grad_ref[0, 0] = dot(rows_ref[...], down_ref[...], 0)
    out_grad_ref[0, 0] = dot(active_ref[...], grads_ref[...], 0)


def expert_grads_low(rows_ref, active_ref, grads_ref, down_ref, _, __, in_grad_ref, out_grad_ref):
    expert_grads_top(rows_ref, active_ref, grads_ref, down_ref, in_grad_ref, out_grad_ref)


def combine_first(got_ref, across_ref, gates_ref, part_ref, picked_ref):
    main, rest = got_ref[:, :WIDTH], got_ref[:, WIDTH:]
    across, gates = across_ref[...], gates_ref[...]
    left, right = 0.0, 0.0
    for route in range(2):
        one, two = pick(across, route, main, rest)
        picked_ref[route, :, :HALF] = one.astype(bf16)
        picked_ref[route, :, HALF:] = two.astype(bf16)
        left = left + gates[:, route : route + 1] * one
        right = right + gates[:, route : route + 1] * two
    part_ref[:, :HALF] = left.astype(bf16)
    part_ref[:, HALF:] = right.astype(bf16)


def gate_rows(grads):
    place = iota((8, ROWS), 0)
    rows = [row_of(grad, ROWS) for grad in grads]
    both = jnp.where(place == 0, rows[0], jnp.where(place == 1, rows[1], 0.0))
    moved = jnp.where(place == 2, rows[0], jnp.where(place == 3, rows[1], 0.0))
    left = moved - moved.astype(bf16).astype(f32)
    return (both + left).astype(bf16)


def gathered_back(got_ref, offset, across, rows, into_ref):
    main = got_ref[:, offset : offset + WIDTH]
    rest = got_ref[:, offset + WIDTH : offset + SENT]
    left, right = pick(across, 0, main, rest)
    other_left, other_right = pick(across, 1, main, rest)
    into_ref[:ROWS, :HALF] = (left + other_left).astype(bf16)
    into_ref[:ROWS, HALF:] = (right + other_right).astype(bf16)
    into_ref[ROWS:, :ROWS] = rows
    into_ref[ROWS:, ROWS:] = jnp.zeros((8, WIDTH - ROWS), bf16)


def combine_next(got_ref, across_ref, gates_ref, cotangent_ref, part_ref, back_ref):
    main, rest = got_ref[:, :WIDTH], got_ref[:, WIDTH:SENT]
    across, gates = across_ref[...], gates_ref[...]
    gradient = cotangent_ref[...].astype(f32)
    left, right, grads = 0.0, 0.0, []
    for route in range(2):
        one, two = pick(across, route, main, rest)
        left = left + gates[:, route : route + 1] * one
        right = right + gates[:, route : route + 1] * two
        grads.append(
            jnp.sum(gradient[:, :HALF] * one + gradient[:, HALF:] * two, axis=1, keepdims=True)
        )
    part_ref[:, :HALF] = left.astype(bf16)
    part_ref[:, HALF:] = right.astype(bf16)
    gathered_back(got_ref, SENT, across, gate_rows(grads), back_ref)


def combine_back(got_ref, across_ref, rows_ref, back_ref):
    gathered_back(got_ref, 0, across_ref[...], rows_ref[...], back_ref)


def attention_back(
    e0,
    e1,
    e2,
    e3,
    gates_ref,
    across_ref,
    router_ref,
    middle_ref,
    gain_ref,
    gradient_ref,
    out_ref,
    triple_ref,
    weights_ref,
    qkv_ref,
    hot_ref,
    after_ref,
    low_ref,
    back_triple_ref,
    part_ref,
    logits_ref,
    gain_grad_ref,
    table_grad_ref,
):
    total = four(e0[...], e1[...], e2[...], e3[...])
    gates = gates_ref[...]
    across = across_ref[...]
    gate = [gates[:, k : k + 1] for k in range(2)]
    rows = total[ROWS:, :ROWS]
    grad_gate = [column_of(rows[k : k + 1] + rows[k + 2 : k + 3], ROWS) for k in range(2)]
    mean = gate[0] * grad_gate[0] + gate[1] * grad_gate[1]
    lane = iota((ROWS, EXPERTS), 1).astype(f32)
    grad_logits = 0.0
    for k in range(2):
        grad_logits = grad_logits + jnp.where(
            lane == across[:, 6 + k : 7 + k], gate[k] * (grad_gate[k] - mean), 0.0
        )
    high = grad_logits.astype(bf16)
    low = (grad_logits - high.astype(f32)).astype(bf16)
    logits_ref[:, :EXPERTS] = high
    logits_ref[:, EXPERTS : 2 * EXPERTS] = low
    logits_ref[:, 2 * EXPERTS :] = jnp.zeros((ROWS, 128 - 2 * EXPERTS), bf16)
    grad_low = total[:ROWS] + dot(high, router_ref[...]) + dot(low, router_ref[...])
    grad_middle, gain_grad_ref[...] = norm_back(middle_ref[...], gain_ref[1:2, :], grad_low)
    after = gradient_ref[...].astype(f32) + grad_middle
    after_ref[...] = after
    low_after = after.astype(bf16)
    low_ref[...] = low_after
    go(after_ref, low_ref, logits_ref, gain_grad_ref)
    grad_mixture = dot(low_after, out_ref[...], 1, 1).astype(bf16)
    queries, keys, values = triple_ref[0], triple_ref[1], triple_ref[2]
    grad_queries = jnp.zeros((ROWS, QUARTER), f32)
    grad_keys, grad_values = grad_queries, grad_queries
    diagonals = jnp.zeros((8, 256), f32)
    flip = one_hot(iota((ROWS, ROWS), 0) + iota((ROWS, ROWS), 1) == ROWS - 1)
    for head in range(HERE):
        mask = head_mask(head)
        masked_grad = grad_mixture * mask
        weights = weights_ref[head]
        grad_values = grad_values + dot(weights.astype(bf16), masked_grad, 0)
        grad_weights = dot(masked_grad, values, 1, 1)
        grad_scores = weights * (
            grad_weights - jnp.sum(weights * grad_weights, axis=-1, keepdims=True)
        )
        grad_scores = grad_scores.astype(bf16)
        grad_queries = grad_queries + dot(grad_scores, keys * mask)
        grad_keys = grad_keys + dot(grad_scores, queries * mask, 0)
        wide = jnp.concatenate([dot(flip, grad_scores), jnp.zeros((ROWS, 128), f32)], axis=1)
        turned = pltpu.roll(wide, 0, axis=1, stride=1, stride_axis=0)
        diagonals = jnp.where(
            iota((8, 256), 0) == head, jnp.sum(turned, axis=0, keepdims=True), diagonals
        )
    table_grad_ref[...] = dot(diagonals, hot_ref[...], 1, 1, precision=highest)
    grad_input = 0.0
    for k, grad in enumerate((grad_queries * HEAD**-0.5, grad_keys * HEAD**-0.5, grad_values)):
        grad = grad.astype(bf16)
        back_triple_ref[:, k * QUARTER : (k + 1) * QUARTER] = grad
        grad_input = grad_input + dot(grad, qkv_ref[k])
    go(back_triple_ref)
    part_ref[...] = grad_input.astype(bf16)


SHARE = WIDTH // EXPERTS
GROUPS = WIDTH // 128


def router_places():
    row, column = iota((WIDTH, GROUPS * EXPERTS), 0), iota((WIDTH, GROUPS * EXPERTS), 1)
    return one_hot(row == (column & (EXPERTS - 1)) * SHARE + (column >> 5))


def folded(line):
    place = iota((8, 128), 0)
    rows = jnp.zeros((8, 128), f32)
    for part in range(GROUPS):
        rows = jnp.where(place == part, line[:, part * 128 : (part + 1) * 128], rows)
    return rows


def unfolded(rows):
    return jnp.concatenate([rows[part : part + 1, :] for part in range(GROUPS)], axis=1)


def fill_grads(low, back_triple, mixture, after, low_two, logits, gains, table, grads_ref):
    kind = grads_ref.dtype
    qkv_rows = 3 * QUARTER
    both = dot(logits, low_two, 0)
    total = both[:EXPERTS] + both[EXPERTS : 2 * EXPERTS]
    parts = jnp.concatenate([total[:, r * 128 : (r + 1) * 128] for r in range(GROUPS)], axis=0)
    places = router_places()
    high = parts.astype(bf16)
    rest = (parts - high.astype(f32)).astype(bf16)
    grads_ref[:, WIDTH:] = (dot(places, high) + dot(places, rest)).astype(kind)
    for chunk, gain in enumerate(gains):
        start = chunk * SHARE + 8
        grads_ref[start : start + 8, WIDTH:] = folded(gain).astype(kind)
    start = 2 * SHARE + 8
    grads_ref[start : start + 8, WIDTH : WIDTH + EXPERTS] = table.astype(kind)
    grads_ref[qkv_rows:, :WIDTH] = dot(mixture, after, 0).astype(kind)
    grads_ref.go(2)
    grads_ref[:384, :WIDTH] = dot(back_triple[:, :384], low, 0).astype(kind)
    grads_ref.go(0)
    grads_ref[384:qkv_rows, :WIDTH] = dot(back_triple[:, 384:], low, 0).astype(kind)
    grads_ref.go(1)


def weight_grads(
    low_ref, back_triple_ref, mixture_ref, after_ref, low_two_ref, logits_ref, gain, table, grads_ref
):
    operands = (low_ref, back_triple_ref, mixture_ref, after_ref, low_two_ref, logits_ref)
    fill_grads(*[ref[...] for ref in operands], [gain[...]], table[...], grads_ref)


def attention_back_low(*refs):
    operands, (low_ref, mixture_ref, low_two_ref, gain10_ref) = refs[:15], refs[15:19]
    after_ref, part_ref, grads_ref, held_low, held_triple, held_logits, held_gain, held_table = refs[19:]
    attention_back(
        *operands,
        after_ref,
        held_low,
        held_triple,
        part_ref,
        held_logits,
        held_gain,
        held_table,
    )
    operands = (low_ref, held_triple, mixture_ref, held_low, low_two_ref, held_logits)
    fill_grads(
        *[ref[...] for ref in operands],
        [held_gain[...], gain10_ref[...]],
        held_table[...],
        grads_ref,
    )


def start_back(
    after_ref,
    d0,
    d1,
    d2,
    d3,
    input_ref,
    gain_ref,
    gates_ref,
    down_ref,
    picked_ref,
    gradient_ref,
    gain_grad_ref,
    rows_ref,
    send_ref,
):
    grad_low = four(d0[...], d1[...], d2[...], d3[...])
    grad_input, gain_grad_ref[...] = norm_back(input_ref[...].astype(f32), gain_ref[0:1, :], grad_low)
    gradient = after_ref[...] + grad_input
    gradient_ref[...] = gradient
    go(gradient_ref, gain_grad_ref)
    gates = gates_ref[...]
    weighted = [(gates[:, k : k + 1] * gradient).astype(bf16) for k in range(2)]
    main, rest = dispatch(down_ref[...], weighted)
    send_ref[:, :WIDTH] = main
    send_ref[:, WIDTH:] = rest
    rows_ref[...] = gate_rows(
        [jnp.sum(gradient * picked_ref[k].astype(f32), axis=1, keepdims=True) for k in range(2)]
    )


def finish_back(after_ref, d0, d1, d2, d3, input_ref, gain_ref, gradient_ref, gain_grad_ref):
    grad_low = four(d0[...], d1[...], d2[...], d3[...])
    grad_input, gain_grad_ref[...] = norm_back(input_ref[...].astype(f32), gain_ref[0:1, :], grad_low)
    gradient_ref[...] = after_ref[...] + grad_input


def finish_output(middle_ref, z0, z1, z2, z3, output_ref):
    output_ref[...] = (middle_ref[...] + four(z0[...], z1[...], z2[...], z3[...])).astype(bf16)


def add_chunks(chunks_ref, gain00_ref, spread_ref):
    total = chunks_ref[0:SHARE, :].astype(f32)
    for block in range(1, EXPERTS):
        total = total + chunks_ref[block * SHARE : (block + 1) * SHARE, :].astype(f32)
    total = total.astype(bf16)
    gain = folded(gain00_ref[...]).astype(bf16)
    for block in range(EXPERTS):
        start = block * SHARE
        spread_ref[start : start + SHARE, :] = total
        spread_ref[start + 16 : start + SHARE, WIDTH:] = gain


def router_rows(small):
    places = router_places()
    high = small.astype(bf16)
    parts = dot(places, high, 0) + dot(places, (small - high.astype(f32)).astype(bf16), 0)
    return jnp.concatenate(
        [parts[r * EXPERTS : (r + 1) * EXPERTS] for r in range(GROUPS)], axis=1
    )


def place_top(
    grads_ref, qkv_ref, out_ref, router_ref, gain_ref, table_ref, wide, small, rows, done
):
    fetch = pltpu.make_async_copy(grads_ref.at[:, WIDTH:], small, done.at[0])
    fetch.start()
    arriving, leaving = [], []
    for k in range(4):
        source = grads_ref.at[k * QUARTER : (k + 1) * QUARTER, :WIDTH]
        target = qkv_ref.at[1, k] if k < 3 else out_ref.at[1]
        arriving.append(pltpu.make_async_copy(source, wide.at[k], done.at[1 + k]))
        leaving.append(pltpu.make_async_copy(wide.at[k], target, done.at[5 + k]))
        arriving[-1].start()
    fetch.wait()
    lanes = small[...]
    rows[...] = router_rows(lanes)
    leaving.append(pltpu.make_async_copy(rows, router_ref.at[1], done.at[9]))
    leaving[-1].start()
    gain_ref[...] = unfolded(lanes[8:16])
    table_ref[...] = lanes[2 * SHARE + 8 : 2 * SHARE + 16]
    for k in range(4):
        arriving[k].wait()
        leaving[k].start()
    for copy in leaving:
        copy.wait()


def place_low(
    grads_ref,
    gain_ref,
    table_ref,
    _,
    __,
    ___,
    qkv_ref,
    out_ref,
    router_ref,
    gains_ref,
    tables_ref,
    wide,
    rows,
    done,
):
    copies = []
    for k in range(4):
        wide[k] = grads_ref[k * QUARTER : (k + 1) * QUARTER, :WIDTH].astype(f32)
        target = qkv_ref.at[0, k] if k < 3 else out_ref.at[0]
        copies.append(pltpu.make_async_copy(wide.at[k], target, done.at[k]))
        copies[-1].start()
    small = grads_ref[:, WIDTH:].astype(f32)
    rows[...] = router_rows(small)
    copies.append(pltpu.make_async_copy(rows, router_ref.at[0], done.at[4]))
    copies[-1].start()
    first = small[16:SHARE]
    for block in range(1, EXPERTS):
        first = first + small[block * SHARE + 16 : (block + 1) * SHARE]
    gains_ref[0, 0:1, :] = unfolded(first)
    gains_ref[0, 1:2, :] = unfolded(small[8:16])
    gains_ref[1, 0:1, :] = unfolded(small[SHARE + 8 : SHARE + 16])
    gains_ref[1, 1:2, :] = gain_ref[...]
    table = small[2 * SHARE + 8 : 2 * SHARE + 16]
    for head in range(HERE):
        tables_ref[head, 0:1, :] = table[head : head + 1, :EXPERTS]
        tables_ref[head, 1:2, :] = table_ref[head : head + 1, :EXPERTS]
    for copy in copies:
        copy.wait()


def place(top_grads, low_grads):
    stacks = [
        pltpu.HBM((2, 3, QUARTER, WIDTH), f32),
        pltpu.HBM((2, QUARTER, WIDTH), f32),
        pltpu.HBM((2, EXPERTS, WIDTH), f32),
    ]
    hbm, vmem = pl.BlockSpec(memory_space=pltpu.HBM), pl.BlockSpec(memory_space=pltpu.VMEM)
    params = pltpu.CompilerParams(vmem_limit_bytes=16 * 1024 * 1024)
    *stacked, gain, table = pl.pallas_call(
        place_top,
        out_shape=[
            *stacks,
            jax.ShapeDtypeStruct((1, WIDTH), f32),
            jax.ShapeDtypeStruct((8, 128), f32),
        ],
        in_specs=[hbm],
        out_specs=[hbm] * 3 + [vmem] * 2,
        scratch_shapes=[
            pltpu.VMEM((4, QUARTER, WIDTH), f32),
            pltpu.VMEM((WIDTH, 128), f32),
            pltpu.VMEM((EXPERTS, WIDTH), f32),
            pltpu.SemaphoreType.DMA((10,)),
        ],
        compiler_params=params,
        name="place_top",
    )(in_hbm(top_grads))
    return pl.pallas_call(
        place_low,
        out_shape=[
            *stacks,
            jax.ShapeDtypeStruct((2, 2, WIDTH), f32),
            jax.ShapeDtypeStruct((HERE, 2, EXPERTS), f32),
        ],
        in_specs=[vmem] * 3 + [hbm] * 3,
        out_specs=[hbm] * 3 + [vmem] * 2,
        scratch_shapes=[
            pltpu.VMEM((4, QUARTER, WIDTH), f32),
            pltpu.VMEM((EXPERTS, WIDTH), f32),
            pltpu.SemaphoreType.DMA((5,)),
        ],
        input_output_aliases={3: 0, 4: 1, 5: 2},
        compiler_params=params,
        name="place_low",
    )(low_grads, gain, table, *[in_hbm(s) for s in stacked])


def around(values):
    sent = [
        lax.ppermute(values, "tensor", [(i, (i + shift) % 4) for i in range(4)]) for shift in (1, 2, 3)
    ]
    return [values, *sent]


def across_experts(values):
    return lax.all_to_all(values, "expert", 0, 0, tiled=True)


def shards(
    tokens,
    segment_ids,
    expert_routes,
    bucket_ids,
    proj_qkv,
    proj_out,
    bias_table,
    norm_gains,
    router,
    expert_in,
    expert_out,
    cotangent,
):
    qkv = proj_qkv.transpose(0, 1, 3, 2)
    router = router.transpose(0, 2, 1)
    expert_in, expert_out = expert_in[:, 0], expert_out[:, 0]
    gains = norm_gains
    row = (ROWS, WIDTH)
    narrow = (ROWS, QUARTER)
    scores = (HERE, ROWS, ROWS)
    slots = (MAIN + REST, WIDTH)
    stacked = (2, 1, WIDTH, WIDTH)
    bias, across, down, hot = call(
        setup,
        [
            ((2, HERE, ROWS, ROWS), f32),
            ((2, ROWS, ROWS), f32),
            ((2, 8, ROWS), f32),
            ((EXPERTS, 256), f32),
        ],
        Late(bucket_ids.reshape(1, -1)),
        Late(bias_table.transpose(2, 0, 1)),
        Late(segment_ids),
        Late(expert_routes.transpose(0, 2, 1)),
    )
    kept = [
        Kept(row, bf16),
        Kept((3, *narrow), bf16),
        Kept(scores, f32),
        Kept(narrow, bf16),
        (row, bf16),
    ]

    low_a0, triple0, weights0, mixture0, part = call(
        attention_first,
        kept,
        Late(tokens),
        Late(Layer(gains, 0)),
        Late(Layer(qkv, 0)),
        Layer(bias, 0),
        Late(Layer(proj_out, 0)),
    )
    middle0, low_b0, gates0, send = call(
        route_first,
        [Kept(row, f32), Kept(row, bf16), ((ROWS, ROWS), f32), ((MAIN, SENT), bf16)],
        tokens,
        *around(part),
        Layer(gains, 0),
        Late(Layer(router, 0)),
        Layer(across, 0),
        Layer(down, 0),
    )
    rows0, slope0, active0, send = call(
        expert_forward,
        [Kept(slots, bf16), Kept(slots, bf16), Kept(slots, bf16), ((MAIN, SENT), bf16)],
        across_experts(send),
        Layer(expert_in, 0),
        Layer(expert_out, 0),
    )
    part, picked0 = call(
        combine_first,
        [(row, bf16), Kept((2, *row), bf16)],
        across_experts(send),
        Layer(across, 0),
        gates0,
    )

    current1, low_a1, triple1, weights1, mixture1, part = call(
        attention_next,
        [Kept(row, f32), *kept],
        Late(middle0),
        *around(part),
        Layer(gains, 1),
        Late(Layer(qkv, 1)),
        Late(Layer(bias, 1)),
        Late(Layer(proj_out, 1)),
    )
    middle1, low_b1, gates1, send = call(
        route_next,
        [Kept(row, f32), Kept(row, bf16), ((ROWS, ROWS), f32), ((MAIN, 2 * SENT), bf16)],
        Late(current1),
        *around(part),
        Layer(gains, 1),
        Late(Layer(router, 1)),
        Layer(across, 1),
        Layer(down, 1),
        cotangent,
    )
    rows1, active1, grads1, down1, send = call(
        expert_both,
        [*[Kept(slots, bf16)] * 4, ((MAIN, 2 * SENT), bf16)],
        across_experts(send),
        Layer(expert_in, 1),
        Layer(expert_out, 1),
    )
    got = across_experts(send)
    in_grads, out_grads = call_stacked(
        expert_grads_top, 1, (rows1, active1, grads1, down1), stacked
    )
    moved, back = call(
        combine_next,
        [(row, bf16), ((LONG, WIDTH), bf16)],
        got,
        Layer(across, 1),
        gates1,
        cotangent,
    )

    back_kept = [
        Kept(row, f32),
        Kept(row, bf16),
        Kept((ROWS, 3 * QUARTER), bf16),
        (row, bf16),
        Kept((ROWS, 128), bf16),
        Kept((1, WIDTH), f32),
        Kept((8, EXPERTS), f32),
    ]
    after1, low_after1, back_triple1, part, logits1, gain11, table1 = call(
        attention_back,
        back_kept,
        *around(back),
        gates1,
        Layer(across, 1),
        Late(Layer(router, 1)),
        middle1,
        Layer(gains, 1),
        cotangent,
        Late(Layer(proj_out, 1)),
        triple1,
        weights1,
        Late(Layer(qkv, 1)),
        hot,
    )
    parts = around(part)
    (top_grads,) = call(
        weight_grads,
        [Kept((WIDTH, SUMMED), f32)],
        Late(low_a1),
        Late(back_triple1),
        Late(mixture1),
        Late(low_after1),
        Late(low_b1),
        Late(logits1),
        Late(gain11),
        Late(table1),
    )
    top_grads = lax.psum(top_grads, "expert")
    parts, in_grads = lax.optimization_barrier((parts, in_grads))

    def low_layer(_, carried):
        in_grads, out_grads, after, _ = carried
        gradient0, gain10, rows0b, send = call(
            start_back,
            [Kept(row, f32), Kept((1, WIDTH), f32), ((8, ROWS), bf16), ((MAIN, SENT), bf16)],
            Late(after),
            *parts,
            Late(current1),
            Late(Layer(gains, 1)),
            gates0,
            Layer(down, 0),
            Late(picked0),
        )
        grads0, down0, send = call(
            expert_backward,
            [Kept(slots, bf16), Kept(slots, bf16), ((MAIN, SENT), bf16)],
            across_experts(send),
            Late(Layer(expert_out, 0)),
            Late(slope0),
            Late(Layer(expert_in, 0)),
        )
        got = across_experts(send)
        in_grads, out_grads = call_stacked(
            expert_grads_low, 0, (rows0, active0, grads0, down0), stacked, (in_grads, out_grads)
        )
        (back,) = call(combine_back, [((LONG, WIDTH), bf16)], got, Layer(across, 0), rows0b)
        backs = around(back)
        backs, in_grads = lax.optimization_barrier((backs, in_grads))
        after0, part, grads = call(
            attention_back_low,
            [Kept(row, f32), (row, bf16), Kept((WIDTH, SUMMED), bf16)],
            *backs,
            gates0,
            Layer(across, 0),
            Layer(router, 0),
            Late(middle0),
            Layer(gains, 0),
            Late(gradient0),
            Layer(proj_out, 0),
            Late(triple0),
            Late(weights0),
            Layer(qkv, 0),
            Late(hot),
            Late(low_a0),
            Late(mixture0),
            Late(low_b0),
            Late(gain10),
            held=[
                (row, bf16),
                ((ROWS, 3 * QUARTER), bf16),
                ((ROWS, 128), bf16),
                ((1, WIDTH), f32),
                ((8, EXPERTS), f32),
            ],
        )
        low_parts = around(part)
        tokens_grad, gain00 = call(
            finish_back,
            [Kept(row, f32), Kept((1, WIDTH), f32)],
            after0,
            *low_parts,
            tokens,
            Layer(gains, 0),
        )
        (spread,) = call(
            add_chunks,
            [Kept((WIDTH, SUMMED), bf16)],
            across_experts(grads),
            Late(gain00),
        )
        return in_grads, out_grads, tokens_grad, spread

    once = jnp.minimum(jnp.maximum(bucket_ids[0], 0) + 1, 1)
    in_grads, out_grads, tokens_grad, spread = lax.fori_loop(
        0,
        once,
        low_layer,
        (
            in_grads,
            out_grads,
            after1,
            jnp.zeros((WIDTH, SUMMED), bf16),
        ),
    )
    low_grads = across_experts(spread)
    (output,) = call(finish_output, [Kept(row, bf16)], middle1, *around(moved))
    qkv_grad, out_grad, router_grad, gain_grads, table_grad = place(top_grads, low_grads)
    return (
        output,
        tokens_grad,
        qkv_grad.transpose(0, 1, 3, 2),
        out_grad,
        table_grad.transpose(1, 2, 0),
        gain_grads,
        router_grad.transpose(0, 2, 1),
        in_grads,
        out_grads,
    )


def solution(mesh):
    placed = (
        P("expert", None),
        P("expert", None),
        P(None, "expert", None),
        P(),
        P(None, None, None, "tensor"),
        P(None, "tensor", None),
        P(None, None, "tensor"),
        P(),
        P(),
        P(None, "expert", None, "tensor"),
        P(None, "expert", "tensor", None),
        P("expert", None),
    )
    return jax.shard_map(
        shards,
        mesh=mesh,
        in_specs=placed,
        out_specs=(
            P("expert", None),
            P("expert", None),
            P(None, None, None, "tensor"),
            P(None, "tensor", None),
            P(None, None, "tensor"),
            P(),
            P(),
            P(None, "expert", None, "tensor"),
            P(None, "expert", "tensor", None),
        ),
        check_vma=False,
    )
```
